32 devices in a mesh: group: 2 (over y), row: 4 (over z), col: 4 (over x, core).
Axes of the slice: x: 2, y: 2, z: 4, core: 2. Of those that a mesh axis runs over, the one named last changes fastest.
Arguments:
- tokens: bfloat16 [512, 10240], P(('group', 'col'), 'row'), parts along dimension 0, may hold values from -6 to 6
- token_job_index: int32 [512], P('group'), parts along dimension 0, may hold values from 0 to 3, never falling along the last dimension, each value on 1 to 128 neighbouring positions
- job_adapter_index: int32 [8], P('group'), parts along dimension 0, may hold values from 0 to 7
- first_weight: bfloat16 [10240, 24576], P('row', 'col'), may hold values from -0.0625 to 0.0625
- first_bias: float32 [24576], P('col'), may hold values from -3 to 3
- first_down_maps: bfloat16 [10240, 128], P('row'), may hold values from -0.0625 to 0.0625
- first_up_maps: bfloat16 [128, 24576], P(None, 'col'), may hold values from -1.5 to 1.5
- second_weight: bfloat16 [24576, 10240], P('col', 'row'), may hold values from -0.0390625 to 0.0390625
- second_bias: float32 [10240], P('row'), may hold values from -3 to 3
- second_down_maps: bfloat16 [24576, 128], P('col'), may hold values from -0.0390625 to 0.0390625
- second_up_maps: bfloat16 [128, 10240], P(None, 'row'), may hold values from -1.5 to 1.5
Outputs:
- ffn_out: bfloat16 [512, 10240], P(('group', 'col'), 'row'), parts along dimension 0
The draws below stay inside these ranges and needn't reach their ends.
There are 2 independent parts, one for each index of `group`. The reference program is written for one: setup_inputs(seed, part) draws one part's arguments, and reference() takes and returns one part's arrays. A program takes and returns all parts, laid end to end along the dimension named above; an argument that names none is the same for every part. Nothing has to cross between parts.
Inputs may be any that keep to these rules, and one draw needn't show every extreme that they name: token_job_index never falls along the tokens; each of the 4 jobs holds 1 to 128 tokens.
All inputs are finite; a program needn't handle non-finite values.
Results may differ from the reference program's by a relative error of at most 0.018.
Values may be sent and summed in bfloat16 or wider, within the bound.
No kernel may reach another device: no remote copies, remote signals or barrier semaphores. Data moves between devices by JAX's collectives and lax.ppermute only.
A program may use at most 192 MiB of HBM per device.

```python
import math
import jax
import jax.numpy as jnp
import numpy as np
from jax import lax

MODEL_FEATURES = 10240
HIDDEN_UNITS = 24576
ADAPTER_RANK = 16
ADAPTER_COUNT = 8
JOBS = 4
TOKENS = 256
N_ROW = 4
N_COL = 4


def plant(result, key, least, high):
    place = [jax.random.randint(jax.random.fold_in(key, axis), (), 0, length) for axis, length in enumerate(result.shape)]
    longest = result.shape.index(max(result.shape))
    beside = place[:longest] + [(place[longest] + 1) % result.shape[longest]] + place[longest + 1:]
    return result.at[tuple(place)].set(least).at[tuple(beside)].set(high)


def steps_of(rng, dims, cuts, smallest, top_value):
    def one(position, blocks):
        heights = jax.random.uniform(jax.random.fold_in(jax.random.fold_in(rng, 6), position), (blocks,), jnp.float32, smallest / len(cuts), top_value / len(cuts))
        return jnp.repeat(jnp.exp(heights), dims[position] // blocks).reshape((-1,) + (1,) * (len(dims) - position - 1))

    gain = one(*cuts[0])
    for cut in cuts[1:]:
        gain = gain * one(*cut)
    return gain


def length_profile(amount, total, limit, skew):
    loads = [(1 << 20) // math.isqrt(rank ** skew) + 1 for rank in range(2, amount + 1)]
    rest, counts = total - limit - (amount - 1), [1] * (amount - 1)
    while rest > 0:
        candidates = [i for i in range(amount - 1) if counts[i] < limit]
        whole, left = sum([loads[i] for i in candidates]), rest
        for i in candidates:
            more = min(limit - counts[i], max(1, left * loads[i] // whole), rest)
            counts[i] = counts[i] + more
            rest = rest - more
    return np.array([limit] + counts)


def uneven_parts(own_key, number_of, total, bound, skew):
    if number_of == 2:
        one = jax.random.randint(own_key, (), max(1, total - bound), min(bound, total - 1) + 1)
        return jnp.stack([one, total - one])
    tallies = jnp.asarray(length_profile(number_of, total, bound, skew), jnp.int32)
    twos = (number_of - 1) // 2
    source_of, receiver = tallies[1:1 + 2 * twos:2], tallies[2:2 + 2 * twos:2]
    margin = jnp.minimum(source_of - 1, bound - receiver)
    shifted = jax.random.randint(jax.random.fold_in(own_key, 1), (twos,), 0, 1 << 20) % (margin + 1)
    tallies = tallies.at[1:1 + 2 * twos:2].set(source_of - shifted).at[2:2 + 2 * twos:2].set(receiver + shifted)
    return tallies[jax.random.permutation(jax.random.fold_in(own_key, 2), number_of)]


def normal_values(rng, shape, spread, reach, shards=(), held_as=jnp.bfloat16):
    result = jax.random.normal(rng, shape, jnp.float32) * spread
    if len(shards) > 0:
        result = steps_of(rng, shape, shards, -0.22, 0.18) * result
    return jnp.clip(result, min=-reach, max=reach).astype(held_as)


def setup_inputs(seed: int = 0, part: int = 0) -> dict:
    keys = jax.random.split(jax.random.key(seed), 12)
    own_keys = jax.random.split(jax.random.fold_in(keys[11], part), 12)
    tokens = normal_values(own_keys[0], (TOKENS, MODEL_FEATURES), 1.0, 6.0, ((0, 4), (1, 4)))
    token_job_index = jnp.searchsorted(jnp.cumsum(uneven_parts(own_keys[1], JOBS, TOKENS, TOKENS // 2, 2)), jnp.arange(TOKENS), side="right").astype(jnp.int32)
    job_adapter_index = plant(jax.random.randint(own_keys[2], (JOBS,), 0, ADAPTER_COUNT), jax.random.fold_in(own_keys[2], 1), 0, ADAPTER_COUNT - 1).astype(jnp.int32)
    first_weight = normal_values(keys[3], (MODEL_FEATURES, HIDDEN_UNITS), MODEL_FEATURES ** -0.5, 0.0625, ((0, 4), (1, 4)))
    first_bias = normal_values(keys[4], (HIDDEN_UNITS,), 0.5, 3.0, ((0, 4),), jnp.float32)
    first_down_maps = normal_values(keys[5], (MODEL_FEATURES, ADAPTER_COUNT * ADAPTER_RANK), MODEL_FEATURES ** -0.5, 0.0625, ((0, 4),))
    first_up_maps = normal_values(keys[6], (ADAPTER_COUNT * ADAPTER_RANK, HIDDEN_UNITS), ADAPTER_RANK ** -0.5, 1.5, ((1, 4),))
    second_weight = normal_values(keys[7], (HIDDEN_UNITS, MODEL_FEATURES), HIDDEN_UNITS ** -0.5, 0.0390625, ((0, 4), (1, 4)))
    second_bias = normal_values(keys[8], (MODEL_FEATURES,), 0.5, 3.0, ((0, 4),), jnp.float32)
    second_down_maps = normal_values(keys[9], (HIDDEN_UNITS, ADAPTER_COUNT * ADAPTER_RANK), HIDDEN_UNITS ** -0.5, 0.0390625, ((0, 4),))
    second_up_maps = normal_values(keys[10], (ADAPTER_COUNT * ADAPTER_RANK, MODEL_FEATURES), ADAPTER_RANK ** -0.5, 1.5, ((1, 4),))
    return dict(tokens=tokens, token_job_index=token_job_index, job_adapter_index=job_adapter_index, first_weight=first_weight, first_bias=first_bias, first_down_maps=first_down_maps, first_up_maps=first_up_maps, second_weight=second_weight, second_bias=second_bias, second_down_maps=second_down_maps, second_up_maps=second_up_maps)


def gelu_tanh(values):
    return 0.5 * values * (1.0 + jnp.tanh(0.7978845608 * (values + 0.044715 * values * values * values)))


def token_mask(token_job_index, job_adapter_index):
    one_hot = token_job_index[:, None] == jnp.arange(JOBS, dtype=jnp.int32)[None, :]
    chosen = jnp.sum(jnp.where(one_hot, job_adapter_index[None, :], 0), axis=1).astype(jnp.int32)
    slot_ids = jnp.arange(ADAPTER_COUNT * ADAPTER_RANK, dtype=jnp.int32) // ADAPTER_RANK
    return (slot_ids[None, :] == chosen[:, None]).astype(jnp.int32)


def block_partial_sum(left, first_right, second_right, blocks):
    block_width = left.shape[1] // blocks
    running = jnp.zeros((left.shape[0], first_right.shape[1] + second_right.shape[1]), jnp.float32)
    for block in range(blocks):
        lower = block * block_width
        upper = lower + block_width
        left_block = left[:, lower:upper].astype(jnp.float32)
        partial_value = jnp.concatenate([
            jnp.dot(left_block, first_right[lower:upper].astype(jnp.float32)),
            jnp.dot(left_block, second_right[lower:upper].astype(jnp.float32))], axis=1)
        rounded = lax.optimization_barrier(partial_value.astype(jnp.bfloat16))
        running = running + rounded.astype(jnp.float32)
    return running


def reference(tokens, token_job_index, job_adapter_index, first_weight, first_bias, first_down_maps, first_up_maps, second_weight, second_bias, second_down_maps, second_up_maps):
    chosen_mask = token_mask(token_job_index, job_adapter_index)
    first_layer_total = block_partial_sum(tokens, first_weight, first_down_maps, N_ROW)
    first_reduced = jnp.where(chosen_mask == 1, first_layer_total[:, HIDDEN_UNITS:], 0.0).astype(jnp.bfloat16)
    preactivation_sum = first_layer_total[:, :HIDDEN_UNITS] + first_bias[None, :] + jnp.dot(first_reduced, first_up_maps, preferred_element_type=jnp.float32)
    hidden_state = gelu_tanh(preactivation_sum).astype(jnp.bfloat16)
    second_layer_total = block_partial_sum(hidden_state, second_weight, second_down_maps, N_COL)
    second_reduced = jnp.where(chosen_mask == 1, second_layer_total[:, MODEL_FEATURES:], 0.0).astype(jnp.bfloat16)
    layer_output = second_layer_total[:, :MODEL_FEATURES] + second_bias[None, :] + jnp.dot(second_reduced, second_up_maps, preferred_element_type=jnp.float32)
    return layer_output.astype(jnp.bfloat16)
```

```python
import jax
import jax.numpy as jnp
from jax import lax
from jax.sharding import PartitionSpec as P

ADAPTER_RANK = 16
ADAPTER_COUNT = 8
JOBS = 4
CHUNKS = 8
F32 = jnp.float32
BF16 = jnp.bfloat16


def gelu_tanh(values):
    return (
        0.5
        * values
        * (1.0 + jnp.tanh(0.7978845608 * (values + 0.044715 * values * values * values)))
    )


def token_mask(token_job_index, job_adapter_index):
    one_hot = token_job_index[:, None] == jnp.arange(JOBS, dtype=jnp.int32)[None, :]
    chosen = jnp.sum(jnp.where(one_hot, job_adapter_index[None, :], 0), axis=1)
    slot_ids = jnp.arange(ADAPTER_COUNT * ADAPTER_RANK, dtype=jnp.int32) // ADAPTER_RANK
    return slot_ids[None, :] == chosen[:, None]


def dot(left, right):
    return jnp.dot(left, right, preferred_element_type=F32)


def add_rounded(left, right):
    return (left.astype(F32) + right.astype(F32)).astype(BF16)


def make_local(n_row, n_col):
    chips = n_col // 2
    half = n_row // 2

    def col_swap(value, flip):
        return lax.ppermute(value, "col", [(i, i ^ flip) for i in range(n_col)])

    def gather_tokens(tokens):
        shards = [tokens, col_swap(tokens, 1)]
        for step in range(1, chips):
            far = col_swap(tokens, 2 * step)
            shards += [far, col_swap(far, 1)]
        return jnp.concatenate(shards, axis=0)

    def fold_rows(value):
        for step in range(half - 1):
            pairs = [(step, step + 1), (n_row - 1 - step, n_row - 2 - step)]
            value = add_rounded(value, lax.ppermute(value, "row", pairs))
        return value

    def cross_rows(value):
        if n_row == 1:
            return value.astype(F32)
        other = lax.ppermute(value, "row", [(half - 1, half), (half, half - 1)])
        return value.astype(F32) + other.astype(F32)

    def spread_rows(value, place):
        for step in reversed(range(half - 1)):
            pairs = [(step + 1, step), (n_row - 2 - step, n_row - 1 - step)]
            come = lax.ppermute(value, "row", pairs)
            value = jnp.where((place <= step) | (place >= n_row - 1 - step), come, value)
        return value

    def local(
        tokens,
        token_job_index,
        job_adapter_index,
        first_weight,
        first_bias,
        first_down_maps,
        first_up_maps,
        second_weight,
        second_bias,
        second_down_maps,
        second_up_maps,
    ):
        rows = tokens.shape[0]
        hidden = first_weight.shape[1]
        width = hidden // CHUNKS
        out_width = second_weight.shape[1]
        place = lax.axis_index("row")
        mine = lax.axis_index("col")
        mask_all = token_mask(token_job_index, job_adapter_index)
        mask = jnp.concatenate(
            [
                lax.dynamic_slice_in_dim(mask_all, (mine ^ i) * rows, rows, 0)
                for i in range(n_col)
            ],
            axis=0,
        )
        gathered = gather_tokens(tokens)
        total = None
        low_in = None
        for chunk in range(CHUNKS):
            span = slice(chunk * width, (chunk + 1) * width)
            partial = dot(gathered, first_weight[:, span]).astype(BF16)
            if chunk == 0:
                low = dot(gathered, first_down_maps).astype(BF16)
                partial = jnp.concatenate([partial, low], axis=1)
            summed = cross_rows(fold_rows(partial))
            if chunk == 0:
                low_in = jnp.where(mask, summed[:, width:], 0.0).astype(BF16)
                summed = summed[:, :width]
            before = summed + first_bias[None, span] + dot(low_in, first_up_maps[:, span])
            states = spread_rows(gelu_tanh(before).astype(BF16), place)
            part = dot(states, second_weight[span])
            low_part = dot(states, second_down_maps[span])
            total = part if total is None else total + part
            low_total = low_part if chunk == 0 else low_total + low_part
        outputs = jnp.concatenate([total, low_total], axis=1)
        blocks = [outputs[i * rows : (i + 1) * rows] for i in range(n_col)]
        ours = jnp.concatenate(blocks[0::2], axis=0)
        theirs = jnp.concatenate(blocks[1::2], axis=0).astype(BF16)
        ours = ours + col_swap(theirs, 1).astype(F32)
        result = ours[:rows]
        for step in range(1, chips):
            piece = ours[step * rows : (step + 1) * rows].astype(BF16)
            result = result + col_swap(piece, 2 * step).astype(F32)
        low_out = jnp.where(mask[:rows], result[:, out_width:], 0.0).astype(BF16)
        layer_output = result[:, :out_width] + second_bias[None, :] + dot(low_out, second_up_maps)
        return layer_output.astype(BF16)

    return local


def solution(mesh):
    return jax.shard_map(
        make_local(mesh.shape["row"], mesh.shape["col"]),
        mesh=mesh,
        in_specs=(
            P(("group", "col"), "row"),
            P("group"),
            P("group"),
            P("row", "col"),
            P("col"),
            P("row", None),
            P(None, "col"),
            P("col", "row"),
            P("row"),
            P("col", None),
            P(None, "row"),
        ),
        out_specs=P(("group", "col"), "row"),
        check_vma=False,
    )
```

```python
import functools

import jax
import jax.numpy as jnp
from jax import lax
from jax.experimental import pallas as pl
from jax.experimental.pallas import tpu as pltpu
from jax.sharding import PartitionSpec as P

ADAPTER_RANK = 16
ADAPTER_COUNT = 8
JOBS = 4
LANES = 128
AHEAD = 2
F32 = jnp.float32
BF16 = jnp.bfloat16
ANY = pl.BlockSpec(memory_space=pl.ANY)
COST = pl.CostEstimate(flops=1000, bytes_accessed=1000, transcendentals=0)
PARAMS = pltpu.CompilerParams(vmem_limit_bytes=30 << 20)


def gelu_tanh(values):
    return (
        0.5
        * values
        * (1.0 + jnp.tanh(0.7978845608 * (values + 0.044715 * values * values * values)))
    )


def token_mask(token_job_index, job_adapter_index):
    one_hot = token_job_index[:, None] == jnp.arange(JOBS, dtype=jnp.int32)[None, :]
    chosen = jnp.sum(jnp.where(one_hot, job_adapter_index[None, :], 0), axis=1)
    slot_ids = jnp.arange(ADAPTER_COUNT * ADAPTER_RANK, dtype=jnp.int32) // ADAPTER_RANK
    return slot_ids[None, :] == chosen[:, None]


def dot(left, right):
    return jnp.dot(left, right, preferred_element_type=F32)


def tile_of(width, most):
    tile = LANES
    for count in range(2, most // LANES + 1):
        if width % (count * LANES) == 0:
            tile = count * LANES
    return tile


def whole(shape):
    return pl.BlockSpec(shape, lambda *_: (0,) * len(shape))


def chunk_spans(hidden):
    units = hidden // LANES
    count = max(n for n in range(1, 9) if units % n == 0)
    width = hidden // count
    return [(start, width) for start in range(0, hidden, width)]


def first_kernel(x_ref, w_ref, after_ref, out_ref):
    out_ref[...] = dot(x_ref[...], w_ref[...]).astype(BF16)


def first_product(x, weight, span, after):
    start, width = span
    tile = tile_of(width, 256)
    while start % tile:
        tile -= LANES
    base = start // tile
    return pl.pallas_call(
        first_kernel,
        grid=(width // tile,),
        in_specs=[
            whole(x.shape),
            pl.BlockSpec((x.shape[1], tile), lambda j: (0, base + j)),
            ANY,
        ],
        out_specs=pl.BlockSpec((x.shape[0], tile), lambda j: (0, j)),
        out_shape=jax.ShapeDtypeStruct((x.shape[0], width), BF16),
        compiler_params=PARAMS,
        cost_estimate=COST,
    )(x, weight, after)


def low_kernel(x_ref, w_ref, d_ref, after_ref, out_ref, *, tiles, width):
    j = pl.program_id(0)

    @pl.when(j < tiles)
    def _():
        out_ref[...] = dot(x_ref[...], w_ref[...]).astype(BF16)

    @pl.when(j == tiles)
    def _():
        out_ref[...] = dot(x_ref[...], d_ref[...]).astype(BF16)


def first_product_low(x, weight, down, span, after):
    start, width = span
    tile = LANES
    tiles = width // tile
    low = down.shape[1]
    return pl.pallas_call(
        functools.partial(low_kernel, tiles=tiles, width=width),
        grid=(tiles + 1,),
        in_specs=[
            whole(x.shape),
            pl.BlockSpec((x.shape[1], tile), lambda j: (0, start // tile + jnp.minimum(j, tiles - 1))),
            whole(down.shape),
            ANY,
        ],
        out_specs=pl.BlockSpec((x.shape[0], tile), lambda j: (0, j)),
        out_shape=jax.ShapeDtypeStruct((x.shape[0], width + low), BF16),
        compiler_params=PARAMS,
        cost_estimate=COST,
    )(x, weight, down, after)


def add_kernel(a_ref, b_ref, after_ref, out_ref):
    out_ref[...] = (a_ref[...].astype(F32) + b_ref[...].astype(F32)).astype(BF16)


def add_rounded(a, b, after):
    return pl.pallas_call(
        add_kernel,
        grid=(1,),
        in_specs=[whole(a.shape), whole(b.shape), ANY],
        out_specs=whole(a.shape),
        out_shape=jax.ShapeDtypeStruct(a.shape, BF16),
        compiler_params=PARAMS,
        cost_estimate=COST,
    )(a, b, after)


def gelu_kernel(m_ref, low_ref, up_ref, bias_ref, after_ref, out_ref):
    summed = m_ref[0].astype(F32) + m_ref[1].astype(F32)
    before = summed + bias_ref[...] + dot(low_ref[...], up_ref[...])
    out_ref[...] = gelu_tanh(before).astype(BF16)


def gelu_chunk(pair, low_in, up_maps, bias, span, after):
    start, width = span
    rows = pair.shape[1]
    tile = tile_of(width, 256)
    while start % tile:
        tile -= LANES
    base = start // tile
    return pl.pallas_call(
        gelu_kernel,
        grid=(width // tile,),
        in_specs=[
            pl.BlockSpec((2, rows, tile), lambda j: (0, 0, j)),
            whole(low_in.shape),
            pl.BlockSpec((up_maps.shape[0], tile), lambda j: (0, base + j)),
            pl.BlockSpec((1, tile), lambda j: (0, base + j)),
            ANY,
        ],
        out_specs=pl.BlockSpec((rows, tile), lambda j: (0, j)),
        out_shape=jax.ShapeDtypeStruct((rows, width), BF16),
        compiler_params=PARAMS,
        cost_estimate=COST,
    )(pair, low_in, up_maps, bias, after)


def second_kernel(end_ref, h_ref, r_ref, w_ref, d_ref, acc_ref, low_ref, after_ref, out_ref, low_out_ref, state, *, first):
    j = pl.program_id(0)

    @pl.when(j == 0)
    def _():
        @pl.when(end_ref[0] == 1)
        def _():
            state[...] = r_ref[...]

        @pl.when(end_ref[0] == 0)
        def _():
            state[...] = h_ref[...]

        low = dot(state[...], d_ref[...])
        low_out_ref[...] = low if first else low + low_ref[...]

    part = dot(state[...], w_ref[...])
    out_ref[...] = part if first else part + acc_ref[...]


def second_product(is_end, h, r, weight, down, total, low_total, span, after):
    start, width = span
    rows = h.shape[0]
    out_width = weight.shape[1]
    tile = tile_of(out_width, 512)
    first = total is None
    base = start // width
    if first:
        total, low_total = after, after
        total_spec, low_spec = ANY, ANY
    else:
        total_spec = pl.BlockSpec((rows, tile), lambda j: (0, j))
        low_spec = whole((rows, down.shape[1]))
    return pl.pallas_call(
        functools.partial(second_kernel, first=first),
        grid=(out_width // tile,),
        in_specs=[
            pl.BlockSpec(memory_space=pltpu.SMEM),
            whole(h.shape),
            whole(r.shape),
            pl.BlockSpec((width, tile), lambda j: (base, j)),
            pl.BlockSpec((width, down.shape[1]), lambda j: (base, 0)),
            total_spec,
            low_spec,
            ANY,
        ],
        out_specs=[
            pl.BlockSpec((rows, tile), lambda j: (0, j)),
            whole((rows, down.shape[1])),
        ],
        out_shape=[
            jax.ShapeDtypeStruct((rows, out_width), F32),
            jax.ShapeDtypeStruct((rows, down.shape[1]), F32),
        ],
        scratch_shapes=[pltpu.VMEM(h.shape, BF16)],
        compiler_params=PARAMS,
        cost_estimate=COST,
    )(is_end, h, r, weight, down, total, low_total, after)


def make_local(n_group, n_row, n_col):
    chips = n_col // 2
    half = n_row // 2

    def place_of(group, row, col):
        return (group * n_row + row) * n_col + col

    cross_groups = []
    for group in range(n_group):
        for col in range(n_col):
            cross_groups.append([place_of(group, half - 1, col), place_of(group, half, col)])
        for row in range(n_row):
            if row not in (half - 1, half):
                for col in range(0, n_col, 2):
                    cross_groups.append([place_of(group, row, col), place_of(group, row, col + 1)])

    def col_swap(value, flip):
        return lax.ppermute(value, "col", [(i, i ^ flip) for i in range(n_col)])

    def gather_tokens(tokens):
        shards = [tokens, col_swap(tokens, 1)]
        for step in range(1, chips):
            far = col_swap(tokens, 2 * step)
            shards += [far, col_swap(far, 1)]
        return jnp.concatenate(shards, axis=0)

    def fold(value, step):
        pairs = [(step, step + 1), (n_row - 1 - step, n_row - 2 - step)]
        return lax.ppermute(value, "row", pairs)

    def cross(value):
        return lax.all_gather(
            value, ("group", "row", "col"), axis=0, tiled=False, axis_index_groups=cross_groups
        )

    def spread(value, place):
        for step in reversed(range(half - 1)):
            pairs = [(step + 1, step), (n_row - 2 - step, n_row - 1 - step)]
            come = lax.ppermute(value, "row", pairs)
            if step > 0:
                value = jnp.where((place <= step) | (place >= n_row - 1 - step), come, value)
            else:
                value = come
        return value

    def local(
        tokens,
        token_job_index,
        job_adapter_index,
        first_weight,
        first_bias,
        first_down_maps,
        first_up_maps,
        second_weight,
        second_bias,
        second_down_maps,
        second_up_maps,
    ):
        rows = tokens.shape[0]
        hidden = first_weight.shape[1]
        out_width = second_weight.shape[1]
        spans = chunk_spans(hidden)
        count = len(spans)
        place = lax.axis_index("row")
        mine = lax.axis_index("col")
        edge = (place == 0) | (place == n_row - 1)
        is_end = edge.astype(jnp.int32).reshape(1)
        bias = first_bias[None, :]
        mask_all = token_mask(token_job_index, job_adapter_index)
        mask = jnp.concatenate(
            [
                lax.dynamic_slice_in_dim(mask_all, (mine ^ i) * rows, rows, 0)
                for i in range(n_col)
            ],
            axis=0,
        )
        gathered = gather_tokens(tokens)
        last = gathered
        partials, folded, pairs, states, returned = {}, {}, {}, {}, {}
        total, low_total, low_in = None, None, None

        def start_chunk(t):
            nonlocal last
            if t == 0:
                last = first_product_low(gathered, first_weight, first_down_maps, spans[t], last)
            else:
                last = first_product(gathered, first_weight, spans[t], last)
            partials[t] = last
            folded[t] = fold(last, 0)

        for t in range(min(AHEAD, count)):
            start_chunk(t)
        for t in range(count + 2):
            if t < count:
                value = add_rounded(partials[t], folded[t], last)
                for step in range(1, half - 1):
                    value = add_rounded(value, fold(value, step), value)
                last = value
                pairs[t] = cross(value)
            if t + AHEAD < count:
                start_chunk(t + AHEAD)
            if 0 <= t - 1 < count:
                k = t - 1
                width = spans[k][1]
                if k == 0:
                    low = pairs[k][:, :, width:].astype(F32)
                    low_in = jnp.where(mask, low[0] + low[1], 0.0).astype(BF16)
                last = gelu_chunk(pairs[k], low_in, first_up_maps, bias, spans[k], last)
                states[k] = last
                returned[k] = spread(last, place)
            if 0 <= t - 2 < count:
                k = t - 2
                total, low_total = second_product(
                    is_end, states[k], returned[k], second_weight, second_down_maps,
                    total, low_total, spans[k], last,
                )
                last = low_total
        outputs = jnp.concatenate([total, low_total], axis=1)
        blocks = [outputs[i * rows : (i + 1) * rows] for i in range(n_col)]
        ours = jnp.concatenate(blocks[0::2], axis=0)
        theirs = jnp.concatenate(blocks[1::2], axis=0).astype(BF16)
        ours = ours + col_swap(theirs, 1).astype(F32)
        result = ours[:rows]
        for step in range(1, chips):
            piece = ours[step * rows : (step + 1) * rows].astype(BF16)
            result = result + col_swap(piece, 2 * step).astype(F32)
        low_out = jnp.where(mask[:rows], result[:, out_width:], 0.0).astype(BF16)
        layer_output = result[:, :out_width] + second_bias[None, :] + dot(low_out, second_up_maps)
        return layer_output.astype(BF16)

    return local


def solution(mesh):
    shape = mesh.shape
    return jax.shard_map(
        make_local(shape["group"], shape["row"], shape["col"]),
        mesh=mesh,
        in_specs=(
            P(("group", "col"), "row"),
            P("group"),
            P("group"),
            P("row", "col"),
            P("col"),
            P("row", None),
            P(None, "col"),
            P("col", "row"),
            P("row"),
            P("col", None),
            P(None, "row"),
        ),
        out_specs=P(("group", "col"), "row"),
        check_vma=False,
    )
```

```python
import functools

import jax
import jax.numpy as jnp
from jax import lax
from jax.experimental import pallas as pl
from jax.experimental.pallas import tpu as pltpu
from jax.sharding import PartitionSpec as P

ADAPTER_RANK = 16
ADAPTER_COUNT = 8
JOBS = 4
LANES = 128
AHEAD = 2
F32 = jnp.float32
BF16 = jnp.bfloat16
ANY = pl.BlockSpec(memory_space=pl.ANY)
COST = pl.CostEstimate(flops=1000, bytes_accessed=1000, transcendentals=0)
PARAMS = pltpu.CompilerParams(vmem_limit_bytes=30 << 20)


def gelu_tanh(values):
    return (
        0.5
        * values
        * (1.0 + jnp.tanh(0.7978845608 * (values + 0.044715 * values * values * values)))
    )


def token_mask(token_job_index, job_adapter_index):
    one_hot = token_job_index[:, None] == jnp.arange(JOBS, dtype=jnp.int32)[None, :]
    chosen = jnp.sum(jnp.where(one_hot, job_adapter_index[None, :], 0), axis=1)
    slot_ids = jnp.arange(ADAPTER_COUNT * ADAPTER_RANK, dtype=jnp.int32) // ADAPTER_RANK
    return slot_ids[None, :] == chosen[:, None]


def dot(left, right):
    return jnp.dot(left, right, preferred_element_type=F32)


def tile_of(width, most):
    tile = LANES
    for count in range(2, most // LANES + 1):
        if width % (count * LANES) == 0:
            tile = count * LANES
    return tile


def whole(shape):
    return pl.BlockSpec(shape, lambda *_: (0,) * len(shape))


def chunk_spans(hidden):
    units = hidden // LANES
    count = max(n for n in range(1, 5) if units % n == 0)
    width = hidden // count
    return [(start, width) for start in range(0, hidden, width)]


def first_kernel(x_ref, w_ref, after_ref, out_ref):
    out_ref[...] = dot(x_ref[...], w_ref[...]).astype(BF16)


def first_product(x, weight, span, after):
    start, width = span
    tile = tile_of(width, 256)
    while start % tile:
        tile -= LANES
    base = start // tile
    return pl.pallas_call(
        first_kernel,
        grid=(width // tile,),
        in_specs=[
            whole(x.shape),
            pl.BlockSpec((x.shape[1], tile), lambda j: (0, base + j)),
            ANY,
        ],
        out_specs=pl.BlockSpec((x.shape[0], tile), lambda j: (0, j)),
        out_shape=jax.ShapeDtypeStruct((x.shape[0], width), BF16),
        compiler_params=PARAMS,
        cost_estimate=COST,
    )(x, weight, after)


def low_kernel(x_ref, w_ref, d_ref, after_ref, out_ref, *, tiles, width):
    j = pl.program_id(0)

    @pl.when(j < tiles)
    def _():
        out_ref[...] = dot(x_ref[...], w_ref[...]).astype(BF16)

    @pl.when(j == tiles)
    def _():
        out_ref[...] = dot(x_ref[...], d_ref[...]).astype(BF16)


def first_product_low(x, weight, down, span, after):
    start, width = span
    tile = LANES
    tiles = width // tile
    low = down.shape[1]
    return pl.pallas_call(
        functools.partial(low_kernel, tiles=tiles, width=width),
        grid=(tiles + 1,),
        in_specs=[
            whole(x.shape),
            pl.BlockSpec((x.shape[1], tile), lambda j: (0, start // tile + jnp.minimum(j, tiles - 1))),
            whole(down.shape),
            ANY,
        ],
        out_specs=pl.BlockSpec((x.shape[0], tile), lambda j: (0, j)),
        out_shape=jax.ShapeDtypeStruct((x.shape[0], width + low), BF16),
        compiler_params=PARAMS,
        cost_estimate=COST,
    )(x, weight, down, after)


def tie(value, after):
    return lax.optimization_barrier((value, after))[0]


def add_rounded(a, b, after):
    return (tie(a, after).astype(F32) + b.astype(F32)).astype(BF16)


def gelu_chunk(pair, low_in, up_maps, bias, span, after):
    start, width = span
    part = slice(start, start + width)
    pair = tie(pair, after)[:, :, :width].astype(F32)
    before = pair[0] + pair[1] + bias[:, part] + dot(low_in, up_maps[:, part])
    return gelu_tanh(before).astype(BF16)


def second_kernel(end_ref, h_ref, r_ref, w_ref, d_ref, acc_ref, low_ref, after_ref, out_ref, low_out_ref, state, *, first):
    j = pl.program_id(0)

    @pl.when(j == 0)
    def _():
        @pl.when(end_ref[0] == 1)
        def _():
            state[...] = r_ref[...]

        @pl.when(end_ref[0] == 0)
        def _():
            state[...] = h_ref[...]

        low = dot(state[...], d_ref[...])
        low_out_ref[...] = low if first else low + low_ref[...]

    part = dot(state[...], w_ref[...])
    out_ref[...] = part if first else part + acc_ref[...]


def second_product(is_end, h, r, weight, down, total, low_total, span, after):
    start, width = span
    rows = h.shape[0]
    out_width = weight.shape[1]
    tile = tile_of(out_width, 512)
    first = total is None
    base = start // width
    if first:
        total, low_total = after, after
        total_spec, low_spec = ANY, ANY
    else:
        total_spec = pl.BlockSpec((rows, tile), lambda j: (0, j))
        low_spec = whole((rows, down.shape[1]))
    return pl.pallas_call(
        functools.partial(second_kernel, first=first),
        grid=(out_width // tile,),
        in_specs=[
            pl.BlockSpec(memory_space=pltpu.SMEM),
            whole(h.shape),
            whole(r.shape),
            pl.BlockSpec((width, tile), lambda j: (base, j)),
            pl.BlockSpec((width, down.shape[1]), lambda j: (base, 0)),
            total_spec,
            low_spec,
            ANY,
        ],
        out_specs=[
            pl.BlockSpec((rows, tile), lambda j: (0, j)),
            whole((rows, down.shape[1])),
        ],
        out_shape=[
            jax.ShapeDtypeStruct((rows, out_width), F32),
            jax.ShapeDtypeStruct((rows, down.shape[1]), F32),
        ],
        scratch_shapes=[pltpu.VMEM(h.shape, BF16)],
        compiler_params=PARAMS,
        cost_estimate=COST,
    )(is_end, h, r, weight, down, total, low_total, after)


def make_local(n_group, n_row, n_col):
    chips = n_col // 2
    half = n_row // 2

    def place_of(group, row, col):
        return (group * n_row + row) * n_col + col

    cross_groups = []
    for group in range(n_group):
        for col in range(n_col):
            cross_groups.append([place_of(group, half - 1, col), place_of(group, half, col)])
        for row in range(n_row):
            if row not in (half - 1, half):
                for col in range(0, n_col, 2):
                    cross_groups.append([place_of(group, row, col), place_of(group, row, col + 1)])

    def col_swap(value, flip):
        return lax.ppermute(value, "col", [(i, i ^ flip) for i in range(n_col)])

    def gather_tokens(tokens):
        shards = [tokens, col_swap(tokens, 1)]
        for step in range(1, chips):
            far = col_swap(tokens, 2 * step)
            shards += [far, col_swap(far, 1)]
        return jnp.concatenate(shards, axis=0)

    def fold(value, step):
        pairs = [(step, step + 1), (n_row - 1 - step, n_row - 2 - step)]
        return lax.ppermute(value, "row", pairs)

    def cross(value):
        return lax.all_gather(
            value, ("group", "row", "col"), axis=0, tiled=False, axis_index_groups=cross_groups
        )

    def spread(value, place):
        for step in reversed(range(half - 1)):
            pairs = [(step + 1, step), (n_row - 2 - step, n_row - 1 - step)]
            come = lax.ppermute(value, "row", pairs)
            if step > 0:
                value = jnp.where((place <= step) | (place >= n_row - 1 - step), come, value)
            else:
                value = come
        return value

    def local(
        tokens,
        token_job_index,
        job_adapter_index,
        first_weight,
        first_bias,
        first_down_maps,
        first_up_maps,
        second_weight,
        second_bias,
        second_down_maps,
        second_up_maps,
    ):
        rows = tokens.shape[0]
        hidden = first_weight.shape[1]
        out_width = second_weight.shape[1]
        spans = chunk_spans(hidden)
        count = len(spans)
        place = lax.axis_index("row")
        mine = lax.axis_index("col")
        edge = (place == 0) | (place == n_row - 1)
        is_end = edge.astype(jnp.int32).reshape(1)
        bias = first_bias[None, :]
        mask_all = token_mask(token_job_index, job_adapter_index)
        mask = jnp.concatenate(
            [
                lax.dynamic_slice_in_dim(mask_all, (mine ^ i) * rows, rows, 0)
                for i in range(n_col)
            ],
            axis=0,
        )
        gathered = gather_tokens(tokens)
        last = gathered
        partials, folded, pairs, states, returned = {}, {}, {}, {}, {}
        total, low_total, low_in = None, None, None

        def start_chunk(t):
            nonlocal last
            if t == 0:
                last = first_product_low(gathered, first_weight, first_down_maps, spans[t], last)
            else:
                last = first_product(gathered, first_weight, spans[t], last)
            partials[t] = last
            folded[t] = fold(last, 0)

        for t in range(min(AHEAD, count)):
            start_chunk(t)
        for t in range(count + 2):
            if t < count:
                value = add_rounded(partials[t], folded[t], last)
                for step in range(1, half - 1):
                    value = add_rounded(value, fold(value, step), value)
                last = value
                pairs[t] = cross(value)
            if t + AHEAD < count:
                start_chunk(t + AHEAD)
            if 0 <= t - 1 < count:
                k = t - 1
                width = spans[k][1]
                if k == 0:
                    low = pairs[k][:, :, width:].astype(F32)
                    low_in = jnp.where(mask, low[0] + low[1], 0.0).astype(BF16)
                last = gelu_chunk(pairs[k], low_in, first_up_maps, bias, spans[k], last)
                states[k] = last
                returned[k] = spread(last, place)
            if 0 <= t - 2 < count:
                k = t - 2
                total, low_total = second_product(
                    is_end, states[k], returned[k], second_weight, second_down_maps,
                    total, low_total, spans[k], last,
                )
                last = low_total
        outputs = jnp.concatenate([total, low_total], axis=1)
        blocks = [outputs[i * rows : (i + 1) * rows] for i in range(n_col)]
        ours = jnp.concatenate(blocks[0::2], axis=0)
        theirs = jnp.concatenate(blocks[1::2], axis=0).astype(BF16)
        ours = ours + col_swap(theirs, 1).astype(F32)
        result = ours[:rows]
        for step in range(1, chips):
            piece = ours[step * rows : (step + 1) * rows].astype(BF16)
            result = result + col_swap(piece, 2 * step).astype(F32)
        low_out = jnp.where(mask[:rows], result[:, out_width:], 0.0).astype(BF16)
        layer_output = result[:, :out_width] + second_bias[None, :] + dot(low_out, second_up_maps)
        return layer_output.astype(BF16)

    return local


def solution(mesh):
    shape = mesh.shape
    return jax.shard_map(
        make_local(shape["group"], shape["row"], shape["col"]),
        mesh=mesh,
        in_specs=(
            P(("group", "col"), "row"),
            P("group"),
            P("group"),
            P("row", "col"),
            P("col"),
            P("row", None),
            P(None, "col"),
            P("col", "row"),
            P("row"),
            P("col", None),
            P(None, "row"),
        ),
        out_specs=P(("group", "col"), "row"),
        check_vma=False,
    )
```

```python
import functools

import jax
import jax.numpy as jnp
import numpy as np
from jax import lax
from jax.experimental import pallas as pl
from jax.experimental.pallas import tpu as pltpu
from jax.sharding import PartitionSpec as P

ADAPTER_RANK = 16
ADAPTER_COUNT = 8
JOBS = 4
LANES = 128
AHEAD = 2
SHARES = (6, 8, 8, 8, 8, 6, 4)
PER_CALL = 2
F32 = jnp.float32
BF16 = jnp.bfloat16
ANY = pl.BlockSpec(memory_space=pl.ANY)
COST = pl.CostEstimate(flops=1000, bytes_accessed=1000, transcendentals=0)
PARAMS = pltpu.CompilerParams(vmem_limit_bytes=34 << 20)


def gelu_tanh(values):
    return (
        0.5
        * values
        * (1.0 + jnp.tanh(0.7978845608 * (values + 0.044715 * values * values * values)))
    )


def token_mask(token_job_index, job_adapter_index):
    one_hot = token_job_index[:, None] == jnp.arange(JOBS, dtype=jnp.int32)[None, :]
    chosen = jnp.sum(jnp.where(one_hot, job_adapter_index[None, :], 0), axis=1)
    slot_ids = jnp.arange(ADAPTER_COUNT * ADAPTER_RANK, dtype=jnp.int32) // ADAPTER_RANK
    return slot_ids[None, :] == chosen[:, None]


def dot(left, right):
    return jnp.dot(left, right, preferred_element_type=F32)


def tiles_of(width, most):
    tiles, start = [], 0
    while start < width:
        size = min(most, width - start)
        tiles.append((start, size))
        start += size
    return tiles


def chunk_spans(hidden):
    units = hidden // LANES
    cuts = [round(units * part / sum(SHARES)) for part in np.cumsum((0,) + SHARES)]
    return [(lo * LANES, (hi - lo) * LANES) for lo, hi in zip(cuts, cuts[1:]) if hi > lo]


def first_kernel(*refs, start, tiles, low):
    x_hbm, w_hbm = refs[:2]
    d_hbm = refs[2] if low else None
    out_hbm, x_v, w_v, d_v, o_v, x_sem, w_sem, d_sem, o_sem = refs[-9:]
    width = tiles[-1][0] + tiles[-1][1]
    x_copy = pltpu.make_async_copy(x_hbm, x_v, x_sem)
    w_copies = [
        pltpu.make_async_copy(
            w_hbm.at[:, pl.ds(start + at, size)], w_v.at[:, pl.ds(at, size)], w_sem.at[i]
        )
        for i, (at, size) in enumerate(tiles)
    ]
    w_copies[0].start()
    x_copy.start()
    for copy in w_copies[1:]:
        copy.start()
    sent = []

    def finish(at, size, right, sem):
        o_v[:, pl.ds(at, size)] = dot(x_v[...], right).astype(BF16)
        copy = pltpu.make_async_copy(o_v.at[:, pl.ds(at, size)], out_hbm.at[:, pl.ds(at, size)], sem)
        copy.start()
        sent.append(copy)

    if low:
        d_copy = pltpu.make_async_copy(d_hbm, d_v, d_sem)
        d_copy.start()
    x_copy.wait()
    for i, (at, size) in enumerate(tiles):
        w_copies[i].wait()
        finish(at, size, w_v[:, pl.ds(at, size)], o_sem.at[i])
    if low:
        d_copy.wait()
        finish(width, LANES, d_v[...], o_sem.at[len(tiles)])
    for copy in sent:
        copy.wait()


def first_product(x, weight, down, span, after):
    start, width = span
    rows, depth = x.shape
    low = down is not None
    tiles = tiles_of(width, 256)
    total = width + (LANES if low else 0)
    operands = [x, weight] + ([down] if low else []) + [after]
    return pl.pallas_call(
        functools.partial(first_kernel, start=start, tiles=tiles, low=low),
        in_specs=[ANY] * len(operands),
        out_specs=ANY,
        out_shape=jax.ShapeDtypeStruct((rows, total), BF16),
        scratch_shapes=[
            pltpu.VMEM((rows, depth), BF16),
            pltpu.VMEM((depth, width), BF16),
            pltpu.VMEM((depth if low else 16, LANES), BF16),
            pltpu.VMEM((rows, total), BF16),
            pltpu.SemaphoreType.DMA,
            pltpu.SemaphoreType.DMA((len(tiles),)),
            pltpu.SemaphoreType.DMA,
            pltpu.SemaphoreType.DMA((len(tiles) + 1,)),
        ],
        compiler_params=PARAMS,
        cost_estimate=COST,
    )(*operands)


def tie(value, after):
    return lax.optimization_barrier((value, after))[0]


def add_rounded(a, b, after):
    return (tie(a, after).astype(F32) + b.astype(F32)).astype(BF16)


def gelu_chunk(ours, theirs, low_in, up_maps, bias, span, after):
    start, width = span
    part = slice(start, start + width)
    summed = tie(ours, after)[:, :width].astype(F32) + theirs[:, :width].astype(F32)
    before = summed + bias[:, part] + dot(low_in, up_maps[:, part])
    return gelu_tanh(before).astype(BF16)


def second_kernel(*refs, count, widths, start, tiles, first):
    end_ref = refs[0]
    own_refs = refs[1 : 1 + count]
    come_refs = refs[1 + count : 1 + 2 * count]
    w_hbm, d_hbm = refs[1 + 2 * count : 3 + 2 * count]
    acc_hbm, low_hbm = (None, None) if first else refs[3 + 2 * count : 5 + 2 * count]
    (out_hbm, low_out_hbm, state, w_v, d_v, acc_v, low_v,
     s_sem, w_sem, d_sem, a_sem, l_sem, o_sem) = refs[-13:]
    depth = sum(widths)
    w_copies = [
        pltpu.make_async_copy(
            w_hbm.at[pl.ds(start, depth), pl.ds(at, size)], w_v.at[:, pl.ds(at, size)], w_sem.at[i]
        )
        for i, (at, size) in enumerate(tiles)
    ]
    w_copies[0].start()

    def load_states(sources):
        copies, at = [], 0
        for i, source in enumerate(sources):
            copy = pltpu.make_async_copy(source, state.at[:, pl.ds(at, widths[i])], s_sem.at[i])
            copy.start()
            copies.append(copy)
            at += widths[i]
        for copy in copies:
            copy.wait()

    for copy in w_copies[1:]:
        copy.start()
    d_copy = pltpu.make_async_copy(d_hbm.at[pl.ds(start, depth), :], d_v, d_sem)
    d_copy.start()
    if not first:
        a_copies = [
            pltpu.make_async_copy(acc_hbm.at[:, pl.ds(at, size)], acc_v.at[:, pl.ds(at, size)], a_sem.at[i])
            for i, (at, size) in enumerate(tiles)
        ]
        l_copy = pltpu.make_async_copy(low_hbm, low_v, l_sem)
        for copy in a_copies:
            copy.start()
        l_copy.start()

    @pl.when(end_ref[0] == 1)
    def _():
        load_states(come_refs)

    @pl.when(end_ref[0] == 0)
    def _():
        load_states(own_refs)

    sent = []
    for i, (at, size) in enumerate(tiles):
        part = pl.ds(at, size)
        w_copies[i].wait()
        if first:
            acc_v[:, part] = dot(state[...], w_v[:, part])
        else:
            a_copies[i].wait()
            acc_v[:, part] += dot(state[...], w_v[:, part])
        copy = pltpu.make_async_copy(acc_v.at[:, part], out_hbm.at[:, part], o_sem.at[i])
        copy.start()
        sent.append(copy)
    d_copy.wait()
    if first:
        low_v[...] = dot(state[...], d_v[...])
    else:
        l_copy.wait()
        low_v[...] += dot(state[...], d_v[...])
    copy = pltpu.make_async_copy(low_v, low_out_hbm, o_sem.at[len(tiles)])
    copy.start()
    sent.append(copy)
    for copy in sent:
        copy.wait()


def second_product(is_end, own, come, weight, down, total, low_total, start, after):
    rows = own[0].shape[0]
    widths = [h.shape[1] for h in own]
    depth = sum(widths)
    out_width = weight.shape[1]
    tiles = tiles_of(out_width, 512)
    first = total is None
    operands = [*own, *come, weight, down] + ([] if first else [total, low_total]) + [after]
    return pl.pallas_call(
        functools.partial(
            second_kernel, count=len(own), widths=widths, start=start, tiles=tiles, first=first
        ),
        in_specs=[pl.BlockSpec(memory_space=pltpu.SMEM)] + [ANY] * len(operands),
        out_specs=[ANY, ANY],
        out_shape=[
            jax.ShapeDtypeStruct((rows, out_width), F32),
            jax.ShapeDtypeStruct((rows, LANES), F32),
        ],
        scratch_shapes=[
            pltpu.VMEM((rows, depth), BF16),
            pltpu.VMEM((depth, out_width), BF16),
            pltpu.VMEM((depth, LANES), BF16),
            pltpu.VMEM((rows, out_width), F32),
            pltpu.VMEM((rows, LANES), F32),
            pltpu.SemaphoreType.DMA((len(own),)),
            pltpu.SemaphoreType.DMA((len(tiles),)),
            pltpu.SemaphoreType.DMA,
            pltpu.SemaphoreType.DMA((len(tiles),)),
            pltpu.SemaphoreType.DMA,
            pltpu.SemaphoreType.DMA((len(tiles) + 1,)),
        ],
        compiler_params=PARAMS,
        cost_estimate=COST,
    )(is_end, *operands)


def make_local(n_group, n_row, n_col):
    chips = n_col // 2
    half = n_row // 2

    def place_of(group, row, col):
        return (group * n_row + row) * n_col + col

    cross_pairs = []
    for group in range(n_group):
        for row in range(n_row):
            for col in range(n_col):
                if row in (half - 1, half):
                    other = place_of(group, n_row - 1 - row, col)
                else:
                    other = place_of(group, row, col ^ 1)
                cross_pairs.append((place_of(group, row, col), other))

    def col_swap(value, flip):
        return lax.ppermute(value, "col", [(i, i ^ flip) for i in range(n_col)])

    def gather_tokens(tokens):
        shards = [tokens, col_swap(tokens, 1)]
        for step in range(1, chips):
            far = col_swap(tokens, 2 * step)
            shards += [far, col_swap(far, 1)]
        return jnp.concatenate(shards, axis=0)

    def fold(value, step):
        pairs = [(step, step + 1), (n_row - 1 - step, n_row - 2 - step)]
        return lax.ppermute(value, "row", pairs)

    def cross(value):
        return lax.ppermute(value, ("group", "row", "col"), cross_pairs)

    def spread(value, place):
        for step in reversed(range(half - 1)):
            pairs = [(step + 1, step), (n_row - 2 - step, n_row - 1 - step)]
            come = lax.ppermute(value, "row", pairs)
            if step > 0:
                value = jnp.where((place <= step) | (place >= n_row - 1 - step), come, value)
            else:
                value = come
        return value

    def local(
        tokens,
        token_job_index,
        job_adapter_index,
        first_weight,
        first_bias,
        first_down_maps,
        first_up_maps,
        second_weight,
        second_bias,
        second_down_maps,
        second_up_maps,
    ):
        rows = tokens.shape[0]
        hidden = first_weight.shape[1]
        out_width = second_weight.shape[1]
        spans = chunk_spans(hidden)
        count = len(spans)
        place = lax.axis_index("row")
        mine = lax.axis_index("col")
        edge = (place == 0) | (place == n_row - 1)
        is_end = edge.astype(jnp.int32).reshape(1)
        bias = first_bias[None, :]
        mask_all = token_mask(token_job_index, job_adapter_index)
        mask = jnp.concatenate(
            [
                lax.dynamic_slice_in_dim(mask_all, (mine ^ i) * rows, rows, 0)
                for i in range(n_col)
            ],
            axis=0,
        )
        gathered = gather_tokens(tokens)
        last = gathered
        partials, folded, sums, crossed, states, returned = {}, {}, {}, {}, {}, {}
        total, low_total, low_in = None, None, None
        ready = []

        def start_chunk(t):
            nonlocal last
            down = first_down_maps if t == 0 else None
            last = first_product(gathered, first_weight, down, spans[t], last)
            partials[t] = last
            folded[t] = fold(last, 0)

        for t in range(min(AHEAD, count)):
            start_chunk(t)
        for t in range(count + 2):
            if t < count:
                value = add_rounded(partials[t], folded[t], last)
                for step in range(1, half - 1):
                    value = add_rounded(value, fold(value, step), value)
                last = value
                sums[t] = value
                crossed[t] = cross(value)
            if t + AHEAD < count:
                start_chunk(t + AHEAD)
            if 0 <= t - 1 < count:
                k = t - 1
                width = spans[k][1]
                if k == 0:
                    low = sums[k][:, width:].astype(F32) + crossed[k][:, width:].astype(F32)
                    low_in = jnp.where(mask, low, 0.0).astype(BF16)
                last = gelu_chunk(sums[k], crossed[k], low_in, first_up_maps, bias, spans[k], last)
                states[k] = last
                returned[k] = spread(last, place)
            if 0 <= t - 2 < count:
                ready.append(t - 2)
                if len(ready) == PER_CALL or t - 2 == count - 1:
                    total, low_total = second_product(
                        is_end, [states[k] for k in ready], [returned[k] for k in ready],
                        second_weight, second_down_maps, total, low_total, spans[ready[0]][0], last,
                    )
                    last = low_total
                    ready = []
        outputs = jnp.concatenate([total, low_total], axis=1)
        blocks = [outputs[i * rows : (i + 1) * rows] for i in range(n_col)]
        ours = jnp.concatenate(blocks[0::2], axis=0)
        theirs = jnp.concatenate(blocks[1::2], axis=0).astype(BF16)
        ours = ours + col_swap(theirs, 1).astype(F32)
        result = ours[:rows]
        for step in range(1, chips):
            piece = ours[step * rows : (step + 1) * rows].astype(BF16)
            result = result + col_swap(piece, 2 * step).astype(F32)
        low_out = jnp.where(mask[:rows], result[:, out_width:], 0.0).astype(BF16)
        layer_output = result[:, :out_width] + second_bias[None, :] + dot(low_out, second_up_maps)
        return layer_output.astype(BF16)

    return local


def solution(mesh):
    shape = mesh.shape
    return jax.shard_map(
        make_local(shape["group"], shape["row"], shape["col"]),
        mesh=mesh,
        in_specs=(
            P(("group", "col"), "row"),
            P("group"),
            P("group"),
            P("row", "col"),
            P("col"),
            P("row", None),
            P(None, "col"),
            P("col", "row"),
            P("row"),
            P("col", None),
            P(None, "row"),
        ),
        out_specs=P(("group", "col"), "row"),
        check_vma=False,
    )
```

```python
import functools

import jax
import jax.numpy as jnp
import numpy as np
from jax import lax
from jax.experimental import pallas as pl
from jax.experimental.pallas import tpu as pltpu
from jax.sharding import PartitionSpec as P

ADAPTER_RANK = 16
ADAPTER_COUNT = 8
JOBS = 4
LANES = 128
AHEAD = 2
SHARES = (6, 8, 8, 8, 8, 6, 4)
PER_CALL = 2
WINDOW = 3
EARLY = 4
F32 = jnp.float32
BF16 = jnp.bfloat16
ANY = pl.BlockSpec(memory_space=pl.ANY)
COST = pl.CostEstimate(flops=1000, bytes_accessed=1000, transcendentals=0)
PARAMS = pltpu.CompilerParams(vmem_limit_bytes=18 << 20)


def gelu_tanh(values):
    return (
        0.5
        * values
        * (1.0 + jnp.tanh(0.7978845608 * (values + 0.044715 * values * values * values)))
    )


def token_mask(token_job_index, job_adapter_index):
    one_hot = token_job_index[:, None] == jnp.arange(JOBS, dtype=jnp.int32)[None, :]
    chosen = jnp.sum(jnp.where(one_hot, job_adapter_index[None, :], 0), axis=1)
    slot_ids = jnp.arange(ADAPTER_COUNT * ADAPTER_RANK, dtype=jnp.int32) // ADAPTER_RANK
    return slot_ids[None, :] == chosen[:, None]


def dot(left, right):
    return jnp.dot(left, right, preferred_element_type=F32)


def tiles_of(width, most):
    tiles, start = [], 0
    while start < width:
        size = min(most, width - start)
        tiles.append((start, size))
        start += size
    return tiles


def chunk_spans(hidden):
    units = hidden // LANES
    cuts = [round(units * part / sum(SHARES)) for part in np.cumsum((0,) + SHARES)]
    return [(lo * LANES, (hi - lo) * LANES) for lo, hi in zip(cuts, cuts[1:]) if hi > lo]


def load_kernel(w_hbm, after_ref, *refs, spans):
    outs, sem = refs[:-1], refs[-1]
    copies = [
        pltpu.make_async_copy(w_hbm.at[:, pl.ds(start, width)], out, sem.at[i])
        for i, ((start, width), out) in enumerate(zip(spans, outs))
    ]
    for copy in copies:
        copy.start()
    for copy in copies:
        copy.wait()


def load_chunks(weight, spans, after):
    return pl.pallas_call(
        functools.partial(load_kernel, spans=spans),
        in_specs=[ANY, ANY],
        out_specs=[pl.BlockSpec(memory_space=pltpu.VMEM)] * len(spans),
        out_shape=[pltpu.VMEM((weight.shape[0], width), BF16) for _, width in spans],
        scratch_shapes=[pltpu.SemaphoreType.DMA((len(spans),))],
        compiler_params=pltpu.CompilerParams(vmem_limit_bytes=1 << 20),
        cost_estimate=COST,
    )(pltpu.with_memory_space_constraint(weight, pltpu.HBM), after)


def tie(value, after):
    return lax.optimization_barrier((value, after))[0]


def first_product(x, part, down, after):
    x = tie(x, after)
    out = dot(x, part).astype(BF16)
    if down is not None:
        out = jnp.concatenate([out, dot(x, down).astype(BF16)], axis=1)
    return out


def add_rounded(a, b, after):
    return (tie(a, after).astype(F32) + b.astype(F32)).astype(BF16)


def gelu_chunk(ours, theirs, low_in, up_maps, bias, span, after):
    start, width = span
    part = slice(start, start + width)
    summed = tie(ours, after)[:, :width].astype(F32) + theirs[:, :width].astype(F32)
    before = summed + bias[:, part] + dot(low_in, up_maps[:, part])
    return gelu_tanh(before).astype(BF16)


def second_kernel(*refs, count, widths, start, tiles, first):
    end_ref = refs[0]
    own_refs = refs[1 : 1 + count]
    come_refs = refs[1 + count : 1 + 2 * count]
    w_hbm, d_hbm = refs[1 + 2 * count : 3 + 2 * count]
    acc_hbm, low_hbm = (None, None) if first else refs[3 + 2 * count : 5 + 2 * count]
    (out_hbm, low_out_hbm, state, w_v, d_v, acc_v, low_v,
     s_sem, w_sem, d_sem, a_sem, l_sem, o_sem) = refs[-13:]
    depth = sum(widths)
    w_copies = [
        pltpu.make_async_copy(
            w_hbm.at[pl.ds(start, depth), pl.ds(at, size)], w_v.at[:, pl.ds(at, size)], w_sem.at[i]
        )
        for i, (at, size) in enumerate(tiles)
    ]
    w_copies[0].start()

    def load_states(sources):
        copies, at = [], 0
        for i, source in enumerate(sources):
            copy = pltpu.make_async_copy(source, state.at[:, pl.ds(at, widths[i])], s_sem.at[i])
            copy.start()
            copies.append(copy)
            at += widths[i]
        for copy in copies:
            copy.wait()

    for copy in w_copies[1:WINDOW]:
        copy.start()
    d_copy = pltpu.make_async_copy(d_hbm.at[pl.ds(start, depth), :], d_v, d_sem)
    d_copy.start()
    if not first:
        a_copies = [
            pltpu.make_async_copy(acc_hbm.at[:, pl.ds(at, size)], acc_v.at[:, pl.ds(at, size)], a_sem.at[i])
            for i, (at, size) in enumerate(tiles)
        ]
        l_copy = pltpu.make_async_copy(low_hbm, low_v, l_sem)
        for copy in a_copies:
            copy.start()
        l_copy.start()

    @pl.when(end_ref[0] == 1)
    def _():
        load_states(come_refs)

    @pl.when(end_ref[0] == 0)
    def _():
        load_states(own_refs)

    sent = []
    for i, (at, size) in enumerate(tiles):
        part = pl.ds(at, size)
        w_copies[i].wait()
        if first:
            acc_v[:, part] = dot(state[...], w_v[:, part])
        else:
            a_copies[i].wait()
            acc_v[:, part] += dot(state[...], w_v[:, part])
        copy = pltpu.make_async_copy(acc_v.at[:, part], out_hbm.at[:, part], o_sem.at[i])
        copy.start()
        sent.append(copy)
        if i + WINDOW < len(tiles):
            w_copies[i + WINDOW].start()
    d_copy.wait()
    if first:
        low_v[...] = dot(state[...], d_v[...])
    else:
        l_copy.wait()
        low_v[...] += dot(state[...], d_v[...])
    copy = pltpu.make_async_copy(low_v, low_out_hbm, o_sem.at[len(tiles)])
    copy.start()
    sent.append(copy)
    for copy in sent:
        copy.wait()


def second_product(is_end, own, come, weight, down, total, low_total, start, after):
    rows = own[0].shape[0]
    widths = [h.shape[1] for h in own]
    depth = sum(widths)
    out_width = weight.shape[1]
    tiles = tiles_of(out_width, 256)
    first = total is None
    operands = [*own, *come, weight, down] + ([] if first else [total, low_total]) + [after]
    return pl.pallas_call(
        functools.partial(
            second_kernel, count=len(own), widths=widths, start=start, tiles=tiles, first=first
        ),
        in_specs=[pl.BlockSpec(memory_space=pltpu.SMEM)] + [ANY] * len(operands),
        out_specs=[ANY, ANY],
        out_shape=[
            jax.ShapeDtypeStruct((rows, out_width), F32),
            jax.ShapeDtypeStruct((rows, LANES), F32),
        ],
        scratch_shapes=[
            pltpu.VMEM((rows, depth), BF16),
            pltpu.VMEM((depth, out_width), BF16),
            pltpu.VMEM((depth, LANES), BF16),
            pltpu.VMEM((rows, out_width), F32),
            pltpu.VMEM((rows, LANES), F32),
            pltpu.SemaphoreType.DMA((len(own),)),
            pltpu.SemaphoreType.DMA((len(tiles),)),
            pltpu.SemaphoreType.DMA,
            pltpu.SemaphoreType.DMA((len(tiles),)),
            pltpu.SemaphoreType.DMA,
            pltpu.SemaphoreType.DMA((len(tiles) + 1,)),
        ],
        compiler_params=PARAMS,
        cost_estimate=COST,
    )(is_end, *operands)


def make_local(n_group, n_row, n_col):
    chips = n_col // 2
    half = n_row // 2

    def place_of(group, row, col):
        return (group * n_row + row) * n_col + col

    cross_pairs = []
    for group in range(n_group):
        for row in range(n_row):
            for col in range(n_col):
                if row in (half - 1, half):
                    other = place_of(group, n_row - 1 - row, col)
                else:
                    other = place_of(group, row, col ^ 1)
                cross_pairs.append((place_of(group, row, col), other))

    def col_swap(value, flip):
        return lax.ppermute(value, "col", [(i, i ^ flip) for i in range(n_col)])

    def gather_tokens(tokens, loaded):
        shards = [tokens, col_swap(tokens, 1)]
        for step in range(1, chips):
            far = tie(col_swap(tokens, 2 * step), loaded)
            shards += [far, col_swap(far, 1)]
        return jnp.concatenate(shards, axis=0)

    def fold(value, step):
        pairs = [(step, step + 1), (n_row - 1 - step, n_row - 2 - step)]
        return lax.ppermute(value, "row", pairs)

    def cross(value):
        return lax.ppermute(value, ("group", "row", "col"), cross_pairs)

    def spread(value, place):
        for step in reversed(range(half - 1)):
            pairs = [(step + 1, step), (n_row - 2 - step, n_row - 1 - step)]
            come = lax.ppermute(value, "row", pairs)
            if step > 0:
                value = jnp.where((place <= step) | (place >= n_row - 1 - step), come, value)
            else:
                value = come
        return value

    def local(
        tokens,
        token_job_index,
        job_adapter_index,
        first_weight,
        first_bias,
        first_down_maps,
        first_up_maps,
        second_weight,
        second_bias,
        second_down_maps,
        second_up_maps,
    ):
        rows = tokens.shape[0]
        hidden = first_weight.shape[1]
        out_width = second_weight.shape[1]
        spans = chunk_spans(hidden)
        count = len(spans)
        place = lax.axis_index("row")
        mine = lax.axis_index("col")
        edge = (place == 0) | (place == n_row - 1)
        is_end = edge.astype(jnp.int32).reshape(1)
        bias = first_bias[None, :]
        mask_all = token_mask(token_job_index, job_adapter_index)
        mask = jnp.concatenate(
            [
                lax.dynamic_slice_in_dim(mask_all, (mine ^ i) * rows, rows, 0)
                for i in range(n_col)
            ],
            axis=0,
        )
        loads = list(load_chunks(first_weight, spans[:EARLY], tokens))
        gathered = gather_tokens(tokens, loads[-1])
        last = gathered
        partials, folded, sums, crossed, states, returned = {}, {}, {}, {}, {}, {}
        total, low_total, low_in = None, None, None
        ready = []

        def start_chunk(t):
            nonlocal last
            down = first_down_maps if t == 0 else None
            last = first_product(gathered, loads[t], down, last)
            partials[t] = last
            folded[t] = fold(last, 0)

        for t in range(min(AHEAD, count)):
            start_chunk(t)
        if count > EARLY:
            loads += load_chunks(first_weight, spans[EARLY:], last)
            last = loads[-1]
        for t in range(count + 2):
            if t < count:
                value = add_rounded(partials[t], folded[t], last)
                for step in range(1, half - 1):
                    value = add_rounded(value, fold(value, step), value)
                last = value
                sums[t] = value
                crossed[t] = cross(value)
            if t + AHEAD < count:
                start_chunk(t + AHEAD)
            if 0 <= t - 1 < count:
                k = t - 1
                width = spans[k][1]
                if k == 0:
                    low = sums[k][:, width:].astype(F32) + crossed[k][:, width:].astype(F32)
                    low_in = jnp.where(mask, low, 0.0).astype(BF16)
                last = gelu_chunk(sums[k], crossed[k], low_in, first_up_maps, bias, spans[k], last)
                states[k] = last
                returned[k] = spread(last, place)
            if 0 <= t - 2 < count:
                ready.append(t - 2)
                if len(ready) == PER_CALL or t - 2 == count - 1:
                    total, low_total = second_product(
                        is_end, [states[k] for k in ready], [returned[k] for k in ready],
                        second_weight, second_down_maps, total, low_total, spans[ready[0]][0], last,
                    )
                    last = low_total
                    ready = []
        outputs = jnp.concatenate([total, low_total], axis=1)
        blocks = [outputs[i * rows : (i + 1) * rows] for i in range(n_col)]
        ours = jnp.concatenate(blocks[0::2], axis=0)
        theirs = jnp.concatenate(blocks[1::2], axis=0).astype(BF16)
        ours = ours + col_swap(theirs, 1).astype(F32)
        result = ours[:rows]
        for step in range(1, chips):
            piece = ours[step * rows : (step + 1) * rows].astype(BF16)
            result = result + col_swap(piece, 2 * step).astype(F32)
        low_out = jnp.where(mask[:rows], result[:, out_width:], 0.0).astype(BF16)
        layer_output = result[:, :out_width] + second_bias[None, :] + dot(low_out, second_up_maps)
        return layer_output.astype(BF16)

    return local


def solution(mesh):
    shape = mesh.shape
    return jax.shard_map(
        make_local(shape["group"], shape["row"], shape["col"]),
        mesh=mesh,
        in_specs=(
            P(("group", "col"), "row"),
            P("group"),
            P("group"),
            P("row", "col"),
            P("col"),
            P("row", None),
            P(None, "col"),
            P("col", "row"),
            P("row"),
            P("col", None),
            P(None, "row"),
        ),
        out_specs=P(("group", "col"), "row"),
        check_vma=False,
    )
```

```python
import jax
import jax.numpy as jnp
from jax import lax
from jax.sharding import PartitionSpec as P

ADAPTER_RANK = 16
ADAPTER_COUNT = 8
JOBS = 4
LANES = 128
CHUNKS = 12
LAG = 3
GROUP = 3
F32 = jnp.float32
BF16 = jnp.bfloat16


def gelu_tanh(values):
    return (
        0.5
        * values
        * (1.0 + jnp.tanh(0.7978845608 * (values + 0.044715 * values * values * values)))
    )


def token_mask(token_job_index, job_adapter_index):
    one_hot = token_job_index[:, None] == jnp.arange(JOBS, dtype=jnp.int32)[None, :]
    chosen = jnp.sum(jnp.where(one_hot, job_adapter_index[None, :], 0), axis=1)
    slot_ids = jnp.arange(ADAPTER_COUNT * ADAPTER_RANK, dtype=jnp.int32) // ADAPTER_RANK
    return slot_ids[None, :] == chosen[:, None]


def dot(left, right):
    return jnp.dot(left, right, preferred_element_type=F32)


def tie(value, after):
    return lax.optimization_barrier((value, after))[0]


def chunk_spans(hidden):
    units = hidden // LANES
    count = max(n for n in range(1, CHUNKS + 1) if units % n == 0)
    width = hidden // count
    return [(start, width) for start in range(0, hidden, width)]


def activate(summed, low_in, first_up_maps, first_bias, span):
    start, width = span
    part = slice(start, start + width)
    before = summed + first_bias[None, part] + dot(low_in, first_up_maps[:, part])
    return gelu_tanh(before).astype(BF16)


def hidden_plain(tokens, mask, first_weight, first_bias, first_down_maps, first_up_maps):
    width = first_weight.shape[1]
    joined = jnp.concatenate([dot(tokens, first_weight), dot(tokens, first_down_maps)], axis=1)
    summed = lax.psum_scatter(
        joined.astype(BF16), "row", scatter_dimension=0, tiled=True
    ).astype(F32)
    rows = summed.shape[0]
    own_mask = lax.dynamic_slice_in_dim(mask, lax.axis_index("row") * rows, rows, 0)
    low_in = jnp.where(own_mask, summed[:, width:], 0.0).astype(BF16)
    states = activate(summed[:, :width], low_in, first_up_maps, first_bias, (0, width))
    return lax.all_gather(states, "row", axis=0, tiled=True)


def make_local(n_group, n_row, n_col):
    chips = n_col // 2

    def place_of(group, row, col):
        return (group * n_row + row) * n_col + col

    cross_pairs = []
    for group in range(n_group):
        for row in range(n_row):
            for col in range(n_col):
                if n_row == 4 and row in (1, 2):
                    other = place_of(group, 3 - row, col)
                else:
                    other = place_of(group, row, col ^ 1)
                cross_pairs.append((place_of(group, row, col), other))

    def col_swap(value, flip):
        return lax.ppermute(value, "col", [(i, i ^ flip) for i in range(n_col)])

    def end_swap(value):
        return lax.ppermute(value, "row", [(i, i ^ 1) for i in range(n_row)])

    def cross(value):
        return lax.ppermute(value, ("group", "row", "col"), cross_pairs)

    def gather_tokens(tokens):
        shards = [tokens, col_swap(tokens, 1)]
        for step in range(1, chips):
            far = col_swap(tokens, 2 * step)
            shards += [far, col_swap(far, 1)]
        return jnp.concatenate(shards, axis=0)

    def pipeline(
        gathered,
        mask,
        first_weight,
        first_bias,
        first_down_maps,
        first_up_maps,
        second_weight,
        second_down_maps,
    ):
        spans = chunk_spans(first_weight.shape[1])
        count = len(spans)
        place = lax.axis_index("row")
        is_end = (place == 0) | (place == 3)
        last = gathered
        partials, payloads, swaps, sums, crosses = {}, {}, {}, {}, {}
        total, low_total, low_in = None, None, None
        ready = []

        def start_chunk(t):
            nonlocal last
            start, width = spans[t]
            x = tie(gathered, last)
            value = dot(x, first_weight[:, start : start + width]).astype(BF16)
            if t == 0:
                value = jnp.concatenate([value, dot(x, first_down_maps).astype(BF16)], axis=1)
            partials[t] = value
            last = value

        def send(t, value):
            payloads[t] = value
            swaps[t] = end_swap(value)

        for t in range(min(LAG, count)):
            start_chunk(t)
            if t < LAG - 1:
                send(t, partials[t])
        for t in range(count + LAG):
            if t < count:
                ours = tie(partials[t], last).astype(F32)
                sums[t] = (ours + swaps[t].astype(F32)).astype(BF16)
                last = sums[t]
                crosses[t] = cross(sums[t])
            if t == 0:
                send(LAG - 1, partials[LAG - 1])
            if 0 <= t - 1 < count:
                k = t - 1
                width = spans[k][1]
                summed = tie(sums[k], last).astype(F32) + crosses[k].astype(F32)
                if k == 0:
                    low_in = jnp.where(mask, summed[:, width:], 0.0).astype(BF16)
                    summed = summed[:, :width]
                value = activate(summed, low_in, first_up_maps, first_bias, spans[k])
                if k + LAG < count:
                    value = jnp.where(is_end, partials[k + LAG], value)
                last = value
                send(k + LAG, value)
            if t + LAG < count:
                start_chunk(t + LAG)
            if t >= LAG:
                ready.append(t - LAG)
                if len(ready) == GROUP or t - LAG >= count - 1:
                    own = [payloads[k + LAG] for k in ready]
                    come = [swaps[k + LAG] for k in ready]
                    states = jnp.where(
                        is_end, jnp.concatenate(come, axis=1), jnp.concatenate(own, axis=1)
                    )
                    states = tie(states, last)
                    part = slice(spans[ready[0]][0], spans[ready[-1]][0] + spans[ready[-1]][1])
                    value = dot(states, second_weight[part])
                    low = dot(states, second_down_maps[part])
                    total = value if total is None else total + value
                    low_total = low if low_total is None else low_total + low
                    last = low_total
                    ready = []
        return total, low_total

    def local(
        tokens,
        token_job_index,
        job_adapter_index,
        first_weight,
        first_bias,
        first_down_maps,
        first_up_maps,
        second_weight,
        second_bias,
        second_down_maps,
        second_up_maps,
    ):
        rows = tokens.shape[0]
        out_width = second_weight.shape[1]
        mine = lax.axis_index("col")
        mask_all = token_mask(token_job_index, job_adapter_index)
        mask = jnp.concatenate(
            [
                lax.dynamic_slice_in_dim(mask_all, (mine ^ i) * rows, rows, 0)
                for i in range(n_col)
            ],
            axis=0,
        )
        gathered = gather_tokens(tokens)
        first = (first_weight, first_bias, first_down_maps, first_up_maps)
        if n_row == 4:
            total, low_total = pipeline(gathered, mask, *first, second_weight, second_down_maps)
        else:
            states = hidden_plain(gathered, mask, *first)
            total, low_total = dot(states, second_weight), dot(states, second_down_maps)
        outputs = jnp.concatenate([total, low_total], axis=1)
        blocks = [outputs[i * rows : (i + 1) * rows] for i in range(n_col)]
        ours = jnp.concatenate(blocks[0::2], axis=0)
        theirs = jnp.concatenate(blocks[1::2], axis=0).astype(BF16)
        ours = ours + col_swap(theirs, 1).astype(F32)
        result = ours[:rows]
        for step in range(1, chips):
            piece = ours[step * rows : (step + 1) * rows].astype(BF16)
            result = result + col_swap(piece, 2 * step).astype(F32)
        low_out = jnp.where(mask[:rows], result[:, out_width:], 0.0).astype(BF16)
        layer_output = result[:, :out_width] + second_bias[None, :] + dot(low_out, second_up_maps)
        return layer_output.astype(BF16)

    return local


def solution(mesh):
    shape = mesh.shape
    return jax.shard_map(
        make_local(shape["group"], shape["row"], shape["col"]),
        mesh=mesh,
        in_specs=(
            P(("group", "col"), "row"),
            P("group"),
            P("group"),
            P("row", "col"),
            P("col"),
            P("row", None),
            P(None, "col"),
            P("col", "row"),
            P("row"),
            P("col", None),
            P(None, "row"),
        ),
        out_specs=P(("group", "col"), "row"),
        check_vma=False,
    )
```

```python
import jax
import jax.numpy as jnp
from jax import lax
from jax.sharding import PartitionSpec as P

ADAPTER_RANK = 16
ADAPTER_COUNT = 8
JOBS = 4
LANES = 128
UNITS = 12
LAG = 3
F32 = jnp.float32
BF16 = jnp.bfloat16


def gelu_tanh(values):
    return (
        0.5
        * values
        * (1.0 + jnp.tanh(0.7978845608 * (values + 0.044715 * values * values * values)))
    )


def token_mask(token_job_index, job_adapter_index):
    one_hot = token_job_index[:, None] == jnp.arange(JOBS, dtype=jnp.int32)[None, :]
    chosen = jnp.sum(jnp.where(one_hot, job_adapter_index[None, :], 0), axis=1)
    slot_ids = jnp.arange(ADAPTER_COUNT * ADAPTER_RANK, dtype=jnp.int32) // ADAPTER_RANK
    return slot_ids[None, :] == chosen[:, None]


def dot(left, right):
    return jnp.dot(left, right, preferred_element_type=F32)


def tie(value, after):
    return lax.optimization_barrier((value, after))[0]


def activate(summed, low_in, first_up_maps, first_bias, part):
    before = summed + first_bias[None, part] + dot(low_in, first_up_maps[:, part])
    return gelu_tanh(before).astype(BF16)


def hidden_plain(tokens, mask, first_weight, first_bias, first_down_maps, first_up_maps):
    width = first_weight.shape[1]
    joined = jnp.concatenate([dot(tokens, first_weight), dot(tokens, first_down_maps)], axis=1)
    summed = lax.psum_scatter(
        joined.astype(BF16), "row", scatter_dimension=0, tiled=True
    ).astype(F32)
    rows = summed.shape[0]
    own_mask = lax.dynamic_slice_in_dim(mask, lax.axis_index("row") * rows, rows, 0)
    low_in = jnp.where(own_mask, summed[:, width:], 0.0).astype(BF16)
    states = activate(summed[:, :width], low_in, first_up_maps, first_bias, slice(0, width))
    return lax.all_gather(states, "row", axis=0, tiled=True)


def make_local(n_group, n_row, n_col):
    chips = n_col // 2

    def place_of(group, row, col):
        return (group * n_row + row) * n_col + col

    cross_pairs = []
    for group in range(n_group):
        for row in range(n_row):
            for col in range(n_col):
                if n_row == 4 and row in (1, 2):
                    other = place_of(group, 3 - row, col)
                else:
                    other = place_of(group, row, col ^ 1)
                cross_pairs.append((place_of(group, row, col), other))

    def col_swap(value, flip):
        return lax.ppermute(value, "col", [(i, i ^ flip) for i in range(n_col)])

    def end_swap(value):
        return lax.ppermute(value, "row", [(i, i ^ 1) for i in range(n_row)])

    def cross(value):
        return lax.ppermute(value, ("group", "row", "col"), cross_pairs)

    def gather_tokens(tokens):
        shards = [tokens, col_swap(tokens, 1)]
        for step in range(1, chips):
            far = col_swap(tokens, 2 * step)
            shards += [far, col_swap(far, 1)]
        return jnp.concatenate(shards, axis=0)

    def pipeline(
        tokens,
        mask,
        first_weight,
        first_bias,
        first_down_maps,
        first_up_maps,
        second_weight,
        second_down_maps,
    ):
        rows = tokens.shape[0]
        near = 2 * rows
        width = first_weight.shape[1] // UNITS
        wide = 2 * width
        fold = width // LANES
        place = lax.axis_index("row")
        is_end = (place == 0) | (place == 3)
        last = tokens
        partials, payloads, swaps, sums, crosses = {}, {}, {}, {}, {}
        total, low_total = None, None
        low_in = {}

        def halves(value):
            return jnp.concatenate([value[:, :width], value[:, width:]], axis=0)

        def unfold(value):
            return jnp.concatenate([value[:near], value[near : 2 * near]], axis=1)

        def columns(unit):
            if unit < 4:
                start, size = (unit % 2) * wide, wide
            elif unit < 8:
                start, size = unit * width, width
            else:
                start, size = 8 * width + (unit % 2) * wide, wide
            return slice(start, start + size)

        def own_chip(unit):
            return unit in (0, 1, 10, 11)

        def multiply(left, right):
            nonlocal last
            value = dot(tie(left, last), right).astype(BF16)
            last = value
            return value

        def first_half(unit, x):
            nonlocal last
            value = halves(multiply(x, first_weight[:, columns(unit)]))
            if unit in (0, 2):
                low = dot(x, first_down_maps).astype(BF16)
                low = jnp.concatenate(jnp.split(low, fold, axis=0), axis=1)
                value = jnp.concatenate([value, low], axis=0)
            partials[unit] = value
            last = value

        def first_pair(unit, x):
            value = multiply(x, first_weight[:, unit * width : (unit + 2) * width])
            partials[unit], partials[unit + 1] = value[:, :width], value[:, width:]

        def first_late(unit, x):
            value = multiply(x, first_weight[:, columns(unit)])
            partials[unit + 2], partials[unit] = halves(value[:near]), halves(value[near:])

        def send(t, value):
            payloads[t] = value
            swaps[t] = end_swap(value)

        def state(unit):
            return jnp.where(is_end, swaps[unit + LAG], payloads[unit + LAG])

        def second(states, part):
            nonlocal last
            states = tie(states, last)
            value = dot(states, second_weight[part])
            low = dot(states, second_down_maps[part])
            last = low
            return jnp.concatenate([value, low], axis=1)

        gathered_near = jnp.concatenate([tokens, col_swap(tokens, 1)], axis=0)
        far = col_swap(tokens, 2)
        first_half(0, gathered_near)
        send(0, partials[0])
        first_half(1, gathered_near)
        send(1, partials[1])
        gathered_far = None
        outputs = {}
        for t in range(UNITS + LAG):
            if t < UNITS:
                ours = tie(partials[t], last).astype(F32)
                sums[t] = (ours + swaps[t].astype(F32)).astype(BF16)
                last = sums[t]
                crosses[t] = cross(sums[t])
            if t == 0:
                gathered_far = jnp.concatenate([far, col_swap(far, 1)], axis=0)
                first_half(2, gathered_far)
                send(2, partials[2])
                first_half(3, gathered_far)
                gathered = jnp.concatenate([gathered_near, gathered_far], axis=0)
            k = t - 1
            if 0 <= k < UNITS:
                summed = tie(sums[k], last).astype(F32) + crosses[k].astype(F32)
                if k in (0, 2):
                    low = jnp.concatenate(jnp.split(summed[2 * near :], fold, axis=1), axis=0)
                    own_mask = mask[:near] if k == 0 else mask[near:]
                    low_in[k] = jnp.where(own_mask, low, 0.0).astype(BF16)
                if 4 <= k < 8:
                    low = jnp.concatenate([low_in[0], low_in[2]], axis=0)
                    value = activate(summed, low, first_up_maps, first_bias, columns(k))
                else:
                    low = low_in[0] if own_chip(k) else low_in[2]
                    value = activate(unfold(summed), low, first_up_maps, first_bias, columns(k))
                    value = halves(value)
                if k + LAG < UNITS:
                    value = jnp.where(is_end, partials[k + LAG], value)
                last = value
                send(k + LAG, value)
            if t in (1, 2):
                first_pair(2 * t + 2, gathered)
            elif t in (4, 5):
                first_late(t + 4, gathered)
            elif t == 6:
                top = jnp.concatenate([unfold(state(0)), unfold(state(1))], axis=1)
                bottom = jnp.concatenate([unfold(state(2)), unfold(state(3))], axis=1)
                total = second(jnp.concatenate([top, bottom], axis=0), slice(0, 4 * width))
            elif t == 10:
                states = jnp.concatenate([state(u) for u in range(4, 8)], axis=1)
                total = total + second(states, slice(4 * width, 8 * width))
                outputs["near"], outputs["far"] = total[:near], total[near:]
            elif t >= 11:
                unit = t - LAG
                name = "near" if own_chip(unit) else "far"
                outputs[name] = outputs[name] + second(unfold(state(unit)), columns(unit))
                if t == 12:
                    done = outputs["far"]
                    across = done[:rows] + col_swap(done[rows:].astype(BF16), 1).astype(F32)
                    across = across.astype(BF16)
                    last = across
                    across = col_swap(across, 2)
        done = outputs["near"]
        return done[:rows] + col_swap(done[rows:].astype(BF16), 1).astype(F32) + across.astype(F32)

    def plain(tokens, mask, second_weight, second_down_maps, *first):
        rows = tokens.shape[0]
        states = hidden_plain(gather_tokens(tokens), mask, *first)
        outputs = jnp.concatenate([dot(states, second_weight), dot(states, second_down_maps)], axis=1)
        blocks = [outputs[i * rows : (i + 1) * rows] for i in range(n_col)]
        ours = jnp.concatenate(blocks[0::2], axis=0)
        theirs = jnp.concatenate(blocks[1::2], axis=0).astype(BF16)
        ours = ours + col_swap(theirs, 1).astype(F32)
        result = ours[:rows]
        for step in range(1, chips):
            piece = ours[step * rows : (step + 1) * rows].astype(BF16)
            result = result + col_swap(piece, 2 * step).astype(F32)
        return result

    def local(
        tokens,
        token_job_index,
        job_adapter_index,
        first_weight,
        first_bias,
        first_down_maps,
        first_up_maps,
        second_weight,
        second_bias,
        second_down_maps,
        second_up_maps,
    ):
        rows = tokens.shape[0]
        out_width = second_weight.shape[1]
        mine = lax.axis_index("col")
        mask_all = token_mask(token_job_index, job_adapter_index)
        mask = jnp.concatenate(
            [
                lax.dynamic_slice_in_dim(mask_all, (mine ^ i) * rows, rows, 0)
                for i in range(n_col)
            ],
            axis=0,
        )
        first = (first_weight, first_bias, first_down_maps, first_up_maps)
        even = first_weight.shape[1] % (UNITS * LANES) == 0
        if n_row == 4 and n_col == 4 and even:
            result = pipeline(tokens, mask, *first, second_weight, second_down_maps)
        else:
            result = plain(tokens, mask, second_weight, second_down_maps, *first)
        low_out = jnp.where(mask[:rows], result[:, out_width:], 0.0).astype(BF16)
        layer_output = result[:, :out_width] + second_bias[None, :] + dot(low_out, second_up_maps)
        return layer_output.astype(BF16)

    return local


def solution(mesh):
    shape = mesh.shape
    return jax.shard_map(
        make_local(shape["group"], shape["row"], shape["col"]),
        mesh=mesh,
        in_specs=(
            P(("group", "col"), "row"),
            P("group"),
            P("group"),
            P("row", "col"),
            P("col"),
            P("row", None),
            P(None, "col"),
            P("col", "row"),
            P("row"),
            P("col", None),
            P(None, "row"),
        ),
        out_specs=P(("group", "col"), "row"),
        check_vma=False,
    )
```

```python
import functools

import jax
import jax.numpy as jnp
from jax import lax
from jax.experimental import pallas as pl
from jax.experimental.pallas import tpu as pltpu
from jax.sharding import PartitionSpec as P

ADAPTER_RANK = 16
ADAPTER_COUNT = 8
JOBS = 4
LANES = 128
UNITS = 12
LAG = 3
F32 = jnp.float32
BF16 = jnp.bfloat16


def gelu_tanh(values):
    return (
        0.5
        * values
        * (1.0 + jnp.tanh(0.7978845608 * (values + 0.044715 * values * values * values)))
    )


def token_mask(token_job_index, job_adapter_index):
    one_hot = token_job_index[:, None] == jnp.arange(JOBS, dtype=jnp.int32)[None, :]
    chosen = jnp.sum(jnp.where(one_hot, job_adapter_index[None, :], 0), axis=1)
    slot_ids = jnp.arange(ADAPTER_COUNT * ADAPTER_RANK, dtype=jnp.int32) // ADAPTER_RANK
    return slot_ids[None, :] == chosen[:, None]


def dot(left, right):
    return jnp.dot(left, right, preferred_element_type=F32)


def tie(value, after):
    return lax.optimization_barrier((value, after))[0]


def load_kernel(w_hbm, after_ref, out, sem, *, start):
    copy = pltpu.make_async_copy(w_hbm.at[:, pl.ds(start, out.shape[1])], out, sem)
    copy.start()
    copy.wait()


def load_columns(weight, start, width, after):
    return pl.pallas_call(
        functools.partial(load_kernel, start=start),
        in_specs=[pl.BlockSpec(memory_space=pl.ANY)] * 2,
        out_specs=pl.BlockSpec(memory_space=pltpu.VMEM),
        out_shape=pltpu.VMEM((weight.shape[0], width), BF16),
        scratch_shapes=[pltpu.SemaphoreType.DMA],
        compiler_params=pltpu.CompilerParams(vmem_limit_bytes=1 << 20),
        cost_estimate=pl.CostEstimate(flops=0, bytes_accessed=1000, transcendentals=0),
    )(pltpu.with_memory_space_constraint(weight, pltpu.HBM), after)


def activate(summed, low_in, first_up_maps, first_bias, part):
    before = summed + first_bias[None, part] + dot(low_in, first_up_maps[:, part])
    return gelu_tanh(before).astype(BF16)


def hidden_plain(tokens, mask, first_weight, first_bias, first_down_maps, first_up_maps):
    width = first_weight.shape[1]
    joined = jnp.concatenate([dot(tokens, first_weight), dot(tokens, first_down_maps)], axis=1)
    summed = lax.psum_scatter(
        joined.astype(BF16), "row", scatter_dimension=0, tiled=True
    ).astype(F32)
    rows = summed.shape[0]
    own_mask = lax.dynamic_slice_in_dim(mask, lax.axis_index("row") * rows, rows, 0)
    low_in = jnp.where(own_mask, summed[:, width:], 0.0).astype(BF16)
    states = activate(summed[:, :width], low_in, first_up_maps, first_bias, slice(0, width))
    return lax.all_gather(states, "row", axis=0, tiled=True)


def make_local(n_group, n_row, n_col):
    chips = n_col // 2

    def place_of(group, row, col):
        return (group * n_row + row) * n_col + col

    cross_pairs = []
    for group in range(n_group):
        for row in range(n_row):
            for col in range(n_col):
                if n_row == 4 and row in (1, 2):
                    other = place_of(group, 3 - row, col)
                else:
                    other = place_of(group, row, col ^ 1)
                cross_pairs.append((place_of(group, row, col), other))

    def col_swap(value, flip):
        return lax.ppermute(value, "col", [(i, i ^ flip) for i in range(n_col)])

    def end_swap(value):
        return lax.ppermute(value, "row", [(i, i ^ 1) for i in range(n_row)])

    def cross(value):
        return lax.ppermute(value, ("group", "row", "col"), cross_pairs)

    def gather_tokens(tokens):
        shards = [tokens, col_swap(tokens, 1)]
        for step in range(1, chips):
            far = col_swap(tokens, 2 * step)
            shards += [far, col_swap(far, 1)]
        return jnp.concatenate(shards, axis=0)

    def pipeline(
        tokens,
        mask_of,
        first_weight,
        first_bias,
        first_down_maps,
        first_up_maps,
        second_weight,
        second_down_maps,
    ):
        rows = tokens.shape[0]
        near = 2 * rows
        width = first_weight.shape[1] // UNITS
        wide = 2 * width
        fold = width // LANES
        place = lax.axis_index("row")
        is_end = (place == 0) | (place == 3)
        last = tokens
        partials, payloads, swaps, sums, crosses = {}, {}, {}, {}, {}
        total, low_total = None, None
        low_in = {}

        def halves(value):
            return jnp.concatenate([value[:, :width], value[:, width:]], axis=0)

        def unfold(value):
            return jnp.concatenate([value[:near], value[near : 2 * near]], axis=1)

        def columns(unit):
            if unit < 4:
                start, size = (unit % 2) * wide, wide
            elif unit < 8:
                start, size = unit * width, width
            else:
                start, size = 8 * width + (unit % 2) * wide, wide
            return slice(start, start + size)

        def own_chip(unit):
            return unit in (0, 1, 10, 11)

        def load(block):
            nonlocal last
            loads[block] = load_columns(first_weight, block * 4 * width, 4 * width, last)
            last = loads[block]

        def multiply(left, part):
            nonlocal last
            block, start = divmod(part.start, 4 * width)
            right = loads[block][:, start : start + part.stop - part.start]
            value = dot(tie(left, last), right).astype(BF16)
            last = value
            return value

        def first_half(unit, x):
            nonlocal last
            value = halves(multiply(x, columns(unit)))
            if unit in (0, 2):
                low = dot(x, first_down_maps).astype(BF16)
                low = jnp.concatenate(jnp.split(low, fold, axis=0), axis=1)
                value = jnp.concatenate([value, low], axis=0)
            partials[unit] = value
            last = value

        def first_pair(unit, x):
            value = multiply(x, slice(unit * width, (unit + 2) * width))
            partials[unit], partials[unit + 1] = value[:, :width], value[:, width:]

        def first_late(unit, x):
            value = multiply(x, columns(unit))
            partials[unit + 2], partials[unit] = halves(value[:near]), halves(value[near:])

        def send(t, value):
            payloads[t] = value
            swaps[t] = end_swap(value)

        def state(unit):
            return jnp.where(is_end, swaps[unit + LAG], payloads[unit + LAG])

        def second(states, part):
            nonlocal last
            states = tie(states, last)
            low = dot(states, second_down_maps[part])
            value = dot(states, second_weight[part])
            last = value[:8, :LANES]
            return jnp.concatenate([value, low], axis=1)

        far = col_swap(tokens, 2)
        loads = {}
        load(0)
        gathered_near = jnp.concatenate([tokens, tie(col_swap(tokens, 1), last)], axis=0)
        first_half(0, gathered_near)
        send(0, partials[0])
        first_half(1, gathered_near)
        send(1, partials[1])
        mask = mask_of(last)
        first_bias = tie(first_bias, last)
        load(1)
        gathered_far = None
        outputs = {}
        for t in range(UNITS + LAG):
            if t < UNITS:
                ours = tie(partials[t], last).astype(F32)
                sums[t] = (ours + swaps[t].astype(F32)).astype(BF16)
                last = sums[t]
                crosses[t] = cross(sums[t])
            if t == 0:
                gathered_far = jnp.concatenate([far, col_swap(far, 1)], axis=0)
                first_half(2, gathered_far)
                send(2, partials[2])
                first_half(3, gathered_far)
                gathered = jnp.concatenate([gathered_near, gathered_far], axis=0)
            k = t - 1
            if 0 <= k < UNITS:
                summed = tie(sums[k], last).astype(F32) + crosses[k].astype(F32)
                if k in (0, 2):
                    low = jnp.concatenate(jnp.split(summed[2 * near :], fold, axis=1), axis=0)
                    own_mask = mask[:near] if k == 0 else mask[near:]
                    low_in[k] = jnp.where(own_mask, low, 0.0).astype(BF16)
                if 4 <= k < 8:
                    low = jnp.concatenate([low_in[0], low_in[2]], axis=0)
                    value = activate(summed, low, first_up_maps, first_bias, columns(k))
                else:
                    low = low_in[0] if own_chip(k) else low_in[2]
                    value = activate(unfold(summed), low, first_up_maps, first_bias, columns(k))
                    value = halves(value)
                if k + LAG < UNITS:
                    value = jnp.where(is_end, partials[k + LAG], value)
                last = value
                send(k + LAG, value)
            if t == 0:
                load(2)
            if t in (1, 2):
                first_pair(2 * t + 2, gathered)
            elif t in (4, 5):
                first_late(t + 4, gathered)
            elif t == 9:
                top = jnp.concatenate([unfold(state(0)), unfold(state(1))], axis=1)
                bottom = jnp.concatenate([unfold(state(2)), unfold(state(3))], axis=1)
                total = second(jnp.concatenate([top, bottom], axis=0), slice(0, 4 * width))
            elif t == 10:
                states = jnp.concatenate([state(u) for u in range(4, 8)], axis=1)
                total = total + second(states, slice(4 * width, 8 * width))
                outputs["near"], outputs["far"] = total[:near], total[near:]
            elif t >= 11:
                unit = t - LAG
                name = "near" if own_chip(unit) else "far"
                outputs[name] = outputs[name] + second(unfold(state(unit)), columns(unit))
                if t == 12:
                    done = outputs["far"]
                    across = done[:rows] + col_swap(done[rows:].astype(BF16), 1).astype(F32)
                    across = across.astype(BF16)
                    last = across
                    across = col_swap(across, 2)
        done = outputs["near"]
        done = done[:rows] + col_swap(done[rows:].astype(BF16), 1).astype(F32)
        return done + across.astype(F32), mask

    def plain(tokens, mask, second_weight, second_down_maps, *first):
        rows = tokens.shape[0]
        states = hidden_plain(gather_tokens(tokens), mask, *first)
        outputs = jnp.concatenate([dot(states, second_weight), dot(states, second_down_maps)], axis=1)
        blocks = [outputs[i * rows : (i + 1) * rows] for i in range(n_col)]
        ours = jnp.concatenate(blocks[0::2], axis=0)
        theirs = jnp.concatenate(blocks[1::2], axis=0).astype(BF16)
        ours = ours + col_swap(theirs, 1).astype(F32)
        result = ours[:rows]
        for step in range(1, chips):
            piece = ours[step * rows : (step + 1) * rows].astype(BF16)
            result = result + col_swap(piece, 2 * step).astype(F32)
        return result

    def local(
        tokens,
        token_job_index,
        job_adapter_index,
        first_weight,
        first_bias,
        first_down_maps,
        first_up_maps,
        second_weight,
        second_bias,
        second_down_maps,
        second_up_maps,
    ):
        rows = tokens.shape[0]
        out_width = second_weight.shape[1]
        mine = lax.axis_index("col")

        def mask_of(after):
            mask_all = token_mask(tie(token_job_index, after), job_adapter_index)
            return jnp.concatenate(
                [
                    lax.dynamic_slice_in_dim(mask_all, (mine ^ i) * rows, rows, 0)
                    for i in range(n_col)
                ],
                axis=0,
            )

        first = (first_weight, first_bias, first_down_maps, first_up_maps)
        even = first_weight.shape[1] % (UNITS * LANES) == 0
        if n_row == 4 and n_col == 4 and even:
            result, mask = pipeline(tokens, mask_of, *first, second_weight, second_down_maps)
        else:
            mask = mask_of(tokens)
            result = plain(tokens, mask, second_weight, second_down_maps, *first)
        low_out = jnp.where(mask[:rows], result[:, out_width:], 0.0).astype(BF16)
        layer_output = result[:, :out_width] + second_bias[None, :] + dot(low_out, second_up_maps)
        return layer_output.astype(BF16)

    return local


def solution(mesh):
    shape = mesh.shape
    return jax.shard_map(
        make_local(shape["group"], shape["row"], shape["col"]),
        mesh=mesh,
        in_specs=(
            P(("group", "col"), "row"),
            P("group"),
            P("group"),
            P("row", "col"),
            P("col"),
            P("row", None),
            P(None, "col"),
            P("col", "row"),
            P("row"),
            P("col", None),
            P(None, "row"),
        ),
        out_specs=P(("group", "col"), "row"),
        check_vma=False,
    )
```

```python
import functools

import jax
import jax.numpy as jnp
from jax import lax
from jax.experimental import pallas as pl
from jax.experimental.pallas import tpu as pltpu
from jax.sharding import PartitionSpec as P

ADAPTER_RANK = 16
ADAPTER_COUNT = 8
JOBS = 4
LANES = 128
UNITS = 12
LAG = 3
F32 = jnp.float32
BF16 = jnp.bfloat16


def gelu_tanh(values):
    return (
        0.5
        * values
        * (1.0 + jnp.tanh(0.7978845608 * (values + 0.044715 * values * values * values)))
    )


def token_mask(token_job_index, job_adapter_index):
    one_hot = token_job_index[:, None] == jnp.arange(JOBS, dtype=jnp.int32)[None, :]
    chosen = jnp.sum(jnp.where(one_hot, job_adapter_index[None, :], 0), axis=1)
    slot_ids = jnp.arange(ADAPTER_COUNT * ADAPTER_RANK, dtype=jnp.int32) // ADAPTER_RANK
    return slot_ids[None, :] == chosen[:, None]


def dot(left, right):
    return jnp.dot(left, right, preferred_element_type=F32)


def tie(value, after):
    return lax.optimization_barrier((value, after))[0]


def load_kernel(w_hbm, after_ref, out, sem, *, part):
    copy = pltpu.make_async_copy(w_hbm.at[part], out, sem)
    copy.start()
    copy.wait()


def load_part(weight, part, after):
    shape = tuple(p.size for p in part)
    return pl.pallas_call(
        functools.partial(load_kernel, part=part),
        in_specs=[pl.BlockSpec(memory_space=pl.ANY)] * 2,
        out_specs=pl.BlockSpec(memory_space=pltpu.VMEM),
        out_shape=pltpu.VMEM(shape, BF16),
        scratch_shapes=[pltpu.SemaphoreType.DMA],
        compiler_params=pltpu.CompilerParams(vmem_limit_bytes=1 << 20),
        cost_estimate=pl.CostEstimate(flops=0, bytes_accessed=1000, transcendentals=0),
    )(pltpu.with_memory_space_constraint(weight, pltpu.HBM), after)


def activate(summed, low_in, first_up_maps, first_bias, part):
    before = summed + first_bias[None, part] + dot(low_in, first_up_maps[:, part])
    return gelu_tanh(before).astype(BF16)


def hidden_plain(tokens, mask, first_weight, first_bias, first_down_maps, first_up_maps):
    width = first_weight.shape[1]
    joined = jnp.concatenate([dot(tokens, first_weight), dot(tokens, first_down_maps)], axis=1)
    summed = lax.psum_scatter(
        joined.astype(BF16), "row", scatter_dimension=0, tiled=True
    ).astype(F32)
    rows = summed.shape[0]
    own_mask = lax.dynamic_slice_in_dim(mask, lax.axis_index("row") * rows, rows, 0)
    low_in = jnp.where(own_mask, summed[:, width:], 0.0).astype(BF16)
    states = activate(summed[:, :width], low_in, first_up_maps, first_bias, slice(0, width))
    return lax.all_gather(states, "row", axis=0, tiled=True)


def make_local(n_group, n_row, n_col):
    chips = n_col // 2

    def place_of(group, row, col):
        return (group * n_row + row) * n_col + col

    cross_pairs = []
    for group in range(n_group):
        for row in range(n_row):
            for col in range(n_col):
                if n_row == 4 and row in (1, 2):
                    other = place_of(group, 3 - row, col)
                else:
                    other = place_of(group, row, col ^ 1)
                cross_pairs.append((place_of(group, row, col), other))

    def col_swap(value, flip):
        return lax.ppermute(value, "col", [(i, i ^ flip) for i in range(n_col)])

    def end_swap(value):
        return lax.ppermute(value, "row", [(i, i ^ 1) for i in range(n_row)])

    def cross(value):
        return lax.ppermute(value, ("group", "row", "col"), cross_pairs)

    def gather_tokens(tokens):
        shards = [tokens, col_swap(tokens, 1)]
        for step in range(1, chips):
            far = col_swap(tokens, 2 * step)
            shards += [far, col_swap(far, 1)]
        return jnp.concatenate(shards, axis=0)

    def pipeline(
        tokens,
        mine,
        mask_of,
        first_weight,
        first_bias,
        first_down_maps,
        first_up_maps,
        second_weight,
        second_down_maps,
    ):
        rows = tokens.shape[0]
        near = 2 * rows
        width = first_weight.shape[1] // UNITS
        wide = 2 * width
        fold = width // LANES
        place = lax.axis_index("row")
        is_end = (place == 0) | (place == 3)
        last = tokens
        partials, payloads, swaps, sums, crosses = {}, {}, {}, {}, {}
        total, low_total = None, None
        low_in = {}

        def halves(value):
            return jnp.concatenate([value[:, :width], value[:, width:]], axis=0)

        def unfold(value):
            return jnp.concatenate([value[:near], value[near : 2 * near]], axis=1)

        def columns(unit):
            if unit < 4:
                start, size = (unit % 2) * wide, wide
            elif unit < 8:
                start, size = unit * width, width
            else:
                start, size = 8 * width + (unit % 2) * wide, wide
            return slice(start, start + size)

        def own_chip(unit):
            return unit in (0, 1, 10, 11)

        def load(block):
            nonlocal last
            part = (pl.ds(0, first_weight.shape[0]), pl.ds(block * wide, wide))
            loads[block] = load_part(first_weight, part, last[:16, :LANES])
            last = loads[block]

        def load_second(block):
            nonlocal last
            part = (pl.ds(block * wide, wide), pl.ds(0, second_weight.shape[1]))
            second_loads[block] = load_part(second_weight, part, last[:16, :LANES])
            last = second_loads[block]

        def multiply(x, block):
            nonlocal last
            value = dot(tie(x, last), loads[block]).astype(BF16)
            last = value
            return value

        def first_half(unit, x):
            nonlocal last
            value = halves(multiply(x, unit % 2))
            if unit in (0, 2):
                low = dot(x, first_down_maps).astype(BF16)
                low = jnp.concatenate(jnp.split(low, fold, axis=0), axis=1)
                value = jnp.concatenate([value, low], axis=0)
            partials[unit] = value
            last = value

        def first_pair(unit, x):
            value = multiply(x, unit // 2)
            partials[unit], partials[unit + 1] = value[:, :width], value[:, width:]

        def first_late(unit, x):
            value = multiply(x, unit - 4)
            partials[unit + 2], partials[unit] = halves(value[:near]), halves(value[near:])

        def send(t, value):
            payloads[t] = value
            swaps[t] = end_swap(value)

        def state(unit):
            return jnp.where(is_end, swaps[unit + LAG], payloads[unit + LAG])

        def second(name, states, block):
            nonlocal last
            states = tie(states, last)
            part = slice(block * wide, (block + 1) * wide)
            low = dot(states, second_down_maps[part])
            value = dot(states, second_loads[block] if block in second_loads else second_weight[part])
            last = value[:8, :LANES]
            if name in outputs:
                value, low = outputs[name][0] + value, outputs[name][1] + low
            outputs[name] = (value, low)

        def core_sum(name):
            joined = jnp.concatenate(outputs[name], axis=1)
            return joined[:rows] + col_swap(joined[rows:].astype(BF16), 1).astype(F32)

        far = col_swap(tokens, 2)
        loads, second_loads, outputs = {}, {}, {}
        last, is_end, mine = lax.optimization_barrier((tokens[:16, :LANES], is_end, mine))
        load(0)
        gathered_near = jnp.concatenate([tokens, tie(col_swap(tokens, 1), last)], axis=0)
        first_half(0, gathered_near)
        send(0, partials[0])
        load(1)
        first_half(1, gathered_near)
        send(1, partials[1])
        mask = mask_of(mine, last)
        first_bias = tie(first_bias, last)
        load(2)
        for t in range(UNITS + LAG):
            if t < UNITS:
                ours = tie(partials[t], last).astype(F32)
                sums[t] = (ours + swaps[t].astype(F32)).astype(BF16)
                last = sums[t]
                crosses[t] = cross(sums[t])
            if t == 0:
                gathered_far = jnp.concatenate([far, col_swap(far, 1)], axis=0)
                first_half(2, gathered_far)
                send(2, partials[2])
                first_half(3, gathered_far)
                gathered = jnp.concatenate([gathered_near, gathered_far], axis=0)
            k = t - 1
            if 0 <= k < UNITS:
                summed = tie(sums[k], last).astype(F32) + crosses[k].astype(F32)
                if k in (0, 2):
                    low = jnp.concatenate(jnp.split(summed[2 * near :], fold, axis=1), axis=0)
                    own_mask = mask[:near] if k == 0 else mask[near:]
                    low_in[k] = jnp.where(own_mask, low, 0.0).astype(BF16)
                if 4 <= k < 8:
                    low = jnp.concatenate([low_in[0], low_in[2]], axis=0)
                    value = activate(summed, low, first_up_maps, first_bias, columns(k))
                else:
                    low = low_in[0] if own_chip(k) else low_in[2]
                    value = activate(unfold(summed), low, first_up_maps, first_bias, columns(k))
                    value = halves(value)
                if k + LAG < UNITS:
                    value = jnp.where(is_end, partials[k + LAG], value)
                last = value
                send(k + LAG, value)
            if t < 3:
                load(t + 3)
            if t in (1, 2):
                first_pair(2 * t + 2, gathered)
            elif t == 3:
                first_late(8, gathered)
                first_late(9, gathered)
            elif t in (5, 6):
                top, bottom = unfold(state(t - 5)), unfold(state(t - 3))
                second("all", jnp.concatenate([top, bottom], axis=0), t - 5)
            elif t in (7, 9):
                load_second((t + 1) // 2)
            elif t in (8, 10):
                states = jnp.concatenate([state(t - 4), state(t - 3)], axis=1)
                second("all", states, t // 2 - 2)
            elif t >= 11:
                unit = t - LAG
                if t == 11:
                    value, low = outputs["all"]
                    outputs["near"] = (value[:near], low[:near])
                    outputs["far"] = (value[near:], low[near:])
                second("near" if own_chip(unit) else "far", unfold(state(unit)), 4 + unit % 2)
                if t == 12:
                    across = core_sum("far").astype(BF16)
                    last = across
                    across = col_swap(across, 2)
        return core_sum("near") + across.astype(F32), mask

    def plain(tokens, mask, second_weight, second_down_maps, *first):
        rows = tokens.shape[0]
        states = hidden_plain(gather_tokens(tokens), mask, *first)
        outputs = jnp.concatenate([dot(states, second_weight), dot(states, second_down_maps)], axis=1)
        blocks = [outputs[i * rows : (i + 1) * rows] for i in range(n_col)]
        ours = jnp.concatenate(blocks[0::2], axis=0)
        theirs = jnp.concatenate(blocks[1::2], axis=0).astype(BF16)
        ours = ours + col_swap(theirs, 1).astype(F32)
        result = ours[:rows]
        for step in range(1, chips):
            piece = ours[step * rows : (step + 1) * rows].astype(BF16)
            result = result + col_swap(piece, 2 * step).astype(F32)
        return result

    def local(
        tokens,
        token_job_index,
        job_adapter_index,
        first_weight,
        first_bias,
        first_down_maps,
        first_up_maps,
        second_weight,
        second_bias,
        second_down_maps,
        second_up_maps,
    ):
        rows = tokens.shape[0]
        out_width = second_weight.shape[1]
        mine = lax.axis_index("col")

        def mask_of(mine, after):
            index = tie(token_job_index, after)
            for bit in range(n_col.bit_length() - 1):
                pairs = index.reshape(-1, 2, rows << bit)
                turned = jnp.concatenate([pairs[:, 1:], pairs[:, :1]], axis=1)
                index = jnp.where((mine >> bit) & 1 == 1, turned, pairs).reshape(-1)
            return token_mask(index, job_adapter_index)

        first = (first_weight, first_bias, first_down_maps, first_up_maps)
        even = first_weight.shape[1] % (UNITS * LANES) == 0
        if n_row == 4 and n_col == 4 and even:
            result, mask = pipeline(tokens, mine, mask_of, *first, second_weight, second_down_maps)
        else:
            mask = mask_of(mine, tokens)
            result = plain(tokens, mask, second_weight, second_down_maps, *first)
        low_out = jnp.where(mask[:rows], result[:, out_width:], 0.0).astype(BF16)
        layer_output = result[:, :out_width] + second_bias[None, :] + dot(low_out, second_up_maps)
        return layer_output.astype(BF16)

    return local


def solution(mesh):
    shape = mesh.shape
    return jax.shard_map(
        make_local(shape["group"], shape["row"], shape["col"]),
        mesh=mesh,
        in_specs=(
            P(("group", "col"), "row"),
            P("group"),
            P("group"),
            P("row", "col"),
            P("col"),
            P("row", None),
            P(None, "col"),
            P("col", "row"),
            P("row"),
            P("col", None),
            P(None, "row"),
        ),
        out_specs=P(("group", "col"), "row"),
        check_vma=False,
    )
```

```python
import functools

import jax
import jax.numpy as jnp
from jax import lax
from jax.experimental import pallas as pl
from jax.experimental.pallas import tpu as pltpu
from jax.sharding import PartitionSpec as P

ADAPTER_RANK = 16
ADAPTER_COUNT = 8
JOBS = 4
LANES = 128
UNITS = 12
LAG = 3
F32 = jnp.float32
BF16 = jnp.bfloat16


def gelu_tanh(values):
    return (
        0.5
        * values
        * (1.0 + jnp.tanh(0.7978845608 * (values + 0.044715 * values * values * values)))
    )


def token_mask(token_job_index, job_adapter_index):
    one_hot = token_job_index[:, None] == jnp.arange(JOBS, dtype=jnp.int32)[None, :]
    chosen = jnp.sum(jnp.where(one_hot, job_adapter_index[None, :], 0), axis=1)
    slot_ids = jnp.arange(ADAPTER_COUNT * ADAPTER_RANK, dtype=jnp.int32) // ADAPTER_RANK
    return slot_ids[None, :] == chosen[:, None]


def dot(left, right):
    return jnp.dot(left, right, preferred_element_type=F32)


def tie(value, after):
    return lax.optimization_barrier((value, after))[0]


def load_kernel(w_hbm, after_ref, out, sem, *, part):
    copy = pltpu.make_async_copy(w_hbm.at[part], out, sem)
    copy.start()
    copy.wait()


def load_part(weight, part, after):
    shape = tuple(p.size for p in part)
    return pl.pallas_call(
        functools.partial(load_kernel, part=part),
        in_specs=[pl.BlockSpec(memory_space=pl.ANY)] * 2,
        out_specs=pl.BlockSpec(memory_space=pltpu.VMEM),
        out_shape=pltpu.VMEM(shape, BF16),
        scratch_shapes=[pltpu.SemaphoreType.DMA],
        compiler_params=pltpu.CompilerParams(vmem_limit_bytes=1 << 20),
        cost_estimate=pl.CostEstimate(flops=0, bytes_accessed=1000, transcendentals=0),
    )(pltpu.with_memory_space_constraint(weight, pltpu.HBM), after)


def activate(summed, low_in, first_up_maps, first_bias, part):
    before = summed + first_bias[None, part] + dot(low_in, first_up_maps[:, part])
    return gelu_tanh(before).astype(BF16)


def hidden_plain(tokens, mask, first_weight, first_bias, first_down_maps, first_up_maps):
    width = first_weight.shape[1]
    joined = jnp.concatenate([dot(tokens, first_weight), dot(tokens, first_down_maps)], axis=1)
    summed = lax.psum_scatter(
        joined.astype(BF16), "row", scatter_dimension=0, tiled=True
    ).astype(F32)
    rows = summed.shape[0]
    own_mask = lax.dynamic_slice_in_dim(mask, lax.axis_index("row") * rows, rows, 0)
    low_in = jnp.where(own_mask, summed[:, width:], 0.0).astype(BF16)
    states = activate(summed[:, :width], low_in, first_up_maps, first_bias, slice(0, width))
    return lax.all_gather(states, "row", axis=0, tiled=True)


def make_local(n_group, n_row, n_col):
    chips = n_col // 2

    def place_of(group, row, col):
        return (group * n_row + row) * n_col + col

    cross_pairs = []
    for group in range(n_group):
        for row in range(n_row):
            for col in range(n_col):
                if n_row == 4 and row in (1, 2):
                    other = place_of(group, 3 - row, col)
                else:
                    other = place_of(group, row, col ^ 1)
                cross_pairs.append((place_of(group, row, col), other))

    def col_swap(value, flip):
        return lax.ppermute(value, "col", [(i, i ^ flip) for i in range(n_col)])

    def end_swap(value):
        return lax.ppermute(value, "row", [(i, i ^ 1) for i in range(n_row)])

    def cross(value):
        return lax.ppermute(value, ("group", "row", "col"), cross_pairs)

    def gather_tokens(tokens):
        shards = [tokens, col_swap(tokens, 1)]
        for step in range(1, chips):
            far = col_swap(tokens, 2 * step)
            shards += [far, col_swap(far, 1)]
        return jnp.concatenate(shards, axis=0)

    def pipeline(
        tokens,
        jobs,
        mine,
        mask_of,
        first_weight,
        first_bias,
        first_down_maps,
        first_up_maps,
        second_weight,
        second_down_maps,
    ):
        rows = tokens.shape[0]
        near = 2 * rows
        width = first_weight.shape[1] // UNITS
        wide = 2 * width
        fold = width // LANES
        place = lax.axis_index("row")
        is_end = (place == 0) | (place == 3)
        last = tokens
        partials, payloads, swaps, sums, crosses = {}, {}, {}, {}, {}
        total, low_total = None, None
        low_in = {}

        def halves(value):
            return jnp.concatenate([value[:, :width], value[:, width:]], axis=0)

        def unfold(value):
            return jnp.concatenate([value[:near], value[near : 2 * near]], axis=1)

        def block_of(unit):
            return unit % 3 if unit < 6 else 3 + unit % 3

        def is_near(unit):
            return unit < 3 or unit >= 9

        def columns(unit):
            return slice(block_of(unit) * wide, (block_of(unit) + 1) * wide)

        def load(block):
            nonlocal last
            part = (pl.ds(0, first_weight.shape[0]), pl.ds(block * wide, wide))
            loads[block] = load_part(first_weight, part, last)
            last = loads[block]

        def multiply(x, block):
            nonlocal last
            value = dot(tie(x, last), loads[block]).astype(BF16)
            last = value
            return value

        def first_half(unit, x):
            nonlocal last
            value = halves(multiply(x, block_of(unit)))
            if unit in (0, 3):
                low = dot(x, first_down_maps).astype(BF16)
                low = jnp.concatenate(jnp.split(low, fold, axis=0), axis=1)
                value = jnp.concatenate([value, low], axis=0)
            partials[unit] = value
            last = value

        def first_late(unit, x):
            value = multiply(x, block_of(unit))
            partials[unit + 3], partials[unit] = halves(value[:near]), halves(value[near:])

        def send(t, value):
            payloads[t] = value
            swaps[t] = end_swap(value)

        def state(unit):
            return jnp.where(is_end, swaps[unit + LAG], payloads[unit + LAG])

        def second(name, states, block):
            nonlocal last
            states = tie(states, last)
            part = slice(block * wide, (block + 1) * wide)
            low = dot(states, second_down_maps[part])
            value = dot(states, second_weight[part])
            if name in outputs:
                value, low = outputs[name][0] + value, outputs[name][1] + low
            value = lax.optimization_barrier(value)
            last = value[:8, :LANES]
            outputs[name] = (value, low)

        def core_parts(name):
            joined = jnp.concatenate(outputs[name], axis=1)
            return joined[:rows], joined[rows:].astype(BF16)

        far = col_swap(tokens, 2)
        loads, outputs = {}, {}
        last, is_end, mine = lax.optimization_barrier((jobs, is_end, mine))
        load(0)
        gathered_near = jnp.concatenate([tokens, tie(col_swap(tokens, 1), last)], axis=0)
        for unit in range(3):
            if unit > 0:
                load(unit)
            first_half(unit, gathered_near)
            send(unit, partials[unit])
        mask = mask_of(mine, last)
        first_bias = tie(first_bias, last)
        for t in range(UNITS + LAG):
            if t < UNITS:
                ours = tie(partials[t], last).astype(F32)
                sums[t] = (ours + swaps[t].astype(F32)).astype(BF16)
                last = sums[t]
                crosses[t] = cross(sums[t])
            if t == 0:
                gathered_far = jnp.concatenate([far, col_swap(far, 1)], axis=0)
                gathered = jnp.concatenate([gathered_near, gathered_far], axis=0)
                for unit in range(3, 6):
                    first_half(unit, gathered_far)
            k = t - 1
            if 0 <= k < UNITS:
                summed = tie(sums[k], last).astype(F32) + crosses[k].astype(F32)
                if k in (0, 3):
                    low = jnp.concatenate(jnp.split(summed[2 * near :], fold, axis=1), axis=0)
                    own_mask = mask[:near] if k == 0 else mask[near:]
                    low_in[is_near(k)] = jnp.where(own_mask, low, 0.0).astype(BF16)
                low = low_in[is_near(k)]
                value = activate(unfold(summed), low, first_up_maps, first_bias, columns(k))
                value = halves(value)
                if k + LAG == 3:
                    value = jnp.concatenate([value, jnp.zeros_like(value[: near // fold])], axis=0)
                if k + LAG < UNITS:
                    value = jnp.where(is_end, partials[k + LAG], value)
                last = value
                send(k + LAG, value)
            if t in (1, 2, 3):
                load(t + 2)
                first_late(t + 5, gathered)
            elif t in (6, 7, 8):
                top, bottom = unfold(state(t - 6)), unfold(state(t - 3))
                second("all", jnp.concatenate([top, bottom], axis=0), t - 6)
            elif t >= 9:
                unit = t - LAG
                if t == 9:
                    value, low = outputs["all"]
                    outputs["near"] = (value[:near], low[:near])
                    outputs["far"] = (value[near:], low[near:])
                if t == 13:
                    last = across
                second("near" if is_near(unit) else "far", unfold(state(unit)), block_of(unit))
                if t == 11:
                    ours, theirs = core_parts("far")
                    across = (ours + col_swap(theirs, 1).astype(F32)).astype(BF16)
                    last = across
                    across = col_swap(across, 2)
        ours, theirs = core_parts("near")
        come = col_swap(theirs, 1)
        return ours + come.astype(F32) + across.astype(F32), mask

    def plain(tokens, mask, second_weight, second_down_maps, *first):
        rows = tokens.shape[0]
        states = hidden_plain(gather_tokens(tokens), mask, *first)
        outputs = jnp.concatenate([dot(states, second_weight), dot(states, second_down_maps)], axis=1)
        blocks = [outputs[i * rows : (i + 1) * rows] for i in range(n_col)]
        ours = jnp.concatenate(blocks[0::2], axis=0)
        theirs = jnp.concatenate(blocks[1::2], axis=0).astype(BF16)
        ours = ours + col_swap(theirs, 1).astype(F32)
        result = ours[:rows]
        for step in range(1, chips):
            piece = ours[step * rows : (step + 1) * rows].astype(BF16)
            result = result + col_swap(piece, 2 * step).astype(F32)
        return result

    def local(
        tokens,
        token_job_index,
        job_adapter_index,
        first_weight,
        first_bias,
        first_down_maps,
        first_up_maps,
        second_weight,
        second_bias,
        second_down_maps,
        second_up_maps,
    ):
        rows = tokens.shape[0]
        out_width = second_weight.shape[1]
        mine = lax.axis_index("col")

        def mask_of(mine, after):
            mask = token_mask(tie(token_job_index, after), job_adapter_index).astype(jnp.int32)
            for bit in range(n_col.bit_length() - 1):
                size = rows << bit
                blocks = [mask[i : i + size] for i in range(0, mask.shape[0], size)]
                turned = jnp.concatenate([blocks[i ^ 1] for i in range(len(blocks))], axis=0)
                mask = jnp.where((mine >> bit) & 1 == 1, turned, mask)
            return mask == 1

        first = (first_weight, first_bias, first_down_maps, first_up_maps)
        even = first_weight.shape[1] % (UNITS * LANES) == 0
        if n_row == 4 and n_col == 4 and even:
            result, mask = pipeline(tokens, job_adapter_index, mine, mask_of, *first, second_weight, second_down_maps)
        else:
            mask = mask_of(mine, tokens)
            result = plain(tokens, mask, second_weight, second_down_maps, *first)
        low_out = jnp.where(mask[:rows], result[:, out_width:], 0.0).astype(BF16)
        layer_output = result[:, :out_width] + second_bias[None, :] + dot(low_out, second_up_maps)
        return layer_output.astype(BF16)

    return local


def solution(mesh):
    shape = mesh.shape
    return jax.shard_map(
        make_local(shape["group"], shape["row"], shape["col"]),
        mesh=mesh,
        in_specs=(
            P(("group", "col"), "row"),
            P("group"),
            P("group"),
            P("row", "col"),
            P("col"),
            P("row", None),
            P(None, "col"),
            P("col", "row"),
            P("row"),
            P("col", None),
            P(None, "row"),
        ),
        out_specs=P(("group", "col"), "row"),
        check_vma=False,
    )
```

```python
import functools

import jax
import jax.numpy as jnp
from jax import lax
from jax.experimental import pallas as pl
from jax.experimental.pallas import tpu as pltpu
from jax.sharding import PartitionSpec as P

ADAPTER_RANK = 16
ADAPTER_COUNT = 8
JOBS = 4
LANES = 128
UNITS = 12
LAG = 4
F32 = jnp.float32
BF16 = jnp.bfloat16


def gelu_tanh(values):
    return (
        0.5
        * values
        * (1.0 + jnp.tanh(0.7978845608 * (values + 0.044715 * values * values * values)))
    )


def token_mask(token_job_index, job_adapter_index):
    one_hot = token_job_index[:, None] == jnp.arange(JOBS, dtype=jnp.int32)[None, :]
    chosen = jnp.sum(jnp.where(one_hot, job_adapter_index[None, :], 0), axis=1)
    slot_ids = jnp.arange(ADAPTER_COUNT * ADAPTER_RANK, dtype=jnp.int32) // ADAPTER_RANK
    return slot_ids[None, :] == chosen[:, None]


def dot(left, right):
    return jnp.dot(left, right, preferred_element_type=F32)


def tie(value, after):
    return lax.optimization_barrier((value, after))[0]


def load_kernel(w_hbm, after_ref, out, sem, *, part):
    copy = pltpu.make_async_copy(w_hbm.at[part], out, sem)
    copy.start()
    copy.wait()


def load_part(weight, part, after):
    shape = tuple(p.size for p in part)
    return pl.pallas_call(
        functools.partial(load_kernel, part=part),
        in_specs=[pl.BlockSpec(memory_space=pl.ANY)] * 2,
        out_specs=pl.BlockSpec(memory_space=pltpu.VMEM),
        out_shape=pltpu.VMEM(shape, BF16),
        scratch_shapes=[pltpu.SemaphoreType.DMA],
        compiler_params=pltpu.CompilerParams(vmem_limit_bytes=1 << 20),
        cost_estimate=pl.CostEstimate(flops=0, bytes_accessed=1000, transcendentals=0),
    )(pltpu.with_memory_space_constraint(weight, pltpu.HBM), after)


def activate(summed, low_in, first_up_maps, first_bias, part):
    before = summed + first_bias[None, part] + dot(low_in, first_up_maps[:, part])
    return gelu_tanh(before).astype(BF16)


def hidden_plain(tokens, mask, first_weight, first_bias, first_down_maps, first_up_maps):
    width = first_weight.shape[1]
    joined = jnp.concatenate([dot(tokens, first_weight), dot(tokens, first_down_maps)], axis=1)
    summed = lax.psum_scatter(
        joined.astype(BF16), "row", scatter_dimension=0, tiled=True
    ).astype(F32)
    rows = summed.shape[0]
    own_mask = lax.dynamic_slice_in_dim(mask, lax.axis_index("row") * rows, rows, 0)
    low_in = jnp.where(own_mask, summed[:, width:], 0.0).astype(BF16)
    states = activate(summed[:, :width], low_in, first_up_maps, first_bias, slice(0, width))
    return lax.all_gather(states, "row", axis=0, tiled=True)


def make_local(n_group, n_row, n_col):
    chips = n_col // 2

    def place_of(group, row, col):
        return (group * n_row + row) * n_col + col

    cross_pairs = []
    for group in range(n_group):
        for row in range(n_row):
            for col in range(n_col):
                if n_row == 4 and row in (1, 2):
                    other = place_of(group, 3 - row, col)
                else:
                    other = place_of(group, row, col ^ 1)
                cross_pairs.append((place_of(group, row, col), other))

    def col_swap(value, flip):
        return lax.ppermute(value, "col", [(i, i ^ flip) for i in range(n_col)])

    def end_swap(value):
        return lax.ppermute(value, "row", [(i, i ^ 1) for i in range(n_row)])

    def cross(value):
        return lax.ppermute(value, ("group", "row", "col"), cross_pairs)

    def gather_tokens(tokens):
        shards = [tokens, col_swap(tokens, 1)]
        for step in range(1, chips):
            far = col_swap(tokens, 2 * step)
            shards += [far, col_swap(far, 1)]
        return jnp.concatenate(shards, axis=0)

    def pipeline(
        tokens,
        jobs,
        mine,
        mask_of,
        first_weight,
        first_bias,
        first_down_maps,
        first_up_maps,
        second_weight,
        second_down_maps,
    ):
        rows = tokens.shape[0]
        near = 2 * rows
        width = first_weight.shape[1] // UNITS
        wide = 2 * width
        early = UNITS // 4
        fold = max(n for n in range(1, width // LANES + 1) if near % n == 0)
        place = lax.axis_index("row")
        is_end = (place == 0) | (place == 3)
        last = tokens
        partials, payloads, swaps, sums, crosses = {}, {}, {}, {}, {}
        total, low_total = None, None
        low_in = {}

        def halves(value):
            return jnp.concatenate([value[:, :width], value[:, width:]], axis=0)

        def unfold(value):
            return jnp.concatenate([value[:near], value[near : 2 * near]], axis=1)

        def block_of(unit):
            return unit % early + (early if unit >= 2 * early else 0)

        def is_near(unit):
            return unit < early or unit >= 3 * early

        def columns(unit):
            return slice(block_of(unit) * wide, (block_of(unit) + 1) * wide)

        def load(block):
            nonlocal last
            part = (pl.ds(0, first_weight.shape[0]), pl.ds(block * wide, wide))
            loads[block] = load_part(first_weight, part, last)
            last = loads[block]

        def multiply(x, block):
            nonlocal last
            value = dot(tie(x, last), loads[block]).astype(BF16)
            last = value
            return value

        def first_half(unit, x):
            nonlocal last
            value = halves(multiply(x, block_of(unit)))
            if unit in (0, early):
                low = dot(x, first_down_maps).astype(BF16)
                low = jnp.concatenate(jnp.split(low, fold, axis=0), axis=1)
                low = jnp.pad(low, ((0, 0), (0, width - fold * LANES)))
                value = jnp.concatenate([value, low], axis=0)
            partials[unit] = value
            last = value

        def first_late(unit, x):
            value = multiply(x, block_of(unit))
            partials[unit + early], partials[unit] = halves(value[:near]), halves(value[near:])

        def send(t, value):
            payloads[t] = value
            swaps[t] = end_swap(value)

        def state(unit):
            come = tie(swaps[unit + LAG], last)
            return jnp.where(is_end, come, payloads[unit + LAG])

        def second(name, states, block):
            nonlocal last
            states = tie(states, last)
            part = slice(block * wide, (block + 1) * wide)
            low = dot(states, second_down_maps[part])
            value = dot(states, second_weight[part])
            if name in outputs:
                value, low = outputs[name][0] + value, outputs[name][1] + low
            value = lax.optimization_barrier(value)
            last = value[:8, :LANES]
            outputs[name] = (value, low)

        def core_parts(name):
            joined = jnp.concatenate(outputs[name], axis=1)
            return joined[:rows], joined[rows:].astype(BF16)

        far = col_swap(tokens, 2)
        loads, outputs = {}, {}
        last, is_end, mine = lax.optimization_barrier((jobs, is_end, mine))
        load(0)
        gathered_near = jnp.concatenate([tokens, tie(col_swap(tokens, 1), last)], axis=0)
        for unit in range(early):
            if unit > 0:
                load(unit)
            first_half(unit, gathered_near)
            send(unit, partials[unit])
        mask = mask_of(mine, last)
        first_bias = tie(first_bias, last)
        for t in range(UNITS + LAG):
            if t < UNITS:
                ours = tie(partials[t], last).astype(F32)
                sums[t] = (ours + swaps[t].astype(F32)).astype(BF16)
                last = sums[t]
                crosses[t] = cross(sums[t])
            if t == 0:
                gathered_far = jnp.concatenate([far, col_swap(far, 1)], axis=0)
                gathered = jnp.concatenate([gathered_near, gathered_far], axis=0)
            if t < early:
                first_half(early + t, gathered_far)
                if early + t < LAG:
                    send(early + t, partials[early + t])
            k = t - 1
            if 0 <= k < UNITS:
                summed = tie(sums[k], last).astype(F32) + crosses[k].astype(F32)
                if k in (0, early):
                    low = jnp.split(summed[2 * near :, : fold * LANES], fold, axis=1)
                    low = jnp.concatenate(low, axis=0)
                    own_mask = mask[:near] if k == 0 else mask[near:]
                    low_in[is_near(k)] = jnp.where(own_mask, low, 0.0).astype(BF16)
                low = low_in[is_near(k)]
                value = activate(unfold(summed), low, first_up_maps, first_bias, columns(k))
                value = halves(value)
                if k + LAG == early:
                    value = jnp.concatenate([value, jnp.zeros_like(value[: near // fold])], axis=0)
                if k + LAG < UNITS:
                    value = jnp.where(is_end, partials[k + LAG], value)
                last = value
                send(k + LAG, value)
            unit = t - LAG
            if 1 <= t <= early:
                load(early + t - 1)
                first_late(2 * early + t - 1, gathered)
            if early <= unit < 2 * early:
                top, bottom = unfold(state(unit - early)), unfold(state(unit))
                second("all", jnp.concatenate([top, bottom], axis=0), unit - early)
            elif unit >= 2 * early:
                if unit == 2 * early:
                    value, low = outputs["all"]
                    outputs["near"] = (value[:near], low[:near])
                    outputs["far"] = (value[near:], low[near:])
                if unit == UNITS - 1:
                    last = across
                second("near" if is_near(unit) else "far", unfold(state(unit)), block_of(unit))
                if unit == 3 * early - 1:
                    ours, theirs = core_parts("far")
                    across = (ours + col_swap(theirs, 1).astype(F32)).astype(BF16)
                    across = col_swap(across, 2)
        ours, theirs = core_parts("near")
        come = col_swap(theirs, 1)
        return ours + come.astype(F32) + across.astype(F32), mask

    def plain(tokens, mask, second_weight, second_down_maps, *first):
        rows = tokens.shape[0]
        states = hidden_plain(gather_tokens(tokens), mask, *first)
        outputs = jnp.concatenate([dot(states, second_weight), dot(states, second_down_maps)], axis=1)
        blocks = [outputs[i * rows : (i + 1) * rows] for i in range(n_col)]
        ours = jnp.concatenate(blocks[0::2], axis=0)
        theirs = jnp.concatenate(blocks[1::2], axis=0).astype(BF16)
        ours = ours + col_swap(theirs, 1).astype(F32)
        result = ours[:rows]
        for step in range(1, chips):
            piece = ours[step * rows : (step + 1) * rows].astype(BF16)
            result = result + col_swap(piece, 2 * step).astype(F32)
        return result

    def local(
        tokens,
        token_job_index,
        job_adapter_index,
        first_weight,
        first_bias,
        first_down_maps,
        first_up_maps,
        second_weight,
        second_bias,
        second_down_maps,
        second_up_maps,
    ):
        rows = tokens.shape[0]
        out_width = second_weight.shape[1]
        mine = lax.axis_index("col")

        def mask_of(mine, after):
            mask = token_mask(tie(token_job_index, after), job_adapter_index).astype(jnp.int32)
            for bit in range(n_col.bit_length() - 1):
                size = rows << bit
                blocks = [mask[i : i + size] for i in range(0, mask.shape[0], size)]
                turned = jnp.concatenate([blocks[i ^ 1] for i in range(len(blocks))], axis=0)
                mask = jnp.where((mine >> bit) & 1 == 1, turned, mask)
            return mask == 1

        first = (first_weight, first_bias, first_down_maps, first_up_maps)
        even = first_weight.shape[1] % (UNITS * LANES) == 0
        if n_row == 4 and n_col == 4 and even:
            result, mask = pipeline(tokens, job_adapter_index, mine, mask_of, *first, second_weight, second_down_maps)
        else:
            mask = mask_of(mine, tokens)
            result = plain(tokens, mask, second_weight, second_down_maps, *first)
        low_out = jnp.where(mask[:rows], result[:, out_width:], 0.0).astype(BF16)
        layer_output = result[:, :out_width] + second_bias[None, :] + dot(low_out, second_up_maps)
        return layer_output.astype(BF16)

    return local


def solution(mesh):
    shape = mesh.shape
    return jax.shard_map(
        make_local(shape["group"], shape["row"], shape["col"]),
        mesh=mesh,
        in_specs=(
            P(("group", "col"), "row"),
            P("group"),
            P("group"),
            P("row", "col"),
            P("col"),
            P("row", None),
            P(None, "col"),
            P("col", "row"),
            P("row"),
            P("col", None),
            P(None, "row"),
        ),
        out_specs=P(("group", "col"), "row"),
        check_vma=False,
    )
```

```python
import functools

import jax
import jax.numpy as jnp
from jax import lax
from jax.experimental import pallas as pl
from jax.experimental.pallas import tpu as pltpu
from jax.sharding import PartitionSpec as P

ADAPTER_RANK = 16
ADAPTER_COUNT = 8
JOBS = 4
LANES = 128
UNITS = 12
LAG = 4
F32 = jnp.float32
BF16 = jnp.bfloat16


def gelu_tanh(values):
    return (
        0.5
        * values
        * (1.0 + jnp.tanh(0.7978845608 * (values + 0.044715 * values * values * values)))
    )


def token_mask(token_job_index, job_adapter_index):
    one_hot = token_job_index[:, None] == jnp.arange(JOBS, dtype=jnp.int32)[None, :]
    chosen = jnp.sum(jnp.where(one_hot, job_adapter_index[None, :], 0), axis=1)
    slot_ids = jnp.arange(ADAPTER_COUNT * ADAPTER_RANK, dtype=jnp.int32) // ADAPTER_RANK
    return slot_ids[None, :] == chosen[:, None]


def dot(left, right):
    return jnp.dot(left, right, preferred_element_type=F32)


def tie(value, after):
    return lax.optimization_barrier((value, after))[0]


def load_kernel(w_hbm, after_ref, out, sem, *, part):
    copy = pltpu.make_async_copy(w_hbm.at[part], out, sem)
    copy.start()
    copy.wait()


def load_part(weight, part, after):
    shape = tuple(p.size for p in part)
    return pl.pallas_call(
        functools.partial(load_kernel, part=part),
        in_specs=[pl.BlockSpec(memory_space=pl.ANY)] * 2,
        out_specs=pl.BlockSpec(memory_space=pltpu.VMEM),
        out_shape=pltpu.VMEM(shape, BF16),
        scratch_shapes=[pltpu.SemaphoreType.DMA],
        compiler_params=pltpu.CompilerParams(vmem_limit_bytes=1 << 20),
        cost_estimate=pl.CostEstimate(flops=0, bytes_accessed=1000, transcendentals=0),
    )(pltpu.with_memory_space_constraint(weight, pltpu.HBM), after)


def activate(summed, low_in, first_up_maps, first_bias, part):
    before = summed + first_bias[None, part] + dot(low_in, first_up_maps[:, part])
    return gelu_tanh(before).astype(BF16)


def hidden_plain(tokens, mask, first_weight, first_bias, first_down_maps, first_up_maps):
    width = first_weight.shape[1]
    joined = jnp.concatenate([dot(tokens, first_weight), dot(tokens, first_down_maps)], axis=1)
    summed = lax.psum_scatter(
        joined.astype(BF16), "row", scatter_dimension=0, tiled=True
    ).astype(F32)
    rows = summed.shape[0]
    own_mask = lax.dynamic_slice_in_dim(mask, lax.axis_index("row") * rows, rows, 0)
    low_in = jnp.where(own_mask, summed[:, width:], 0.0).astype(BF16)
    states = activate(summed[:, :width], low_in, first_up_maps, first_bias, slice(0, width))
    return lax.all_gather(states, "row", axis=0, tiled=True)


def make_local(n_group, n_row, n_col):
    chips = n_col // 2

    def place_of(group, row, col):
        return (group * n_row + row) * n_col + col

    cross_pairs = []
    for group in range(n_group):
        for row in range(n_row):
            for col in range(n_col):
                if n_row == 4 and row in (1, 2):
                    other = place_of(group, 3 - row, col)
                else:
                    other = place_of(group, row, col ^ 1)
                cross_pairs.append((place_of(group, row, col), other))

    def col_swap(value, flip):
        return lax.ppermute(value, "col", [(i, i ^ flip) for i in range(n_col)])

    def end_swap(value):
        return lax.ppermute(value, "row", [(i, i ^ 1) for i in range(n_row)])

    def cross(value):
        return lax.ppermute(value, ("group", "row", "col"), cross_pairs)

    def gather_tokens(tokens):
        shards = [tokens, col_swap(tokens, 1)]
        for step in range(1, chips):
            far = col_swap(tokens, 2 * step)
            shards += [far, col_swap(far, 1)]
        return jnp.concatenate(shards, axis=0)

    def pipeline(
        tokens,
        jobs,
        mine,
        mask_of,
        first_weight,
        first_bias,
        first_down_maps,
        first_up_maps,
        second_weight,
        second_down_maps,
    ):
        rows = tokens.shape[0]
        near = 2 * rows
        width = first_weight.shape[1] // UNITS
        wide = 2 * width
        early = UNITS // 4
        fold = max(n for n in range(1, width // LANES + 1) if near % n == 0)
        place = lax.axis_index("row")
        is_end = (place == 0) | (place == 3)
        last = tokens
        partials, payloads, swaps, sums, crosses = {}, {}, {}, {}, {}
        total, low_total = None, None
        low_in = {}

        def halves(value):
            return jnp.concatenate([value[:, :width], value[:, width:]], axis=0)

        def unfold(value):
            return jnp.concatenate([value[:near], value[near : 2 * near]], axis=1)

        def block_of(unit):
            return unit % early + (early if unit >= 2 * early else 0)

        def is_near(unit):
            return unit < early or unit >= 3 * early

        def columns(unit):
            return slice(block_of(unit) * wide, (block_of(unit) + 1) * wide)

        def load(block):
            nonlocal last
            part = (pl.ds(0, first_weight.shape[0]), pl.ds(block * wide, wide))
            loads[block] = load_part(first_weight, part, last)
            last = loads[block]

        def load_second(block):
            nonlocal last
            part = (pl.ds(block * wide, wide), pl.ds(0, second_weight.shape[1]))
            second_loads[block] = load_part(second_weight, part, last)
            last = second_loads[block]

        def multiply(x, block):
            nonlocal last
            value = dot(tie(x, last), loads[block]).astype(BF16)
            last = value
            return value

        def first_half(unit, x):
            nonlocal last
            value = halves(multiply(x, block_of(unit)))
            if unit in (0, early):
                low = dot(x, first_down_maps).astype(BF16)
                low = jnp.concatenate(jnp.split(low, fold, axis=0), axis=1)
                low = jnp.pad(low, ((0, 0), (0, width - fold * LANES)))
                value = jnp.concatenate([value, low], axis=0)
            partials[unit] = value
            last = value

        def first_late(unit, x):
            value = multiply(x, block_of(unit))
            partials[unit + early], partials[unit] = halves(value[:near]), halves(value[near:])

        def send(t, value):
            payloads[t] = value
            swaps[t] = end_swap(value)

        def state(unit):
            come = tie(swaps[unit + LAG], last)
            return jnp.where(is_end, come, payloads[unit + LAG])

        def second(name, states, block):
            nonlocal last
            states = tie(states, last)
            part = slice(block * wide, (block + 1) * wide)
            low = dot(states, second_down_maps[part])
            value = dot(states, second_loads[block])
            if name in outputs:
                value, low = outputs[name][0] + value, outputs[name][1] + low
            value = lax.optimization_barrier(value)
            last = value[:8, :LANES]
            outputs[name] = (value, low)

        def core_parts(name):
            joined = jnp.concatenate(outputs[name], axis=1)
            return joined[:rows], joined[rows:].astype(BF16)

        loads, second_loads, outputs = {}, {}, {}
        last, is_end, mine = lax.optimization_barrier((jobs, is_end, mine))
        load(0)
        gathered_near = jnp.concatenate([tokens, tie(col_swap(tokens, 1), last)], axis=0)
        for unit in range(early):
            if unit > 0:
                load(unit)
            first_half(unit, gathered_near)
            send(unit, partials[unit])
            if unit == 0:
                far = col_swap(tie(tokens, last), 2)
        mask = mask_of(mine, last)
        first_bias = tie(first_bias, last)
        for t in range(UNITS + LAG):
            if t < UNITS:
                ours = tie(partials[t], last).astype(F32)
                sums[t] = (ours + swaps[t].astype(F32)).astype(BF16)
                last = sums[t]
                crosses[t] = cross(sums[t])
            if t == 0:
                gathered_far = jnp.concatenate([far, col_swap(far, 1)], axis=0)
            if t < early:
                first_half(early + t, gathered_far)
                if early + t < LAG:
                    send(early + t, partials[early + t])
            k = t - 1
            if 0 <= k < UNITS:
                summed = tie(sums[k], last).astype(F32) + crosses[k].astype(F32)
                if k in (0, early):
                    low = jnp.split(summed[2 * near :, : fold * LANES], fold, axis=1)
                    low = jnp.concatenate(low, axis=0)
                    own_mask = mask[:near] if k == 0 else mask[near:]
                    low_in[is_near(k)] = jnp.where(own_mask, low, 0.0).astype(BF16)
                low = low_in[is_near(k)]
                value = activate(unfold(summed), low, first_up_maps, first_bias, columns(k))
                value = halves(value)
                if k + LAG == early:
                    value = jnp.concatenate([value, jnp.zeros_like(value[: near // fold])], axis=0)
                if k + LAG < UNITS:
                    value = jnp.where(is_end, partials[k + LAG], value)
                last = value
                send(k + LAG, value)
            unit = t - LAG
            if t == 1:
                whole = tie((gathered_near, gathered_far), last)
                gathered = jnp.concatenate(whole, axis=0)
            if LAG <= t < LAG + 2 * early:
                load_second(t - LAG)
            if 1 <= t <= early:
                load(early + t - 1)
                first_late(2 * early + t - 1, gathered)
            if early <= unit < 2 * early:
                top, bottom = unfold(state(unit - early)), unfold(state(unit))
                second("all", jnp.concatenate([top, bottom], axis=0), unit - early)
            elif unit >= 2 * early:
                if unit == 2 * early:
                    value, low = outputs["all"]
                    outputs["near"] = (value[:near], low[:near])
                    outputs["far"] = (value[near:], low[near:])
                if unit == UNITS - 1:
                    last = across
                second("near" if is_near(unit) else "far", unfold(state(unit)), block_of(unit))
                if unit == 3 * early - 1:
                    ours, theirs = core_parts("far")
                    across = (ours + col_swap(theirs, 1).astype(F32)).astype(BF16)
                    across = col_swap(across, 2)
        ours, theirs = core_parts("near")
        come = col_swap(theirs, 1)
        return ours + come.astype(F32) + across.astype(F32), mask

    def plain(tokens, mask, second_weight, second_down_maps, *first):
        rows = tokens.shape[0]
        states = hidden_plain(gather_tokens(tokens), mask, *first)
        outputs = jnp.concatenate([dot(states, second_weight), dot(states, second_down_maps)], axis=1)
        blocks = [outputs[i * rows : (i + 1) * rows] for i in range(n_col)]
        ours = jnp.concatenate(blocks[0::2], axis=0)
        theirs = jnp.concatenate(blocks[1::2], axis=0).astype(BF16)
        ours = ours + col_swap(theirs, 1).astype(F32)
        result = ours[:rows]
        for step in range(1, chips):
            piece = ours[step * rows : (step + 1) * rows].astype(BF16)
            result = result + col_swap(piece, 2 * step).astype(F32)
        return result

    def local(
        tokens,
        token_job_index,
        job_adapter_index,
        first_weight,
        first_bias,
        first_down_maps,
        first_up_maps,
        second_weight,
        second_bias,
        second_down_maps,
        second_up_maps,
    ):
        rows = tokens.shape[0]
        out_width = second_weight.shape[1]
        mine = lax.axis_index("col")

        def mask_of(mine, after):
            mask = token_mask(tie(token_job_index, after), job_adapter_index).astype(jnp.int32)
            for bit in range(n_col.bit_length() - 1):
                size = rows << bit
                blocks = [mask[i : i + size] for i in range(0, mask.shape[0], size)]
                turned = jnp.concatenate([blocks[i ^ 1] for i in range(len(blocks))], axis=0)
                mask = jnp.where((mine >> bit) & 1 == 1, turned, mask)
            return mask == 1

        first = (first_weight, first_bias, first_down_maps, first_up_maps)
        even = first_weight.shape[1] % (UNITS * LANES) == 0
        if n_row == 4 and n_col == 4 and even:
            result, mask = pipeline(tokens, job_adapter_index, mine, mask_of, *first, second_weight, second_down_maps)
        else:
            mask = mask_of(mine, tokens)
            result = plain(tokens, mask, second_weight, second_down_maps, *first)
        low_out = jnp.where(mask[:rows], result[:, out_width:], 0.0).astype(BF16)
        layer_output = result[:, :out_width] + second_bias[None, :] + dot(low_out, second_up_maps)
        return layer_output.astype(BF16)

    return local


def solution(mesh):
    shape = mesh.shape
    return jax.shard_map(
        make_local(shape["group"], shape["row"], shape["col"]),
        mesh=mesh,
        in_specs=(
            P(("group", "col"), "row"),
            P("group"),
            P("group"),
            P("row", "col"),
            P("col"),
            P("row", None),
            P(None, "col"),
            P("col", "row"),
            P("row"),
            P("col", None),
            P(None, "row"),
        ),
        out_specs=P(("group", "col"), "row"),
        check_vma=False,
    )
```

```python
import functools

import jax
import jax.numpy as jnp
from jax import lax
from jax.experimental import pallas as pl
from jax.experimental.pallas import tpu as pltpu
from jax.sharding import PartitionSpec as P

ADAPTER_RANK = 16
ADAPTER_COUNT = 8
JOBS = 4
LANES = 128
UNITS = 12
LAG = 4
F32 = jnp.float32
BF16 = jnp.bfloat16


def gelu_tanh(values):
    return (
        0.5
        * values
        * (1.0 + jnp.tanh(0.7978845608 * (values + 0.044715 * values * values * values)))
    )


def token_mask(token_job_index, job_adapter_index):
    one_hot = token_job_index[:, None] == jnp.arange(JOBS, dtype=jnp.int32)[None, :]
    chosen = jnp.sum(jnp.where(one_hot, job_adapter_index[None, :], 0), axis=1)
    slot_ids = jnp.arange(ADAPTER_COUNT * ADAPTER_RANK, dtype=jnp.int32) // ADAPTER_RANK
    return slot_ids[None, :] == chosen[:, None]


def dot(left, right):
    return jnp.dot(left, right, preferred_element_type=F32)


def tie(value, after):
    return lax.optimization_barrier((value, after))[0]


def load_kernel(w_hbm, after_ref, out, sem, *, part):
    copy = pltpu.make_async_copy(w_hbm.at[part], out, sem)
    copy.start()
    copy.wait()


def load_part(weight, part, after):
    shape = tuple(p.size for p in part)
    return pl.pallas_call(
        functools.partial(load_kernel, part=part),
        in_specs=[pl.BlockSpec(memory_space=pl.ANY)] * 2,
        out_specs=pl.BlockSpec(memory_space=pltpu.VMEM),
        out_shape=pltpu.VMEM(shape, BF16),
        scratch_shapes=[pltpu.SemaphoreType.DMA],
        compiler_params=pltpu.CompilerParams(vmem_limit_bytes=1 << 20),
        cost_estimate=pl.CostEstimate(flops=0, bytes_accessed=1000, transcendentals=0),
    )(pltpu.with_memory_space_constraint(weight, pltpu.HBM), after)


def activate(summed, low_in, first_up_maps, first_bias, part):
    before = summed + first_bias[None, part] + dot(low_in, first_up_maps[:, part])
    return gelu_tanh(before).astype(BF16)


def hidden_plain(tokens, mask, first_weight, first_bias, first_down_maps, first_up_maps):
    width = first_weight.shape[1]
    joined = jnp.concatenate([dot(tokens, first_weight), dot(tokens, first_down_maps)], axis=1)
    summed = lax.psum_scatter(
        joined.astype(BF16), "row", scatter_dimension=0, tiled=True
    ).astype(F32)
    rows = summed.shape[0]
    own_mask = lax.dynamic_slice_in_dim(mask, lax.axis_index("row") * rows, rows, 0)
    low_in = jnp.where(own_mask, summed[:, width:], 0.0).astype(BF16)
    states = activate(summed[:, :width], low_in, first_up_maps, first_bias, slice(0, width))
    return lax.all_gather(states, "row", axis=0, tiled=True)


def make_local(n_group, n_row, n_col):
    chips = n_col // 2

    def place_of(group, row, col):
        return (group * n_row + row) * n_col + col

    cross_pairs = []
    for group in range(n_group):
        for row in range(n_row):
            for col in range(n_col):
                if n_row == 4 and row in (1, 2):
                    other = place_of(group, 3 - row, col)
                else:
                    other = place_of(group, row, col ^ 1)
                cross_pairs.append((place_of(group, row, col), other))

    def col_swap(value, flip):
        return lax.ppermute(value, "col", [(i, i ^ flip) for i in range(n_col)])

    def end_swap(value):
        return lax.ppermute(value, "row", [(i, i ^ 1) for i in range(n_row)])

    def cross(value):
        return lax.ppermute(value, ("group", "row", "col"), cross_pairs)

    def gather_tokens(tokens):
        shards = [tokens, col_swap(tokens, 1)]
        for step in range(1, chips):
            far = col_swap(tokens, 2 * step)
            shards += [far, col_swap(far, 1)]
        return jnp.concatenate(shards, axis=0)

    def pipeline(
        tokens,
        jobs,
        mine,
        mask_of,
        first_weight,
        first_bias,
        first_down_maps,
        first_up_maps,
        second_weight,
        second_down_maps,
    ):
        rows = tokens.shape[0]
        near = 2 * rows
        width = first_weight.shape[1] // UNITS
        wide = 2 * width
        early = UNITS // 4
        fold = max(n for n in range(1, width // LANES + 1) if near % n == 0)
        place = lax.axis_index("row")
        is_end = (place == 0) | (place == 3)
        last = tokens
        partials, payloads, swaps, sums, crosses = {}, {}, {}, {}, {}
        total, low_total = None, None
        low_in = {}

        def halves(value):
            return jnp.concatenate([value[:, :width], value[:, width:]], axis=0)

        def unfold(value):
            return jnp.concatenate([value[:near], value[near : 2 * near]], axis=1)

        def block_of(unit):
            return unit % early + (early if unit >= 2 * early else 0)

        def is_near(unit):
            return unit < early or unit >= 3 * early

        def columns(unit):
            return slice(block_of(unit) * wide, (block_of(unit) + 1) * wide)

        def load(block):
            nonlocal last
            part = (pl.ds(0, first_weight.shape[0]), pl.ds(block * wide, wide))
            loads[block] = load_part(first_weight, part, last)
            last = loads[block]

        def multiply(x, block):
            nonlocal last
            value = dot(tie(x, last), loads[block]).astype(BF16)
            last = value
            return value

        def first_half(unit, x):
            nonlocal last
            value = halves(multiply(x, block_of(unit)))
            if unit in (0, early):
                low = dot(x, first_down_maps).astype(BF16)
                low = jnp.concatenate(jnp.split(low, fold, axis=0), axis=1)
                low = jnp.pad(low, ((0, 0), (0, width - fold * LANES)))
                value = jnp.concatenate([value, low], axis=0)
            partials[unit] = value
            last = value

        def first_late(unit, x):
            value = multiply(x, block_of(unit))
            partials[unit + early], partials[unit] = halves(value[:near]), halves(value[near:])

        def send(t, value):
            payloads[t] = value
            swaps[t] = end_swap(value)

        def state(unit):
            come = tie(swaps[unit + LAG], last)
            return jnp.where(is_end, come, payloads[unit + LAG])

        def second(name, states, block):
            nonlocal last
            states = tie(states, last)
            part = slice(block * wide, (block + 1) * wide)
            low = dot(states, second_down_maps[part])
            value = dot(states, second_weight[part])
            if name in outputs:
                value, low = outputs[name][0] + value, outputs[name][1] + low
            value = lax.optimization_barrier(value)
            last = value[:8, :LANES]
            outputs[name] = (value, low)

        def core_parts(name):
            joined = jnp.concatenate(outputs[name], axis=1)
            return joined[:rows], joined[rows:].astype(BF16)

        far = col_swap(tokens, 2)
        loads, outputs = {}, {}
        last, is_end, mine = lax.optimization_barrier((jobs, is_end, mine))
        load(0)
        gathered_near = jnp.concatenate([tokens, tie(col_swap(tokens, 1), last)], axis=0)
        for unit in range(early):
            if unit > 0:
                load(unit)
            first_half(unit, gathered_near)
            send(unit, partials[unit])
        mask = mask_of(mine, last)
        first_bias = tie(first_bias, last)
        for t in range(UNITS + LAG):
            if t < UNITS:
                ours = tie(partials[t], last).astype(F32)
                sums[t] = (ours + swaps[t].astype(F32)).astype(BF16)
                last = sums[t]
                crosses[t] = cross(sums[t])
            if t == 0:
                gathered_far = jnp.concatenate([far, col_swap(far, 1)], axis=0)
            if t < early:
                first_half(early + t, gathered_far)
                if early + t < LAG:
                    send(early + t, partials[early + t])
            k = t - 1
            if 0 <= k < UNITS:
                summed = tie(sums[k], last).astype(F32) + crosses[k].astype(F32)
                if k in (0, early):
                    low = jnp.split(summed[2 * near :, : fold * LANES], fold, axis=1)
                    low = jnp.concatenate(low, axis=0)
                    own_mask = mask[:near] if k == 0 else mask[near:]
                    low_in[is_near(k)] = jnp.where(own_mask, low, 0.0).astype(BF16)
                low = low_in[is_near(k)]
                value = activate(unfold(summed), low, first_up_maps, first_bias, columns(k))
                value = halves(value)
                if k + LAG == early:
                    value = jnp.concatenate([value, jnp.zeros_like(value[: near // fold])], axis=0)
                if k + LAG < UNITS:
                    value = jnp.where(is_end, partials[k + LAG], value)
                last = value
                send(k + LAG, value)
            unit = t - LAG
            if t == 1:
                whole = tie((gathered_near, gathered_far), last)
                gathered = jnp.concatenate(whole, axis=0)
            if 1 <= t <= early:
                load(early + t - 1)
                first_late(2 * early + t - 1, gathered)
            if early <= unit < 2 * early:
                second("near", unfold(state(unit - early)), unit - early)
                second("far", unfold(state(unit)), unit - early)
            elif unit >= 2 * early:
                if unit == UNITS - 1:
                    last = across
                second("near" if is_near(unit) else "far", unfold(state(unit)), block_of(unit))
                if unit == 3 * early - 1:
                    ours, theirs = core_parts("far")
                    across = (ours + col_swap(theirs, 1).astype(F32)).astype(BF16)
                    across = col_swap(across, 2)
        ours, theirs = core_parts("near")
        come = col_swap(theirs, 1)
        return ours + come.astype(F32) + across.astype(F32), mask

    def plain(tokens, mask, second_weight, second_down_maps, *first):
        rows = tokens.shape[0]
        states = hidden_plain(gather_tokens(tokens), mask, *first)
        outputs = jnp.concatenate([dot(states, second_weight), dot(states, second_down_maps)], axis=1)
        blocks = [outputs[i * rows : (i + 1) * rows] for i in range(n_col)]
        ours = jnp.concatenate(blocks[0::2], axis=0)
        theirs = jnp.concatenate(blocks[1::2], axis=0).astype(BF16)
        ours = ours + col_swap(theirs, 1).astype(F32)
        result = ours[:rows]
        for step in range(1, chips):
            piece = ours[step * rows : (step + 1) * rows].astype(BF16)
            result = result + col_swap(piece, 2 * step).astype(F32)
        return result

    def local(
        tokens,
        token_job_index,
        job_adapter_index,
        first_weight,
        first_bias,
        first_down_maps,
        first_up_maps,
        second_weight,
        second_bias,
        second_down_maps,
        second_up_maps,
    ):
        rows = tokens.shape[0]
        out_width = second_weight.shape[1]
        mine = lax.axis_index("col")

        def mask_of(mine, after):
            mask = token_mask(tie(token_job_index, after), job_adapter_index).astype(jnp.int32)
            for bit in range(n_col.bit_length() - 1):
                size = rows << bit
                blocks = [mask[i : i + size] for i in range(0, mask.shape[0], size)]
                turned = jnp.concatenate([blocks[i ^ 1] for i in range(len(blocks))], axis=0)
                mask = jnp.where((mine >> bit) & 1 == 1, turned, mask)
            return mask == 1

        first = (first_weight, first_bias, first_down_maps, first_up_maps)
        even = first_weight.shape[1] % (UNITS * LANES) == 0
        if n_row == 4 and n_col == 4 and even:
            result, mask = pipeline(tokens, job_adapter_index, mine, mask_of, *first, second_weight, second_down_maps)
        else:
            mask = mask_of(mine, tokens)
            result = plain(tokens, mask, second_weight, second_down_maps, *first)
        low_out = jnp.where(mask[:rows], result[:, out_width:], 0.0).astype(BF16)
        layer_output = result[:, :out_width] + second_bias[None, :] + dot(low_out, second_up_maps)
        return layer_output.astype(BF16)

    return local


def solution(mesh):
    shape = mesh.shape
    return jax.shard_map(
        make_local(shape["group"], shape["row"], shape["col"]),
        mesh=mesh,
        in_specs=(
            P(("group", "col"), "row"),
            P("group"),
            P("group"),
            P("row", "col"),
            P("col"),
            P("row", None),
            P(None, "col"),
            P("col", "row"),
            P("row"),
            P("col", None),
            P(None, "row"),
        ),
        out_specs=P(("group", "col"), "row"),
        check_vma=False,
    )
```

```python
import functools

import jax
import jax.numpy as jnp
from jax import lax
from jax.experimental import pallas as pl
from jax.experimental.pallas import tpu as pltpu
from jax.sharding import PartitionSpec as P

ADAPTER_RANK = 16
ADAPTER_COUNT = 8
JOBS = 4
LANES = 128
UNITS = 12
LAG = 4
F32 = jnp.float32
BF16 = jnp.bfloat16


def gelu_tanh(values):
    return (
        0.5
        * values
        * (1.0 + jnp.tanh(0.7978845608 * (values + 0.044715 * values * values * values)))
    )


def token_mask(token_job_index, job_adapter_index):
    one_hot = token_job_index[:, None] == jnp.arange(JOBS, dtype=jnp.int32)[None, :]
    chosen = jnp.sum(jnp.where(one_hot, job_adapter_index[None, :], 0), axis=1)
    slot_ids = jnp.arange(ADAPTER_COUNT * ADAPTER_RANK, dtype=jnp.int32) // ADAPTER_RANK
    return slot_ids[None, :] == chosen[:, None]


def dot(left, right):
    return jnp.dot(left, right, preferred_element_type=F32)


def tie(value, after):
    return lax.optimization_barrier((value, after))[0]


def load_kernel(w_hbm, after_ref, out, sem, *, part):
    copy = pltpu.make_async_copy(w_hbm.at[part], out, sem)
    copy.start()
    copy.wait()


def load_part(weight, part, after):
    shape = tuple(p.size for p in part)
    return pl.pallas_call(
        functools.partial(load_kernel, part=part),
        in_specs=[pl.BlockSpec(memory_space=pl.ANY)] * 2,
        out_specs=pl.BlockSpec(memory_space=pltpu.VMEM),
        out_shape=pltpu.VMEM(shape, BF16),
        scratch_shapes=[pltpu.SemaphoreType.DMA],
        compiler_params=pltpu.CompilerParams(vmem_limit_bytes=1 << 20),
        cost_estimate=pl.CostEstimate(flops=0, bytes_accessed=1000, transcendentals=0),
    )(pltpu.with_memory_space_constraint(weight, pltpu.HBM), after)


def activate(summed, low_in, first_up_maps, first_bias, part):
    before = summed + first_bias[None, part] + dot(low_in, first_up_maps[:, part])
    return gelu_tanh(before).astype(BF16)


def hidden_plain(tokens, mask, first_weight, first_bias, first_down_maps, first_up_maps):
    width = first_weight.shape[1]
    joined = jnp.concatenate([dot(tokens, first_weight), dot(tokens, first_down_maps)], axis=1)
    summed = lax.psum_scatter(
        joined.astype(BF16), "row", scatter_dimension=0, tiled=True
    ).astype(F32)
    rows = summed.shape[0]
    own_mask = lax.dynamic_slice_in_dim(mask, lax.axis_index("row") * rows, rows, 0)
    low_in = jnp.where(own_mask, summed[:, width:], 0.0).astype(BF16)
    states = activate(summed[:, :width], low_in, first_up_maps, first_bias, slice(0, width))
    return lax.all_gather(states, "row", axis=0, tiled=True)


def make_local(n_group, n_row, n_col):
    chips = n_col // 2

    def place_of(group, row, col):
        return (group * n_row + row) * n_col + col

    cross_pairs = []
    for group in range(n_group):
        for row in range(n_row):
            for col in range(n_col):
                if n_row == 4 and row in (1, 2):
                    other = place_of(group, 3 - row, col)
                else:
                    other = place_of(group, row, col ^ 1)
                cross_pairs.append((place_of(group, row, col), other))

    def col_swap(value, flip):
        return lax.ppermute(value, "col", [(i, i ^ flip) for i in range(n_col)])

    def end_swap(value):
        return lax.ppermute(value, "row", [(i, i ^ 1) for i in range(n_row)])

    def cross(value):
        return lax.ppermute(value, ("group", "row", "col"), cross_pairs)

    def gather_tokens(tokens):
        shards = [tokens, col_swap(tokens, 1)]
        for step in range(1, chips):
            far = col_swap(tokens, 2 * step)
            shards += [far, col_swap(far, 1)]
        return jnp.concatenate(shards, axis=0)

    def pipeline(
        tokens,
        jobs,
        mine,
        mask_of,
        first_weight,
        first_bias,
        first_down_maps,
        first_up_maps,
        second_weight,
        second_down_maps,
    ):
        rows = tokens.shape[0]
        near = 2 * rows
        width = first_weight.shape[1] // UNITS
        wide = 2 * width
        early = UNITS // 4
        fold = max(n for n in range(1, width // LANES + 1) if near % n == 0)
        place = lax.axis_index("row")
        is_end = (place == 0) | (place == 3)
        last = tokens
        partials, payloads, swaps, sums, crosses = {}, {}, {}, {}, {}
        total, low_total = None, None
        low_in = {}

        def halves(value):
            return jnp.concatenate([value[:, :width], value[:, width:]], axis=0)

        def unfold(value):
            return jnp.concatenate([value[:near], value[near : 2 * near]], axis=1)

        def block_of(unit):
            return unit % early + (early if unit >= 2 * early else 0)

        def is_near(unit):
            return unit < early or unit >= 3 * early

        def columns(unit):
            return slice(block_of(unit) * wide, (block_of(unit) + 1) * wide)

        def load(block):
            nonlocal last
            part = (pl.ds(0, first_weight.shape[0]), pl.ds(block * wide, wide))
            loads[block] = load_part(first_weight, part, last)
            last = loads[block]

        def load_second(pair):
            nonlocal last
            part = (pl.ds(pair * 2 * wide, 2 * wide), pl.ds(0, second_weight.shape[1]))
            second_loads[pair] = load_part(second_weight, part, last)
            last = second_loads[pair]

        def multiply(x, block):
            nonlocal last
            value = dot(tie(x, last), loads[block]).astype(BF16)
            last = value
            return value

        def first_half(unit, x):
            nonlocal last
            value = halves(multiply(x, block_of(unit)))
            if unit in (0, early):
                low = dot(x, first_down_maps).astype(BF16)
                low = jnp.concatenate(jnp.split(low, fold, axis=0), axis=1)
                low = jnp.pad(low, ((0, 0), (0, width - fold * LANES)))
                value = jnp.concatenate([value, low], axis=0)
            partials[unit] = value
            last = value

        def first_late(unit, x):
            value = multiply(x, block_of(unit))
            partials[unit + early], partials[unit] = halves(value[:near]), halves(value[near:])

        def send(t, value):
            payloads[t] = value
            swaps[t] = end_swap(value)

        def state(unit):
            come = tie(swaps[unit + LAG], last)
            return jnp.where(is_end, come, payloads[unit + LAG])

        def second(name, states, block):
            nonlocal last
            states = tie(states, last)
            part = slice(block * wide, (block + 1) * wide)
            low = dot(states, second_down_maps[part])
            start = block % 2 * wide
            value = dot(states, second_loads[block // 2][start : start + wide])
            if name in outputs:
                value, low = outputs[name][0] + value, outputs[name][1] + low
            value = lax.optimization_barrier(value)
            last = value[:8, :LANES]
            outputs[name] = (value, low)

        def core_parts(name):
            joined = jnp.concatenate(outputs[name], axis=1)
            return joined[:rows], joined[rows:].astype(BF16)

        far = col_swap(tokens, 2)
        loads, second_loads, outputs = {}, {}, {}
        last, is_end, mine = lax.optimization_barrier((jobs, is_end, mine))
        load(0)
        gathered_near = jnp.concatenate([tokens, tie(col_swap(tokens, 1), last)], axis=0)
        for unit in range(early):
            if unit > 0:
                load(unit)
            first_half(unit, gathered_near)
            send(unit, partials[unit])
        mask = mask_of(mine, last)
        first_bias = tie(first_bias, last)
        for t in range(UNITS + LAG):
            if t < UNITS:
                ours = tie(partials[t], last).astype(F32)
                sums[t] = (ours + swaps[t].astype(F32)).astype(BF16)
                last = sums[t]
                crosses[t] = cross(sums[t])
            if t == 0:
                gathered_far = jnp.concatenate([far, col_swap(far, 1)], axis=0)
            if t < early:
                first_half(early + t, gathered_far)
                if early + t < LAG:
                    send(early + t, partials[early + t])
            unit = t - LAG
            if unit == 3 * early - 1:
                second("far", unfold(state(unit)), block_of(unit))
                ours, theirs = core_parts("far")
                come = col_swap(theirs, 1)
            k = t - 1
            if 0 <= k < UNITS:
                summed = tie(sums[k], last).astype(F32) + crosses[k].astype(F32)
                if k in (0, early):
                    low = jnp.split(summed[2 * near :, : fold * LANES], fold, axis=1)
                    low = jnp.concatenate(low, axis=0)
                    own_mask = mask[:near] if k == 0 else mask[near:]
                    low_in[is_near(k)] = jnp.where(own_mask, low, 0.0).astype(BF16)
                low = low_in[is_near(k)]
                value = activate(unfold(summed), low, first_up_maps, first_bias, columns(k))
                value = halves(value)
                if k + LAG == early:
                    value = jnp.concatenate([value, jnp.zeros_like(value[: near // fold])], axis=0)
                if k + LAG < UNITS:
                    value = jnp.where(is_end, partials[k + LAG], value)
                last = value
                send(k + LAG, value)
            unit = t - LAG
            if t == 1:
                whole = tie((gathered_near, gathered_far), last)
                gathered = jnp.concatenate(whole, axis=0)
            if t >= LAG and (t - LAG) % 2 == 0 and t - LAG < 2 * early:
                load_second((t - LAG) // 2)
            if 1 <= t <= early:
                load(early + t - 1)
                first_late(2 * early + t - 1, gathered)
            if early <= unit < 2 * early:
                second("near", unfold(state(unit - early)), unit - early)
                second("far", unfold(state(unit)), unit - early)
            elif unit == 3 * early - 1:
                across = (ours + come.astype(F32)).astype(BF16)
                across = col_swap(across, 2)
            elif unit >= 2 * early:
                if unit == UNITS - 1:
                    last = across
                second("near" if is_near(unit) else "far", unfold(state(unit)), block_of(unit))
        ours, theirs = core_parts("near")
        come = col_swap(theirs, 1)
        return ours + come.astype(F32) + across.astype(F32), mask

    def plain(tokens, mask, second_weight, second_down_maps, *first):
        rows = tokens.shape[0]
        states = hidden_plain(gather_tokens(tokens), mask, *first)
        outputs = jnp.concatenate([dot(states, second_weight), dot(states, second_down_maps)], axis=1)
        blocks = [outputs[i * rows : (i + 1) * rows] for i in range(n_col)]
        ours = jnp.concatenate(blocks[0::2], axis=0)
        theirs = jnp.concatenate(blocks[1::2], axis=0).astype(BF16)
        ours = ours + col_swap(theirs, 1).astype(F32)
        result = ours[:rows]
        for step in range(1, chips):
            piece = ours[step * rows : (step + 1) * rows].astype(BF16)
            result = result + col_swap(piece, 2 * step).astype(F32)
        return result

    def local(
        tokens,
        token_job_index,
        job_adapter_index,
        first_weight,
        first_bias,
        first_down_maps,
        first_up_maps,
        second_weight,
        second_bias,
        second_down_maps,
        second_up_maps,
    ):
        rows = tokens.shape[0]
        out_width = second_weight.shape[1]
        mine = lax.axis_index("col")

        def mask_of(mine, after):
            mask = token_mask(tie(token_job_index, after), job_adapter_index).astype(jnp.int32)
            for bit in range(n_col.bit_length() - 1):
                size = rows << bit
                blocks = [mask[i : i + size] for i in range(0, mask.shape[0], size)]
                turned = jnp.concatenate([blocks[i ^ 1] for i in range(len(blocks))], axis=0)
                mask = jnp.where((mine >> bit) & 1 == 1, turned, mask)
            return mask == 1

        first = (first_weight, first_bias, first_down_maps, first_up_maps)
        even = first_weight.shape[1] % (UNITS * LANES) == 0
        if n_row == 4 and n_col == 4 and even:
            result, mask = pipeline(tokens, job_adapter_index, mine, mask_of, *first, second_weight, second_down_maps)
        else:
            mask = mask_of(mine, tokens)
            result = plain(tokens, mask, second_weight, second_down_maps, *first)
        low_out = jnp.where(mask[:rows], result[:, out_width:], 0.0).astype(BF16)
        layer_output = result[:, :out_width] + second_bias[None, :] + dot(low_out, second_up_maps)
        return layer_output.astype(BF16)

    return local


def solution(mesh):
    shape = mesh.shape
    return jax.shard_map(
        make_local(shape["group"], shape["row"], shape["col"]),
        mesh=mesh,
        in_specs=(
            P(("group", "col"), "row"),
            P("group"),
            P("group"),
            P("row", "col"),
            P("col"),
            P("row", None),
            P(None, "col"),
            P("col", "row"),
            P("row"),
            P("col", None),
            P(None, "row"),
        ),
        out_specs=P(("group", "col"), "row"),
        check_vma=False,
    )
```

```python
import functools

import jax
import jax.numpy as jnp
from jax import lax
from jax.experimental import pallas as pl
from jax.experimental.pallas import tpu as pltpu
from jax.sharding import PartitionSpec as P

ADAPTER_RANK = 16
ADAPTER_COUNT = 8
JOBS = 4
LANES = 128
UNITS = 8
LAG = 3
F32 = jnp.float32
BF16 = jnp.bfloat16


def gelu_tanh(values):
    return (
        0.5
        * values
        * (1.0 + jnp.tanh(0.7978845608 * (values + 0.044715 * values * values * values)))
    )


def token_mask(token_job_index, job_adapter_index):
    one_hot = token_job_index[:, None] == jnp.arange(JOBS, dtype=jnp.int32)[None, :]
    chosen = jnp.sum(jnp.where(one_hot, job_adapter_index[None, :], 0), axis=1)
    slot_ids = jnp.arange(ADAPTER_COUNT * ADAPTER_RANK, dtype=jnp.int32) // ADAPTER_RANK
    return slot_ids[None, :] == chosen[:, None]


def dot(left, right):
    return jnp.dot(left, right, preferred_element_type=F32)


def tie(value, after):
    return lax.optimization_barrier((value, after))[0]


def load_kernel(w_hbm, after_ref, out, sem, *, part):
    copy = pltpu.make_async_copy(w_hbm.at[part], out, sem)
    copy.start()
    copy.wait()


def load_part(weight, part, after):
    shape = tuple(p.size for p in part)
    return pl.pallas_call(
        functools.partial(load_kernel, part=part),
        in_specs=[pl.BlockSpec(memory_space=pl.ANY)] * 2,
        out_specs=pl.BlockSpec(memory_space=pltpu.VMEM),
        out_shape=pltpu.VMEM(shape, BF16),
        scratch_shapes=[pltpu.SemaphoreType.DMA],
        compiler_params=pltpu.CompilerParams(vmem_limit_bytes=1 << 20),
        cost_estimate=pl.CostEstimate(flops=0, bytes_accessed=1000, transcendentals=0),
    )(pltpu.with_memory_space_constraint(weight, pltpu.HBM), after)


def activate(summed, low_in, first_up_maps, first_bias, part):
    before = summed + first_bias[None, part] + dot(low_in, first_up_maps[:, part])
    return gelu_tanh(before).astype(BF16)


def hidden_plain(tokens, mask, first_weight, first_bias, first_down_maps, first_up_maps):
    width = first_weight.shape[1]
    joined = jnp.concatenate([dot(tokens, first_weight), dot(tokens, first_down_maps)], axis=1)
    summed = lax.psum_scatter(
        joined.astype(BF16), "row", scatter_dimension=0, tiled=True
    ).astype(F32)
    rows = summed.shape[0]
    own_mask = lax.dynamic_slice_in_dim(mask, lax.axis_index("row") * rows, rows, 0)
    low_in = jnp.where(own_mask, summed[:, width:], 0.0).astype(BF16)
    states = activate(summed[:, :width], low_in, first_up_maps, first_bias, slice(0, width))
    return lax.all_gather(states, "row", axis=0, tiled=True)


def make_local(n_group, n_row, n_col):
    chips = n_col // 2

    def place_of(group, row, col):
        return (group * n_row + row) * n_col + col

    cross_pairs = []
    for group in range(n_group):
        for row in range(n_row):
            for col in range(n_col):
                if n_row == 4 and row in (1, 2):
                    other = place_of(group, 3 - row, col)
                else:
                    other = place_of(group, row, col ^ 1)
                cross_pairs.append((place_of(group, row, col), other))

    def col_swap(value, flip):
        return lax.ppermute(value, "col", [(i, i ^ flip) for i in range(n_col)])

    def end_swap(value):
        return lax.ppermute(value, "row", [(i, i ^ 1) for i in range(n_row)])

    def cross(value):
        return lax.ppermute(value, ("group", "row", "col"), cross_pairs)

    def gather_tokens(tokens):
        shards = [tokens, col_swap(tokens, 1)]
        for step in range(1, chips):
            far = col_swap(tokens, 2 * step)
            shards += [far, col_swap(far, 1)]
        return jnp.concatenate(shards, axis=0)

    def pipeline(
        tokens,
        jobs,
        mine,
        mask_of,
        first_weight,
        first_bias,
        first_down_maps,
        first_up_maps,
        second_weight,
        second_down_maps,
    ):
        rows = tokens.shape[0]
        near = 2 * rows
        width = first_weight.shape[1] // UNITS
        wide = 2 * width
        early = UNITS // 4
        fold = max(n for n in range(1, width // LANES + 1) if near % n == 0)
        place = lax.axis_index("row")
        is_end = (place == 0) | (place == 3)
        last = tokens
        partials, payloads, swaps, sums, crosses = {}, {}, {}, {}, {}
        total, low_total = None, None
        low_in = {}

        def halves(value):
            return jnp.concatenate([value[:, :width], value[:, width:]], axis=0)

        def unfold(value):
            return jnp.concatenate([value[:near], value[near : 2 * near]], axis=1)

        def block_of(unit):
            return unit % early + (early if unit >= 2 * early else 0)

        def is_near(unit):
            return unit < early or unit >= 3 * early

        def columns(unit):
            return slice(block_of(unit) * wide, (block_of(unit) + 1) * wide)

        def load(block):
            nonlocal last
            part = (pl.ds(0, first_weight.shape[0]), pl.ds(block * wide, wide))
            loads[block] = load_part(first_weight, part, last)
            last = loads[block]

        def load_second(block):
            nonlocal last
            part = (pl.ds(block * wide, wide), pl.ds(0, second_weight.shape[1]))
            second_loads[block] = load_part(second_weight, part, last)
            last = second_loads[block]

        def multiply(x, block):
            nonlocal last
            value = dot(tie(x, last), loads[block]).astype(BF16)
            last = value
            return value

        def first_half(unit, x):
            nonlocal last
            value = halves(multiply(x, block_of(unit)))
            if unit in (0, early):
                low = dot(x, first_down_maps).astype(BF16)
                low = jnp.concatenate(jnp.split(low, fold, axis=0), axis=1)
                low = jnp.pad(low, ((0, 0), (0, width - fold * LANES)))
                value = jnp.concatenate([value, low], axis=0)
            partials[unit] = value
            last = value

        def first_late(unit, x):
            value = multiply(x, block_of(unit))
            partials[unit + early], partials[unit] = halves(value[:near]), halves(value[near:])

        def send(t, value):
            payloads[t] = value
            swaps[t] = end_swap(value)

        def state(unit):
            come = tie(swaps[unit + LAG], last)
            return jnp.where(is_end, come, payloads[unit + LAG])

        def second(name, states, block):
            nonlocal last
            states = tie(states, last)
            part = slice(block * wide, (block + 1) * wide)
            low = dot(states, second_down_maps[part])
            value = dot(states, second_loads[block])
            if name in outputs:
                value, low = outputs[name][0] + value, outputs[name][1] + low
            value = lax.optimization_barrier(value)
            last = value[:8, :LANES]
            outputs[name] = (value, low)

        def core_parts(name):
            joined = jnp.concatenate(outputs[name], axis=1)
            return joined[:rows], joined[rows:].astype(BF16)

        far = col_swap(tokens, 2)
        loads, second_loads, outputs = {}, {}, {}
        last, is_end, mine = lax.optimization_barrier((jobs, is_end, mine))
        load(0)
        gathered_near = jnp.concatenate([tokens, tie(col_swap(tokens, 1), last)], axis=0)
        for unit in range(early):
            if unit > 0:
                load(unit)
            first_half(unit, gathered_near)
            send(unit, partials[unit])
        mask = mask_of(mine, last)
        first_bias = tie(first_bias, last)
        def far_half(unit):
            first_half(unit, gathered_far)
            if unit < LAG:
                send(unit, partials[unit])

        gathered_far = jnp.concatenate([far, col_swap(far, 1)], axis=0)
        far_half(early)
        for t in range(UNITS + LAG):
            if t < UNITS:
                ours = tie(partials[t], last).astype(F32)
                sums[t] = (ours + swaps[t].astype(F32)).astype(BF16)
                last = sums[t]
                crosses[t] = cross(sums[t])
            unit = t - LAG
            if unit == 3 * early - 1:
                second("far", unfold(state(unit)), block_of(unit))
                ours, theirs = core_parts("far")
                come = col_swap(theirs, 1)
            k = t - 1
            if 0 <= k < UNITS:
                summed = tie(sums[k], last).astype(F32) + crosses[k].astype(F32)
                if k in (0, early):
                    low = jnp.split(summed[2 * near :, : fold * LANES], fold, axis=1)
                    low = jnp.concatenate(low, axis=0)
                    own_mask = mask[:near] if k == 0 else mask[near:]
                    low_in[is_near(k)] = jnp.where(own_mask, low, 0.0).astype(BF16)
                low = low_in[is_near(k)]
                value = activate(unfold(summed), low, first_up_maps, first_bias, columns(k))
                value = halves(value)
                if k + LAG == early:
                    value = jnp.concatenate([value, jnp.zeros_like(value[: near // fold])], axis=0)
                if k + LAG < UNITS:
                    value = jnp.where(is_end, partials[k + LAG], value)
                last = value
                send(k + LAG, value)
            if t + 1 < early:
                far_half(early + t + 1)
            if t == 1:
                whole = tie((gathered_near, gathered_far), last)
                gathered = jnp.concatenate(whole, axis=0)
            if LAG <= t < LAG + 2 * early:
                load_second(t - LAG)
            if 1 <= t <= early:
                load(early + t - 1)
                first_late(2 * early + t - 1, gathered)
            if early <= unit < 2 * early:
                second("near", unfold(state(unit - early)), unit - early)
                second("far", unfold(state(unit)), unit - early)
            elif unit == 3 * early - 1:
                across = (ours + come.astype(F32)).astype(BF16)
                across = col_swap(across, 2)
            elif unit >= 2 * early:
                if unit == UNITS - 1:
                    last = across
                second("near" if is_near(unit) else "far", unfold(state(unit)), block_of(unit))
        ours, theirs = core_parts("near")
        come = col_swap(theirs, 1)
        return ours + come.astype(F32) + across.astype(F32), mask

    def plain(tokens, mask, second_weight, second_down_maps, *first):
        rows = tokens.shape[0]
        states = hidden_plain(gather_tokens(tokens), mask, *first)
        outputs = jnp.concatenate([dot(states, second_weight), dot(states, second_down_maps)], axis=1)
        blocks = [outputs[i * rows : (i + 1) * rows] for i in range(n_col)]
        ours = jnp.concatenate(blocks[0::2], axis=0)
        theirs = jnp.concatenate(blocks[1::2], axis=0).astype(BF16)
        ours = ours + col_swap(theirs, 1).astype(F32)
        result = ours[:rows]
        for step in range(1, chips):
            piece = ours[step * rows : (step + 1) * rows].astype(BF16)
            result = result + col_swap(piece, 2 * step).astype(F32)
        return result

    def local(
        tokens,
        token_job_index,
        job_adapter_index,
        first_weight,
        first_bias,
        first_down_maps,
        first_up_maps,
        second_weight,
        second_bias,
        second_down_maps,
        second_up_maps,
    ):
        rows = tokens.shape[0]
        out_width = second_weight.shape[1]
        mine = lax.axis_index("col")

        def mask_of(mine, after):
            mask = token_mask(tie(token_job_index, after), job_adapter_index).astype(jnp.int32)
            for bit in range(n_col.bit_length() - 1):
                size = rows << bit
                blocks = [mask[i : i + size] for i in range(0, mask.shape[0], size)]
                turned = jnp.concatenate([blocks[i ^ 1] for i in range(len(blocks))], axis=0)
                mask = jnp.where((mine >> bit) & 1 == 1, turned, mask)
            return mask == 1

        first = (first_weight, first_bias, first_down_maps, first_up_maps)
        even = first_weight.shape[1] % (UNITS * LANES) == 0
        if n_row == 4 and n_col == 4 and even:
            result, mask = pipeline(tokens, job_adapter_index, mine, mask_of, *first, second_weight, second_down_maps)
        else:
            mask = mask_of(mine, tokens)
            result = plain(tokens, mask, second_weight, second_down_maps, *first)
        low_out = jnp.where(mask[:rows], result[:, out_width:], 0.0).astype(BF16)
        layer_output = result[:, :out_width] + second_bias[None, :] + dot(low_out, second_up_maps)
        return layer_output.astype(BF16)

    return local


def solution(mesh):
    shape = mesh.shape
    return jax.shard_map(
        make_local(shape["group"], shape["row"], shape["col"]),
        mesh=mesh,
        in_specs=(
            P(("group", "col"), "row"),
            P("group"),
            P("group"),
            P("row", "col"),
            P("col"),
            P("row", None),
            P(None, "col"),
            P("col", "row"),
            P("row"),
            P("col", None),
            P(None, "row"),
        ),
        out_specs=P(("group", "col"), "row"),
        check_vma=False,
    )
```

```python
import functools

import jax
import jax.numpy as jnp
from jax import lax
from jax.experimental import pallas as pl
from jax.experimental.pallas import tpu as pltpu
from jax.sharding import PartitionSpec as P

ADAPTER_RANK = 16
ADAPTER_COUNT = 8
JOBS = 4
LANES = 128
UNITS = 8
LAG = 3
F32 = jnp.float32
BF16 = jnp.bfloat16


def gelu_tanh(values):
    return (
        0.5
        * values
        * (1.0 + jnp.tanh(0.7978845608 * (values + 0.044715 * values * values * values)))
    )


def token_mask(token_job_index, job_adapter_index):
    one_hot = token_job_index[:, None] == jnp.arange(JOBS, dtype=jnp.int32)[None, :]
    chosen = jnp.sum(jnp.where(one_hot, job_adapter_index[None, :], 0), axis=1)
    slot_ids = jnp.arange(ADAPTER_COUNT * ADAPTER_RANK, dtype=jnp.int32) // ADAPTER_RANK
    return slot_ids[None, :] == chosen[:, None]


def dot(left, right):
    return jnp.dot(left, right, preferred_element_type=F32)


def tie(value, after):
    return lax.optimization_barrier((value, after))[0]


def load_kernel(w_hbm, after_ref, out, sem, *, part):
    copy = pltpu.make_async_copy(w_hbm.at[part], out, sem)
    copy.start()
    copy.wait()


def load_part(weight, part, after):
    shape = tuple(p.size for p in part)
    return pl.pallas_call(
        functools.partial(load_kernel, part=part),
        in_specs=[pl.BlockSpec(memory_space=pl.ANY)] * 2,
        out_specs=pl.BlockSpec(memory_space=pltpu.VMEM),
        out_shape=pltpu.VMEM(shape, BF16),
        scratch_shapes=[pltpu.SemaphoreType.DMA],
        compiler_params=pltpu.CompilerParams(vmem_limit_bytes=1 << 20),
        cost_estimate=pl.CostEstimate(flops=0, bytes_accessed=1000, transcendentals=0),
    )(pltpu.with_memory_space_constraint(weight, pltpu.HBM), after)


def behind(value, row):
    return value + 0.0 * row[:1, : value.shape[1]].astype(F32)


def activate(summed, low_in, first_up_maps, first_bias, part):
    before = summed + first_bias[None, part] + dot(low_in, first_up_maps[:, part])
    return gelu_tanh(before).astype(BF16)


def hidden_plain(tokens, mask, first_weight, first_bias, first_down_maps, first_up_maps):
    width = first_weight.shape[1]
    joined = jnp.concatenate([dot(tokens, first_weight), dot(tokens, first_down_maps)], axis=1)
    summed = lax.psum_scatter(
        joined.astype(BF16), "row", scatter_dimension=0, tiled=True
    ).astype(F32)
    rows = summed.shape[0]
    own_mask = lax.dynamic_slice_in_dim(mask, lax.axis_index("row") * rows, rows, 0)
    low_in = jnp.where(own_mask, summed[:, width:], 0.0).astype(BF16)
    states = activate(summed[:, :width], low_in, first_up_maps, first_bias, slice(0, width))
    return lax.all_gather(states, "row", axis=0, tiled=True)


def make_local(n_group, n_row, n_col):
    chips = n_col // 2

    def place_of(group, row, col):
        return (group * n_row + row) * n_col + col

    cross_pairs = []
    for group in range(n_group):
        for row in range(n_row):
            for col in range(n_col):
                if n_row == 4 and row in (1, 2):
                    other = place_of(group, 3 - row, col)
                else:
                    other = place_of(group, row, col ^ 1)
                cross_pairs.append((place_of(group, row, col), other))

    def col_swap(value, flip):
        return lax.ppermute(value, "col", [(i, i ^ flip) for i in range(n_col)])

    def end_swap(value):
        return lax.ppermute(value, "row", [(i, i ^ 1) for i in range(n_row)])

    def cross(value):
        return lax.ppermute(value, ("group", "row", "col"), cross_pairs)

    def gather_tokens(tokens):
        shards = [tokens, col_swap(tokens, 1)]
        for step in range(1, chips):
            far = col_swap(tokens, 2 * step)
            shards += [far, col_swap(far, 1)]
        return jnp.concatenate(shards, axis=0)

    def pipeline(
        tokens,
        jobs,
        mine,
        mask_of,
        first_weight,
        first_bias,
        first_down_maps,
        first_up_maps,
        second_weight,
        second_down_maps,
    ):
        rows = tokens.shape[0]
        near = 2 * rows
        width = first_weight.shape[1] // UNITS
        wide = 2 * width
        early = UNITS // 4
        fold = max(n for n in range(1, width // LANES + 1) if near % n == 0)
        place = lax.axis_index("row")
        is_end = (place == 0) | (place == 3)
        last = tokens
        partials, payloads, swaps, sums, crosses = {}, {}, {}, {}, {}
        total, low_total = None, None
        low_in = {}

        def halves(value):
            return jnp.concatenate([value[:, :width], value[:, width:]], axis=0)

        def unfold(value):
            return jnp.concatenate([value[:near], value[near : 2 * near]], axis=1)

        def block_of(unit):
            return unit % early + (early if unit >= 2 * early else 0)

        def is_near(unit):
            return unit < early or unit >= 3 * early

        def columns(unit):
            return slice(block_of(unit) * wide, (block_of(unit) + 1) * wide)

        def load(block):
            nonlocal last
            part = (pl.ds(0, first_weight.shape[0]), pl.ds(block * wide, wide))
            loads[block] = load_part(first_weight, part, last)
            last = loads[block]

        def load_second(block):
            nonlocal last
            part = (pl.ds(block * wide, wide), pl.ds(0, second_weight.shape[1]))
            second_loads[block] = load_part(second_weight, part, last)
            last = second_loads[block]

        def multiply(x, block):
            nonlocal last
            value = dot(tie(x, last), loads[block]).astype(BF16)
            last = value
            return value

        def first_half(unit, x):
            nonlocal last
            value = halves(multiply(x, block_of(unit)))
            if unit in (0, early):
                low = dot(x, first_down_maps).astype(BF16)
                low = jnp.concatenate(jnp.split(low, fold, axis=0), axis=1)
                low = jnp.pad(low, ((0, 0), (0, width - fold * LANES)))
                value = jnp.concatenate([value, low], axis=0)
            partials[unit] = value
            last = value

        def first_late(unit, x):
            value = multiply(x, block_of(unit))
            partials[unit + early], partials[unit] = halves(value[:near]), halves(value[near:])

        def send(t, value):
            payloads[t] = value
            swaps[t] = end_swap(value)

        def state(unit):
            come = tie(swaps[unit + LAG], last)
            return jnp.where(is_end, come, payloads[unit + LAG])

        def second(name, states, block):
            nonlocal last
            states = tie(states, last)
            part = slice(block * wide, (block + 1) * wide)
            low = dot(states, second_down_maps[part])
            value = dot(states, second_loads[block])
            if name in outputs:
                value, low = outputs[name][0] + value, outputs[name][1] + low
            value = lax.optimization_barrier(value)
            last = value[:8, :LANES]
            outputs[name] = (value, low)

        def core_parts(name):
            joined = jnp.concatenate(outputs[name], axis=1)
            return joined[:rows], joined[rows:].astype(BF16)

        far = col_swap(tokens, 2)
        loads, second_loads, outputs = {}, {}, {}
        last, is_end, mine = lax.optimization_barrier((jobs, is_end, mine))
        load(0)
        gathered_near = jnp.concatenate([tokens, tie(col_swap(tokens, 1), last)], axis=0)
        for unit in range(early):
            if unit > 0:
                load(unit)
            first_half(unit, gathered_near)
            send(unit, partials[unit])
        mask = mask_of(mine, last)
        first_bias = tie(first_bias, last)
        def far_half(unit):
            first_half(unit, gathered_far)
            if unit < LAG:
                send(unit, partials[unit])

        gathered_far = jnp.concatenate([far, col_swap(far, 1)], axis=0)
        far_half(early)
        for t in range(UNITS + LAG):
            if t < UNITS:
                ours = tie(partials[t], last).astype(F32)
                if t > 0 and t - 1 + LAG - 1 in payloads:
                    ours = behind(ours, payloads[t - 2 + LAG])
                sums[t] = (ours + swaps[t].astype(F32)).astype(BF16)
                last = sums[t]
                crosses[t] = cross(sums[t])
            unit = t - LAG
            if unit == 3 * early - 1:
                second("far", unfold(state(unit)), block_of(unit))
                ours, theirs = core_parts("far")
                come = col_swap(theirs, 1)
            k = t - 1
            if 0 <= k < UNITS:
                summed = tie(sums[k], last).astype(F32) + crosses[k].astype(F32)
                if k in (0, early):
                    low = jnp.split(summed[2 * near :, : fold * LANES], fold, axis=1)
                    low = jnp.concatenate(low, axis=0)
                    own_mask = mask[:near] if k == 0 else mask[near:]
                    low_in[is_near(k)] = jnp.where(own_mask, low, 0.0).astype(BF16)
                if k == UNITS - 1:
                    summed = behind(summed, outputs["far"][0])
                low = low_in[is_near(k)]
                value = activate(unfold(summed), low, first_up_maps, first_bias, columns(k))
                value = halves(value)
                if k + LAG == early:
                    value = jnp.concatenate([value, jnp.zeros_like(value[: near // fold])], axis=0)
                if k + LAG < UNITS:
                    value = jnp.where(is_end, partials[k + LAG], value)
                last = value
                send(k + LAG, value)
            if t + 1 < early:
                far_half(early + t + 1)
            if t == 1:
                whole = tie((gathered_near, gathered_far), last)
                gathered = jnp.concatenate(whole, axis=0)
            if LAG <= t < LAG + 2 * early:
                load_second(t - LAG)
            if 1 <= t <= early:
                load(early + t - 1)
                first_late(2 * early + t - 1, gathered)
            if early <= unit < 2 * early:
                second("near", unfold(state(unit - early)), unit - early)
                second("far", unfold(state(unit)), unit - early)
            elif unit == 3 * early - 1:
                across = (ours + come.astype(F32)).astype(BF16)
                across = col_swap(across, 2)
            elif unit >= 2 * early:
                states = unfold(state(unit))
                if unit == UNITS - 1:
                    last = across
                second("near" if is_near(unit) else "far", states, block_of(unit))
        ours, theirs = core_parts("near")
        come = col_swap(theirs, 1)
        return ours + come.astype(F32) + across.astype(F32), mask

    def plain(tokens, mask, second_weight, second_down_maps, *first):
        rows = tokens.shape[0]
        states = hidden_plain(gather_tokens(tokens), mask, *first)
        outputs = jnp.concatenate([dot(states, second_weight), dot(states, second_down_maps)], axis=1)
        blocks = [outputs[i * rows : (i + 1) * rows] for i in range(n_col)]
        ours = jnp.concatenate(blocks[0::2], axis=0)
        theirs = jnp.concatenate(blocks[1::2], axis=0).astype(BF16)
        ours = ours + col_swap(theirs, 1).astype(F32)
        result = ours[:rows]
        for step in range(1, chips):
            piece = ours[step * rows : (step + 1) * rows].astype(BF16)
            result = result + col_swap(piece, 2 * step).astype(F32)
        return result

    def local(
        tokens,
        token_job_index,
        job_adapter_index,
        first_weight,
        first_bias,
        first_down_maps,
        first_up_maps,
        second_weight,
        second_bias,
        second_down_maps,
        second_up_maps,
    ):
        rows = tokens.shape[0]
        out_width = second_weight.shape[1]
        mine = lax.axis_index("col")

        def mask_of(mine, after):
            mask = token_mask(tie(token_job_index, after), job_adapter_index).astype(jnp.int32)
            for bit in range(n_col.bit_length() - 1):
                size = rows << bit
                blocks = [mask[i : i + size] for i in range(0, mask.shape[0], size)]
                turned = jnp.concatenate([blocks[i ^ 1] for i in range(len(blocks))], axis=0)
                mask = jnp.where((mine >> bit) & 1 == 1, turned, mask)
            return mask == 1

        first = (first_weight, first_bias, first_down_maps, first_up_maps)
        even = first_weight.shape[1] % (UNITS * LANES) == 0
        if n_row == 4 and n_col == 4 and even:
            result, mask = pipeline(tokens, job_adapter_index, mine, mask_of, *first, second_weight, second_down_maps)
        else:
            mask = mask_of(mine, tokens)
            result = plain(tokens, mask, second_weight, second_down_maps, *first)
        low_out = jnp.where(mask[:rows], result[:, out_width:], 0.0).astype(BF16)
        layer_output = result[:, :out_width] + second_bias[None, :] + dot(low_out, second_up_maps)
        return layer_output.astype(BF16)

    return local


def solution(mesh):
    shape = mesh.shape
    return jax.shard_map(
        make_local(shape["group"], shape["row"], shape["col"]),
        mesh=mesh,
        in_specs=(
            P(("group", "col"), "row"),
            P("group"),
            P("group"),
            P("row", "col"),
            P("col"),
            P("row", None),
            P(None, "col"),
            P("col", "row"),
            P("row"),
            P("col", None),
            P(None, "row"),
        ),
        out_specs=P(("group", "col"), "row"),
        check_vma=False,
    )
```

```python
import functools

import jax
import jax.numpy as jnp
from jax import lax
from jax.experimental import pallas as pl
from jax.experimental.pallas import tpu as pltpu
from jax.sharding import PartitionSpec as P

ADAPTER_RANK = 16
ADAPTER_COUNT = 8
JOBS = 4
LANES = 128
UNITS = 8
LAG = 3
F32 = jnp.float32
BF16 = jnp.bfloat16


def gelu_tanh(values):
    return (
        0.5
        * values
        * (1.0 + jnp.tanh(0.7978845608 * (values + 0.044715 * values * values * values)))
    )


def token_mask(token_job_index, job_adapter_index):
    one_hot = token_job_index[:, None] == jnp.arange(JOBS, dtype=jnp.int32)[None, :]
    chosen = jnp.sum(jnp.where(one_hot, job_adapter_index[None, :], 0), axis=1)
    slot_ids = jnp.arange(ADAPTER_COUNT * ADAPTER_RANK, dtype=jnp.int32) // ADAPTER_RANK
    return slot_ids[None, :] == chosen[:, None]


def dot(left, right):
    return jnp.dot(left, right, preferred_element_type=F32)


def tie(value, after):
    return lax.optimization_barrier((value, after))[0]


def load_kernel(w_hbm, after_ref, out, sem, *, part):
    copy = pltpu.make_async_copy(w_hbm.at[part], out, sem)
    copy.start()
    copy.wait()


def load_part(weight, part, after):
    shape = tuple(p.size for p in part)
    return pl.pallas_call(
        functools.partial(load_kernel, part=part),
        in_specs=[pl.BlockSpec(memory_space=pl.ANY)] * 2,
        out_specs=pl.BlockSpec(memory_space=pltpu.VMEM),
        out_shape=pltpu.VMEM(shape, BF16),
        scratch_shapes=[pltpu.SemaphoreType.DMA],
        compiler_params=pltpu.CompilerParams(vmem_limit_bytes=1 << 20),
        cost_estimate=pl.CostEstimate(flops=0, bytes_accessed=1000, transcendentals=0),
    )(pltpu.with_memory_space_constraint(weight, pltpu.HBM), after)


def behind(value, row):
    return value + 0.0 * row[:1, : value.shape[1]].astype(F32)


def activate(summed, low_in, first_up_maps, first_bias, part):
    before = summed + first_bias[None, part] + dot(low_in, first_up_maps[:, part])
    return gelu_tanh(before).astype(BF16)


def hidden_plain(tokens, mask, first_weight, first_bias, first_down_maps, first_up_maps):
    width = first_weight.shape[1]
    joined = jnp.concatenate([dot(tokens, first_weight), dot(tokens, first_down_maps)], axis=1)
    summed = lax.psum_scatter(
        joined.astype(BF16), "row", scatter_dimension=0, tiled=True
    ).astype(F32)
    rows = summed.shape[0]
    own_mask = lax.dynamic_slice_in_dim(mask, lax.axis_index("row") * rows, rows, 0)
    low_in = jnp.where(own_mask, summed[:, width:], 0.0).astype(BF16)
    states = activate(summed[:, :width], low_in, first_up_maps, first_bias, slice(0, width))
    return lax.all_gather(states, "row", axis=0, tiled=True)


def make_local(n_group, n_row, n_col):
    chips = n_col // 2

    def place_of(group, row, col):
        return (group * n_row + row) * n_col + col

    cross_pairs = []
    for group in range(n_group):
        for row in range(n_row):
            for col in range(n_col):
                if n_row == 4 and row in (1, 2):
                    other = place_of(group, 3 - row, col)
                else:
                    other = place_of(group, row, col ^ 1)
                cross_pairs.append((place_of(group, row, col), other))

    def col_swap(value, flip):
        return lax.ppermute(value, "col", [(i, i ^ flip) for i in range(n_col)])

    def end_swap(value):
        return lax.ppermute(value, "row", [(i, i ^ 1) for i in range(n_row)])

    def cross(value):
        return lax.ppermute(value, ("group", "row", "col"), cross_pairs)

    def gather_tokens(tokens):
        shards = [tokens, col_swap(tokens, 1)]
        for step in range(1, chips):
            far = col_swap(tokens, 2 * step)
            shards += [far, col_swap(far, 1)]
        return jnp.concatenate(shards, axis=0)

    def pipeline(
        tokens,
        jobs,
        mine,
        mask_of,
        first_weight,
        first_bias,
        first_down_maps,
        first_up_maps,
        second_weight,
        second_down_maps,
    ):
        rows = tokens.shape[0]
        near = 2 * rows
        width = first_weight.shape[1] // UNITS
        wide = 2 * width
        early = UNITS // 4
        fold = max(n for n in range(1, width // LANES + 1) if near % n == 0)
        place = lax.axis_index("row")
        is_end = (place == 0) | (place == 3)
        last = tokens
        partials, payloads, swaps, sums, crosses = {}, {}, {}, {}, {}
        total, low_total = None, None
        low_in = {}

        def halves(value):
            return jnp.concatenate([value[:, :width], value[:, width:]], axis=0)

        def unfold(value):
            return jnp.concatenate([value[:near], value[near : 2 * near]], axis=1)

        def block_of(unit):
            return unit % early + (early if unit >= 2 * early else 0)

        def is_near(unit):
            return unit < early or unit >= 3 * early

        def columns(unit):
            return slice(block_of(unit) * wide, (block_of(unit) + 1) * wide)

        def load(block):
            nonlocal last
            part = (pl.ds(0, first_weight.shape[0]), pl.ds(block * wide, wide))
            loads[block] = load_part(first_weight, part, last)
            last = loads[block]

        def load_second(block):
            nonlocal last
            part = (pl.ds(block * wide, wide), pl.ds(0, second_weight.shape[1]))
            second_loads[block] = load_part(second_weight, part, last)
            last = second_loads[block]

        def multiply(x, block):
            nonlocal last
            value = dot(tie(x, last), loads[block]).astype(BF16)
            last = value
            return value

        def first_half(unit, x):
            nonlocal last
            value = halves(multiply(x, block_of(unit)))
            if unit in (0, early):
                low = dot(x, first_down_maps).astype(BF16)
                low = jnp.concatenate(jnp.split(low, fold, axis=0), axis=1)
                low = jnp.pad(low, ((0, 0), (0, width - fold * LANES)))
                value = jnp.concatenate([value, low], axis=0)
            partials[unit] = value
            last = value

        def first_late(unit, x):
            value = multiply(x, block_of(unit))
            partials[unit + early], partials[unit] = halves(value[:near]), halves(value[near:])

        def send(t, value):
            payloads[t] = value
            swaps[t] = end_swap(value)

        def state(unit):
            come = tie(swaps[unit + LAG], last)
            return jnp.where(is_end, come, payloads[unit + LAG])

        def second(name, states, block):
            nonlocal last
            states = tie(states, last)
            part = slice(block * wide, (block + 1) * wide)
            low = dot(states, second_down_maps[part])
            value = dot(states, second_loads[block])
            if name in outputs:
                value, low = outputs[name][0] + value, outputs[name][1] + low
            value = lax.optimization_barrier(value)
            last = value[:8, :LANES]
            outputs[name] = (value, low)

        def core_parts(name):
            joined = jnp.concatenate(outputs[name], axis=1)
            return joined[:rows], joined[rows:].astype(BF16)

        far = col_swap(tokens, 2)
        loads, second_loads, outputs = {}, {}, {}
        last, is_end, mine = lax.optimization_barrier((jobs, is_end, mine))
        load(0)
        gathered_near = jnp.concatenate([tokens, tie(col_swap(tokens, 1), last)], axis=0)
        for unit in range(early):
            if unit > 0:
                load(unit)
            first_half(unit, gathered_near)
            send(unit, partials[unit])
        mask = mask_of(mine, last)
        first_bias = tie(first_bias, last)
        def far_half(unit):
            first_half(unit, gathered_far)
            if unit < LAG:
                send(unit, partials[unit])

        gathered_far = jnp.concatenate([far, col_swap(far, 1)], axis=0)
        far_half(early)
        for t in range(UNITS + LAG):
            if t < UNITS:
                ours = tie(partials[t], last).astype(F32)
                if t > 0 and t - 1 + LAG - 1 in payloads:
                    ours = behind(ours, payloads[t - 2 + LAG])
                sums[t] = (ours + swaps[t].astype(F32)).astype(BF16)
                last = sums[t]
                crosses[t] = cross(sums[t])
            unit = t - LAG
            if unit == 3 * early - 1:
                second("far", unfold(state(unit)), block_of(unit))
                ours, theirs = core_parts("far")
                come = col_swap(theirs, 1)
            k = t - 1
            if 0 <= k < UNITS:
                summed = tie(sums[k], last).astype(F32) + crosses[k].astype(F32)
                if k in (0, early):
                    low = jnp.split(summed[2 * near :, : fold * LANES], fold, axis=1)
                    low = jnp.concatenate(low, axis=0)
                    own_mask = mask[:near] if k == 0 else mask[near:]
                    low_in[is_near(k)] = jnp.where(own_mask, low, 0.0).astype(BF16)
                if k == UNITS - 1:
                    summed = behind(summed, outputs["far"][0])
                low = low_in[is_near(k)]
                value = activate(unfold(summed), low, first_up_maps, first_bias, columns(k))
                value = halves(value)
                if k + LAG == early:
                    value = jnp.concatenate([value, jnp.zeros_like(value[: near // fold])], axis=0)
                if k + LAG < UNITS:
                    value = jnp.where(is_end, partials[k + LAG], value)
                last = value
                send(k + LAG, value)
            if t + 1 < early:
                far_half(early + t + 1)
            if t == 1:
                whole = tie((gathered_near, gathered_far), last)
                gathered = jnp.concatenate(whole, axis=0)
            if t < early:
                load(early + t)
            if 1 <= t <= early:
                first_late(2 * early + t - 1, gathered)
            if LAG - 1 <= t < LAG + early:
                load_second(t - LAG + 1)
            if early <= unit < 2 * early:
                second("near", unfold(state(unit - early)), unit - early)
                second("far", unfold(state(unit)), unit - early)
                if unit == early:
                    load_second(2 * early - 1)
            elif unit == 3 * early - 1:
                across = (ours + come.astype(F32)).astype(BF16)
                across = col_swap(across, 2)
            elif unit >= 2 * early:
                states = unfold(state(unit))
                if unit == UNITS - 1:
                    last = across
                second("near" if is_near(unit) else "far", states, block_of(unit))
        ours, theirs = core_parts("near")
        come = col_swap(theirs, 1)
        return ours + come.astype(F32) + across.astype(F32), mask

    def plain(tokens, mask, second_weight, second_down_maps, *first):
        rows = tokens.shape[0]
        states = hidden_plain(gather_tokens(tokens), mask, *first)
        outputs = jnp.concatenate([dot(states, second_weight), dot(states, second_down_maps)], axis=1)
        blocks = [outputs[i * rows : (i + 1) * rows] for i in range(n_col)]
        ours = jnp.concatenate(blocks[0::2], axis=0)
        theirs = jnp.concatenate(blocks[1::2], axis=0).astype(BF16)
        ours = ours + col_swap(theirs, 1).astype(F32)
        result = ours[:rows]
        for step in range(1, chips):
            piece = ours[step * rows : (step + 1) * rows].astype(BF16)
            result = result + col_swap(piece, 2 * step).astype(F32)
        return result

    def local(
        tokens,
        token_job_index,
        job_adapter_index,
        first_weight,
        first_bias,
        first_down_maps,
        first_up_maps,
        second_weight,
        second_bias,
        second_down_maps,
        second_up_maps,
    ):
        rows = tokens.shape[0]
        out_width = second_weight.shape[1]
        mine = lax.axis_index("col")

        def mask_of(mine, after):
            mask = token_mask(tie(token_job_index, after), job_adapter_index).astype(jnp.int32)
            for bit in range(n_col.bit_length() - 1):
                size = rows << bit
                blocks = [mask[i : i + size] for i in range(0, mask.shape[0], size)]
                turned = jnp.concatenate([blocks[i ^ 1] for i in range(len(blocks))], axis=0)
                mask = jnp.where((mine >> bit) & 1 == 1, turned, mask)
            return mask == 1

        first = (first_weight, first_bias, first_down_maps, first_up_maps)
        even = first_weight.shape[1] % (UNITS * LANES) == 0
        if n_row == 4 and n_col == 4 and even:
            result, mask = pipeline(tokens, job_adapter_index, mine, mask_of, *first, second_weight, second_down_maps)
        else:
            mask = mask_of(mine, tokens)
            result = plain(tokens, mask, second_weight, second_down_maps, *first)
        low_out = jnp.where(mask[:rows], result[:, out_width:], 0.0).astype(BF16)
        layer_output = result[:, :out_width] + second_bias[None, :] + dot(low_out, second_up_maps)
        return layer_output.astype(BF16)

    return local


def solution(mesh):
    shape = mesh.shape
    return jax.shard_map(
        make_local(shape["group"], shape["row"], shape["col"]),
        mesh=mesh,
        in_specs=(
            P(("group", "col"), "row"),
            P("group"),
            P("group"),
            P("row", "col"),
            P("col"),
            P("row", None),
            P(None, "col"),
            P("col", "row"),
            P("row"),
            P("col", None),
            P(None, "row"),
        ),
        out_specs=P(("group", "col"), "row"),
        check_vma=False,
    )
```

```python
import functools

import jax
import jax.numpy as jnp
from jax import lax
from jax.experimental import pallas as pl
from jax.experimental.pallas import tpu as pltpu
from jax.sharding import PartitionSpec as P

ADAPTER_RANK = 16
ADAPTER_COUNT = 8
JOBS = 4
LANES = 128
UNITS = 8
LAG = 3
F32 = jnp.float32
BF16 = jnp.bfloat16


def gelu_tanh(values):
    return (
        0.5
        * values
        * (1.0 + jnp.tanh(0.7978845608 * (values + 0.044715 * values * values * values)))
    )


def token_mask(token_job_index, job_adapter_index):
    one_hot = token_job_index[:, None] == jnp.arange(JOBS, dtype=jnp.int32)[None, :]
    chosen = jnp.sum(jnp.where(one_hot, job_adapter_index[None, :], 0), axis=1)
    slot_ids = jnp.arange(ADAPTER_COUNT * ADAPTER_RANK, dtype=jnp.int32) // ADAPTER_RANK
    return slot_ids[None, :] == chosen[:, None]


def dot(left, right):
    return jnp.dot(left, right, preferred_element_type=F32)


def tie(value, after):
    return lax.optimization_barrier((value, after))[0]


def load_kernel(w_hbm, after_ref, out, sem, *, part):
    copy = pltpu.make_async_copy(w_hbm.at[part], out, sem)
    copy.start()
    copy.wait()


def load_part(weight, part, after):
    shape = tuple(p.size for p in part)
    return pl.pallas_call(
        functools.partial(load_kernel, part=part),
        in_specs=[pl.BlockSpec(memory_space=pl.ANY)] * 2,
        out_specs=pl.BlockSpec(memory_space=pltpu.VMEM),
        out_shape=pltpu.VMEM(shape, BF16),
        scratch_shapes=[pltpu.SemaphoreType.DMA],
        compiler_params=pltpu.CompilerParams(vmem_limit_bytes=1 << 20),
        cost_estimate=pl.CostEstimate(flops=0, bytes_accessed=1000, transcendentals=0),
    )(pltpu.with_memory_space_constraint(weight, pltpu.HBM), after)


def behind(value, row):
    return value + 0.0 * row[:1, : value.shape[1]].astype(F32)


def activate(summed, low_in, first_up_maps, first_bias, part):
    before = summed + first_bias[None, part] + dot(low_in, first_up_maps[:, part])
    return gelu_tanh(before).astype(BF16)


def hidden_plain(tokens, mask, first_weight, first_bias, first_down_maps, first_up_maps):
    width = first_weight.shape[1]
    joined = jnp.concatenate([dot(tokens, first_weight), dot(tokens, first_down_maps)], axis=1)
    summed = lax.psum_scatter(
        joined.astype(BF16), "row", scatter_dimension=0, tiled=True
    ).astype(F32)
    rows = summed.shape[0]
    own_mask = lax.dynamic_slice_in_dim(mask, lax.axis_index("row") * rows, rows, 0)
    low_in = jnp.where(own_mask, summed[:, width:], 0.0).astype(BF16)
    states = activate(summed[:, :width], low_in, first_up_maps, first_bias, slice(0, width))
    return lax.all_gather(states, "row", axis=0, tiled=True)


def make_local(n_group, n_row, n_col):
    chips = n_col // 2

    def place_of(group, row, col):
        return (group * n_row + row) * n_col + col

    cross_pairs = []
    for group in range(n_group):
        for row in range(n_row):
            for col in range(n_col):
                if n_row == 4 and row in (1, 2):
                    other = place_of(group, 3 - row, col)
                else:
                    other = place_of(group, row, col ^ 1)
                cross_pairs.append((place_of(group, row, col), other))

    def col_swap(value, flip):
        return lax.ppermute(value, "col", [(i, i ^ flip) for i in range(n_col)])

    def end_swap(value):
        return lax.ppermute(value, "row", [(i, i ^ 1) for i in range(n_row)])

    def cross(value):
        return lax.ppermute(value, ("group", "row", "col"), cross_pairs)

    def gather_tokens(tokens):
        shards = [tokens, col_swap(tokens, 1)]
        for step in range(1, chips):
            far = col_swap(tokens, 2 * step)
            shards += [far, col_swap(far, 1)]
        return jnp.concatenate(shards, axis=0)

    def pipeline(
        tokens,
        jobs,
        mine,
        mask_of,
        first_weight,
        first_bias,
        first_down_maps,
        first_up_maps,
        second_weight,
        second_down_maps,
    ):
        rows = tokens.shape[0]
        near = 2 * rows
        width = first_weight.shape[1] // UNITS
        wide = 2 * width
        early = UNITS // 4
        fold = max(n for n in range(1, width // LANES + 1) if near % n == 0)
        place = lax.axis_index("row")
        is_end = (place == 0) | (place == 3)
        last = tokens
        partials, payloads, swaps, sums, crosses = {}, {}, {}, {}, {}
        total, low_total = None, None
        low_in = {}

        def halves(value):
            return jnp.concatenate([value[:, :width], value[:, width:]], axis=0)

        def unfold(value):
            return jnp.concatenate([value[:near], value[near : 2 * near]], axis=1)

        def block_of(unit):
            return unit % early + (early if unit >= 2 * early else 0)

        def is_near(unit):
            return unit < early or unit >= 3 * early

        def columns(unit):
            return slice(block_of(unit) * wide, (block_of(unit) + 1) * wide)

        def load(block):
            nonlocal last
            part = (pl.ds(0, first_weight.shape[0]), pl.ds(block * wide, wide))
            loads[block] = load_part(first_weight, part, last)
            last = loads[block]

        def load_second(block):
            nonlocal last
            part = (pl.ds(block * wide, wide), pl.ds(0, second_weight.shape[1]))
            second_loads[block] = load_part(second_weight, part, last)
            last = second_loads[block]

        def multiply(x, block):
            nonlocal last
            value = dot(tie(x, last), loads[block]).astype(BF16)
            last = value
            return value

        def first_half(unit, x):
            nonlocal last
            value = halves(multiply(x, block_of(unit)))
            if unit in (0, early):
                low = dot(x, first_down_maps).astype(BF16)
                low = jnp.concatenate(jnp.split(low, fold, axis=0), axis=1)
                low = jnp.pad(low, ((0, 0), (0, width - fold * LANES)))
                value = jnp.concatenate([value, low], axis=0)
            partials[unit] = value
            last = value

        def first_late(unit, x):
            value = multiply(x, block_of(unit))
            partials[unit + early], partials[unit] = halves(value[:near]), halves(value[near:])

        def send(t, value):
            payloads[t] = value
            swaps[t] = end_swap(value)

        def state(unit):
            come = tie(swaps[unit + LAG], last)
            return jnp.where(is_end, come, payloads[unit + LAG])

        def second(name, states, block):
            nonlocal last
            states = tie(states, last)
            part = slice(block * wide, (block + 1) * wide)
            low = dot(states, second_down_maps[part])
            value = dot(states, second_loads[block])
            if name in outputs:
                value, low = outputs[name][0] + value, outputs[name][1] + low
            value = lax.optimization_barrier(value)
            last = value[:8, :LANES]
            outputs[name] = (value, low)

        def core_parts(name):
            joined = jnp.concatenate(outputs[name], axis=1)
            return joined[:rows], joined[rows:].astype(BF16)

        far = col_swap(tokens, 2)
        loads, second_loads, outputs = {}, {}, {}
        last, is_end, mine = lax.optimization_barrier((jobs, is_end, mine))
        load(0)
        gathered_near = jnp.concatenate([tokens, tie(col_swap(tokens, 1), last)], axis=0)
        for unit in range(early):
            if unit > 0:
                load(unit)
            first_half(unit, gathered_near)
            send(unit, partials[unit])
        mask = mask_of(mine, last)
        first_bias = tie(first_bias, last)
        def far_half(unit):
            first_half(unit, gathered_far)
            if unit < LAG:
                send(unit, partials[unit])

        gathered_far = jnp.concatenate([far, col_swap(far, 1)], axis=0)
        far_half(early)
        for t in range(UNITS + LAG):
            if t < UNITS:
                ours = tie(partials[t], last).astype(F32)
                if t > 0 and t - 1 + LAG - 1 in payloads:
                    ours = behind(ours, payloads[t - 2 + LAG])
                sums[t] = (ours + swaps[t].astype(F32)).astype(BF16)
                last = sums[t]
                crosses[t] = cross(sums[t])
            unit = t - LAG
            if unit == 3 * early - 1:
                second("far", unfold(state(unit)), block_of(unit))
                ours, theirs = core_parts("far")
                come = col_swap(theirs, 1)
            k = t - 1
            if 0 <= k < UNITS:
                summed = tie(sums[k], last).astype(F32) + crosses[k].astype(F32)
                if k in (0, early):
                    low = jnp.split(summed[2 * near :, : fold * LANES], fold, axis=1)
                    low = jnp.concatenate(low, axis=0)
                    own_mask = mask[:near] if k == 0 else mask[near:]
                    low_in[is_near(k)] = jnp.where(own_mask, low, 0.0).astype(BF16)
                if k == UNITS - 1:
                    summed = behind(summed, outputs["far"][0])
                low = low_in[is_near(k)]
                value = activate(unfold(summed), low, first_up_maps, first_bias, columns(k))
                value = halves(value)
                if k + LAG == early:
                    value = jnp.concatenate([value, jnp.zeros_like(value[: near // fold])], axis=0)
                if k + LAG < UNITS:
                    value = jnp.where(is_end, partials[k + LAG], value)
                last = value
                send(k + LAG, value)
            if t + 1 < early:
                far_half(early + t + 1)
            if t == 1:
                whole = tie((gathered_near, gathered_far), last)
                gathered = jnp.concatenate(whole, axis=0)
            if LAG <= t < LAG + 2 * early - 1:
                load_second(t - LAG)
            elif t == UNITS - 1:
                load_second(2 * early - 1)
            if 1 <= t <= early:
                load(early + t - 1)
                first_late(2 * early + t - 1, gathered)
            if early <= unit < 2 * early:
                second("near", unfold(state(unit - early)), unit - early)
                second("far", unfold(state(unit)), unit - early)
            elif unit == 3 * early - 1:
                across = (ours + come.astype(F32)).astype(BF16)
                across = col_swap(across, 2)
            elif unit >= 2 * early:
                states = unfold(state(unit))
                if unit == UNITS - 1:
                    last = across
                second("near" if is_near(unit) else "far", states, block_of(unit))
        ours, theirs = core_parts("near")
        come = col_swap(theirs, 1)
        return ours + come.astype(F32) + across.astype(F32), mask

    def plain(tokens, mask, second_weight, second_down_maps, *first):
        rows = tokens.shape[0]
        states = hidden_plain(gather_tokens(tokens), mask, *first)
        outputs = jnp.concatenate([dot(states, second_weight), dot(states, second_down_maps)], axis=1)
        blocks = [outputs[i * rows : (i + 1) * rows] for i in range(n_col)]
        ours = jnp.concatenate(blocks[0::2], axis=0)
        theirs = jnp.concatenate(blocks[1::2], axis=0).astype(BF16)
        ours = ours + col_swap(theirs, 1).astype(F32)
        result = ours[:rows]
        for step in range(1, chips):
            piece = ours[step * rows : (step + 1) * rows].astype(BF16)
            result = result + col_swap(piece, 2 * step).astype(F32)
        return result

    def local(
        tokens,
        token_job_index,
        job_adapter_index,
        first_weight,
        first_bias,
        first_down_maps,
        first_up_maps,
        second_weight,
        second_bias,
        second_down_maps,
        second_up_maps,
    ):
        rows = tokens.shape[0]
        out_width = second_weight.shape[1]
        mine = lax.axis_index("col")

        def mask_of(mine, after):
            mask = token_mask(tie(token_job_index, after), job_adapter_index).astype(jnp.int32)
            for bit in range(n_col.bit_length() - 1):
                size = rows << bit
                blocks = [mask[i : i + size] for i in range(0, mask.shape[0], size)]
                turned = jnp.concatenate([blocks[i ^ 1] for i in range(len(blocks))], axis=0)
                mask = jnp.where((mine >> bit) & 1 == 1, turned, mask)
            return mask == 1

        first = (first_weight, first_bias, first_down_maps, first_up_maps)
        even = first_weight.shape[1] % (UNITS * LANES) == 0
        if n_row == 4 and n_col == 4 and even:
            result, mask = pipeline(tokens, job_adapter_index, mine, mask_of, *first, second_weight, second_down_maps)
        else:
            mask = mask_of(mine, tokens)
            result = plain(tokens, mask, second_weight, second_down_maps, *first)
        low_out = jnp.where(mask[:rows], result[:, out_width:], 0.0).astype(BF16)
        layer_output = result[:, :out_width] + second_bias[None, :] + dot(low_out, second_up_maps)
        return layer_output.astype(BF16)

    return local


def solution(mesh):
    shape = mesh.shape
    return jax.shard_map(
        make_local(shape["group"], shape["row"], shape["col"]),
        mesh=mesh,
        in_specs=(
            P(("group", "col"), "row"),
            P("group"),
            P("group"),
            P("row", "col"),
            P("col"),
            P("row", None),
            P(None, "col"),
            P("col", "row"),
            P("row"),
            P("col", None),
            P(None, "row"),
        ),
        out_specs=P(("group", "col"), "row"),
        check_vma=False,
    )
```
